32 devices in a mesh: dp: 2 (over core), seq: 4 (over y, x), head: 4 (over z).
Axes of the slice: x: 2, y: 2, z: 4, core: 2. Of those that a mesh axis runs over, the one named last changes fastest.
Arguments:
- frames: bfloat16 [2, 3072, 1536], P('dp', ('seq', 'head')), may hold values from -600 to 600
- norm_gain: float32 [1536], replicated, may hold values from 0.1 to 1.9
- w_query: bfloat16 [1536, 1536], P('dp', 'head'), may hold values from -1.6 to 1.6
- w_key: bfloat16 [1536, 1536], P('dp', 'head'), may hold values from -16 to 16
- w_value: bfloat16 [1536, 1536], P('dp', 'head'), may hold values from -0.15625 to 0.15625
- w_out: bfloat16 [1536, 1536], P('head', 'dp'), may hold values from -0.4375 to 0.4375
- group_band: int32 [2, 24, 12], P('dp', 'seq'), may hold values 0 or 1
- lengths: int32 [2], P('dp'), may hold values from 1536 to 3072
Outputs:
- update: bfloat16 [2, 3072, 1536], P('dp', ('seq', 'head'))
The draws below stay inside these ranges and needn't reach their ends.
All inputs are finite; a program needn't handle non-finite values. No bound on the sum of `group_band` on one device may be relied on, other than what follows from the above.
Results may differ from the reference program's by a relative error of at most 0.012.
Values may be sent and summed in bfloat16 or wider, within the bound.
No kernel may reach another device: no remote copies, remote signals or barrier semaphores. Data moves between devices by JAX's collectives and lax.ppermute only.
A program may use at most 128 MiB of HBM per device.

```python
import math
import jax
import jax.numpy as jnp
from jax import lax

D = 1536
HEADS = 24
HD = 64
GROUP = 128
BATCH = 2
FRAMES = 3072
GROUP_DEV = 6
GROUPS = 24


def query_base(key):
    return jnp.clip(jax.random.normal(jax.random.fold_in(key, 11), (D, HEADS * HD), jnp.float32), -6.0, 6.0)


def draw_frames(key, part):
    key = jax.random.fold_in(key, 3)
    noise_key, row_key, col_key = jax.random.split(key, 3)
    row_scale = jnp.exp(jax.random.uniform(row_key, (BATCH, FRAMES, 1), jnp.float32, 0.0, math.log(10.0)))
    col_scale = jnp.exp(jax.random.uniform(col_key, (1, 1, D), jnp.float32, 0.0, math.log(10.0)))
    values = jnp.clip(jax.random.normal(noise_key, (BATCH, FRAMES, D), jnp.float32), -6.0, 6.0)
    return (values * row_scale * col_scale).astype(jnp.bfloat16)


def draw_w_query(key, part):
    return (query_base(key) * (2.0 / math.sqrt(D))).astype(jnp.bfloat16)


def draw_w_key(key, part):
    key = jax.random.fold_in(key, 7)
    noise_key = jax.random.fold_in(key, 0)
    noise = jnp.clip(jax.random.normal(noise_key, (D, HEADS * HD), jnp.float32), -6.0, 6.0) / math.sqrt(D)
    values = noise
    return values.astype(jnp.bfloat16)


def with_ends(result, own_key, low, largest):
    spot = [jax.random.randint(jax.random.fold_in(own_key, axis), (), 0, length) for axis, length in enumerate(result.shape)]
    longest = result.shape.index(max(result.shape))
    next_to = spot[:longest] + [(spot[longest] + 1) % result.shape[longest]] + spot[longest + 1:]
    return result.at[tuple(spot)].set(low).at[tuple(next_to)].set(largest)


def block_scale(own_key, shape, cuts, smallest, largest):
    def one(dim, shards_of):
        heights = jax.random.uniform(jax.random.fold_in(jax.random.fold_in(own_key, 6), dim), (shards_of,), jnp.float32, smallest / len(cuts), largest / len(cuts))
        return jnp.repeat(jnp.exp(heights), shape[dim] // shards_of).reshape((-1,) + (1,) * (len(shape) - dim - 1))

    level = one(*cuts[0])
    for cut in cuts[1:]:
        level = level * one(*cut)
    return level


def gaussian(key, shape, deviation, most, cuts=(), held_as=jnp.bfloat16):
    drawn = jax.random.normal(key, shape, jnp.float32) * deviation
    if len(cuts) > 0:
        drawn = block_scale(key, shape, cuts, -0.22, 0.18) * drawn
    return jnp.clip(drawn, min=-most, max=most).astype(held_as)


def setup_inputs(seed: int = 0) -> dict:
    key_list = jax.random.split(jax.random.key(seed), 9)
    frames = draw_frames(jax.random.fold_in(key_list[8], 71), 0)
    norm_gain = jnp.clip(1.0 + 0.18 * jax.random.normal(key_list[1], (D,), jnp.float32), 0.1, 1.9)
    w_query = draw_w_query(jax.random.fold_in(key_list[8], 71), 0)
    w_key = draw_w_key(jax.random.fold_in(key_list[8], 71), 0)
    w_value = gaussian(key_list[4], (D, HEADS * HD), D ** -0.5, 0.15625, ((0, 2), (1, 4)))
    w_out = gaussian(key_list[5], (HEADS * HD, D), (D // 8) ** -0.5, 0.4375, ((0, 4), (1, 2)))
    group_band = with_ends((jax.random.randint(key_list[6], (BATCH, GROUPS, 2 * GROUP_DEV), 0, 2) < 1).astype(jnp.int32), jax.random.fold_in(key_list[6], 1), 0, 1)
    lengths = jax.random.randint(key_list[7], (BATCH,), FRAMES // 2, FRAMES + 1).astype(jnp.int32)
    return dict(frames=frames, norm_gain=norm_gain, w_query=w_query, w_key=w_key, w_value=w_value, w_out=w_out, group_band=group_band, lengths=lengths)


epsilon = 1e-05

def layer_norm(rows, norm_gain):
    values = rows.astype(jnp.float32)
    center = values - lax.optimization_barrier(jnp.mean(values, axis=-1, keepdims=True))
    spread = lax.optimization_barrier(jnp.mean(center * center, axis=-1, keepdims=True))
    return (center * lax.rsqrt(spread + epsilon) * norm_gain.astype(jnp.float32)).astype(jnp.bfloat16)

def permission(query_start, key_start, query_groups, key_groups, group_size, band_rows, length_value, total_groups):
    query_ids = query_start + jnp.arange(query_groups, dtype=jnp.int32)
    key_ids = key_start + jnp.arange(key_groups, dtype=jnp.int32)
    offsets = key_ids[None, :] - query_ids[:, None]
    reach_groups = band_rows.shape[1] // 2
    column = jnp.where(offsets < 0, offsets + reach_groups, offsets + reach_groups - 1)
    hits = column[:, :, None] == jnp.arange(2 * reach_groups, dtype=jnp.int32)[None, None, :]
    picked = lax.optimization_barrier(jnp.sum(jnp.where(hits, band_rows[:, None, :], 0), axis=-1))
    inside = (key_ids >= 0) & (key_ids < total_groups)
    linked = (offsets != 0) & (jnp.abs(offsets) <= reach_groups) & inside[None, :] & (picked == 1)
    key_frames = key_start * group_size + jnp.arange(key_groups * group_size, dtype=jnp.int32)
    alive_keys = key_frames < length_value
    linked_rows = jnp.repeat(jnp.repeat(linked, group_size, axis=0), group_size, axis=1) & alive_keys[None, :]
    same_group = jnp.repeat(jnp.repeat(offsets == 0, group_size, axis=0), group_size, axis=1)
    return linked_rows | same_group

def utterance(frames_one, norm_gain, w_query, w_key, w_value, w_out, band_one, length_value):
    normalized = layer_norm(frames_one, norm_gain)
    queries = jnp.dot(normalized, w_query, preferred_element_type=jnp.float32).astype(jnp.bfloat16)
    keys_all = jnp.dot(normalized, w_key, preferred_element_type=jnp.float32).astype(jnp.bfloat16)
    values_all = jnp.dot(normalized, w_value, preferred_element_type=jnp.float32).astype(jnp.bfloat16)
    block_rows = GROUP_DEV * GROUP
    margin = jnp.zeros((block_rows, HEADS * HD), jnp.bfloat16)
    keys_padded = jnp.concatenate([margin, keys_all, margin], axis=0)
    values_padded = jnp.concatenate([margin, values_all, margin], axis=0)
    score_scale = 1.0 / math.sqrt(HD)

    def block_context(block_index):
        first_row = block_index * block_rows
        query_block = lax.dynamic_slice_in_dim(queries, first_row, block_rows, 0).astype(jnp.float32).reshape(block_rows, HEADS, HD)
        key_block = lax.dynamic_slice_in_dim(keys_padded, first_row, 3 * block_rows, 0).astype(jnp.float32).reshape(3 * block_rows, HEADS, HD)
        value_block = lax.dynamic_slice_in_dim(values_padded, first_row, 3 * block_rows, 0).astype(jnp.float32).reshape(3 * block_rows, HEADS, HD)
        band_block = lax.dynamic_slice_in_dim(band_one, block_index * GROUP_DEV, GROUP_DEV, 0)
        allowed = permission(block_index * GROUP_DEV, block_index * GROUP_DEV - GROUP_DEV, GROUP_DEV, 3 * GROUP_DEV, GROUP, band_block, length_value, GROUPS)
        scores = jnp.einsum('qhd,khd->hqk', query_block, key_block) * score_scale
        masked = jnp.where(allowed[None, :, :], scores, -jnp.inf)
        row_max = lax.optimization_barrier(jnp.max(masked, axis=-1, keepdims=True))
        weights = jnp.exp(masked - row_max)
        row_total = lax.optimization_barrier(jnp.sum(weights, axis=-1, keepdims=True))
        rounded = lax.optimization_barrier(weights.astype(jnp.bfloat16)).astype(jnp.float32)
        context = jnp.einsum('hqk,khd->hqd', rounded, value_block) / row_total
        return jnp.transpose(context, (1, 0, 2)).reshape(block_rows, HEADS * HD).astype(jnp.bfloat16)
    contexts = lax.map(block_context, jnp.arange(GROUPS // GROUP_DEV, dtype=jnp.int32))
    context = contexts.reshape(FRAMES, HEADS * HD)
    return jnp.dot(context, w_out, preferred_element_type=jnp.float32).astype(jnp.bfloat16)

def reference(frames, norm_gain, w_query, w_key, w_value, w_out, group_band, lengths):
    updates = [utterance(frames[utter_index], norm_gain, w_query, w_key, w_value, w_out, group_band[utter_index], lengths[utter_index]) for utter_index in range(BATCH)]
    return jnp.stack(updates, axis=0)
```

```python
import functools

import jax
import jax.numpy as jnp
from jax import lax
from jax.experimental import pallas as pl
from jax.experimental.pallas import tpu as pltpu
from jax.sharding import PartitionSpec as P

HD = 64
GROUP = 128
LANES = 128

epsilon = 1e-05

VMEM = pl.BlockSpec(memory_space=pltpu.VMEM)
SMEM = pl.BlockSpec(memory_space=pltpu.SMEM)
LIMIT = 56 * 1024 * 1024


def ring_successors(count):
    order = [0] + list(range(1, count, 2)) + list(range(count - 2 + count % 2, 0, -2))
    return {order[i]: order[(i + 1) % count] for i in range(count)}


def lookup(table, index):
    value = jnp.int32(table[0])
    for place in range(1, len(table)):
        value = jnp.where(index == place, jnp.int32(table[place]), value)
    return value


def project_kernel(place_ref, rows_ref, gain_ref, *refs):
    own, other, (query_ref, pair_ref) = refs[:3], refs[3:6], refs[6:]
    values = rows_ref[...].astype(jnp.float32)
    center = values - jnp.mean(values, axis=-1, keepdims=True)
    spread = jnp.mean(center * center, axis=-1, keepdims=True)
    normalized = (center * lax.rsqrt(spread + epsilon) * gain_ref[...]).astype(jnp.bfloat16)
    depth = own[0].shape[0]
    low, high = normalized[:, :depth], normalized[:, depth:]
    first = place_ref[0] == 0
    mine = jnp.where(first, low, high)
    theirs = jnp.where(first, high, low)
    width = own[0].shape[1]
    sums = [
        jnp.dot(mine, a[...], preferred_element_type=jnp.float32)
        + jnp.dot(theirs, b[...], preferred_element_type=jnp.float32)
        for a, b in zip(own, other)
    ]
    query_ref[...] = (sums[0].astype(jnp.bfloat16).astype(jnp.float32) * (HD ** -0.5)).astype(jnp.bfloat16)
    pair_ref[:, :width] = sums[1].astype(jnp.bfloat16)
    pair_ref[:, width:] = sums[2].astype(jnp.bfloat16)


def project(place, rows, gain, own, other):
    count, width = rows.shape[0], own[0].shape[1]
    return pl.pallas_call(
        project_kernel,
        out_shape=(
            jax.ShapeDtypeStruct((count, width), jnp.bfloat16),
            jax.ShapeDtypeStruct((count, 2 * width), jnp.bfloat16),
        ),
        in_specs=[SMEM] + [VMEM] * 8,
        out_specs=(VMEM, VMEM),
        compiler_params=pltpu.CompilerParams(vmem_limit_bytes=LIMIT),
        cost_estimate=pl.CostEstimate(
            flops=2 * count * rows.shape[1] * 3 * width,
            bytes_accessed=2 * (rows.shape[1] * 3 * width + count * (rows.shape[1] + 3 * width)),
            transcendentals=count,
        ),
        name="project",
    )(place, rows, gain, *own, *other)


def attend_kernel(steps, groups, reach, place_ref, band_ref, *refs):
    queries = refs[:steps]
    owns = refs[steps:2 * steps]
    sides = refs[2 * steps:4 * steps]
    outs = refs[4 * steps:5 * steps]
    q_all, k_all, v_all, vt_all, score, ctx, chosen, limits = refs[5 * steps:]
    rows, width = queries[0].shape
    pairs = width // LANES
    block = steps * rows
    core, first_group, total, length = (place_ref[i] for i in range(4))
    chip_base = jnp.where(core == 0, 2 * block, 0)
    link_base = jnp.where(core == 0, 0, 2 * block)
    for step in range(steps):
        at = place_ref[4 + step] * rows
        q_at = pl.ds(pl.multiple_of(at, 64), rows)
        for pair in range(pairs):
            cols = slice(pair * LANES, (pair + 1) * LANES)
            q_all[pair, q_at, :] = queries[step][:, cols]
        for source, base in ((owns[step], block), (sides[step], chip_base), (sides[steps + step], link_base)):
            to = pl.ds(pl.multiple_of(base + at, 64), rows)
            for pair in range(pairs):
                k_all[pair, to, :] = source[:, pair * LANES:(pair + 1) * LANES]
                v_all[pair, to, :] = source[:, width + pair * LANES:width + (pair + 1) * LANES]

    def turn(index, carry):
        for pair in range(pairs):
            vt_all[pair, index] = v_all[pair, pl.ds(pl.multiple_of(index * GROUP, GROUP), GROUP), :].T
        return carry

    lax.fori_loop(0, 3 * groups, turn, 0)

    slots = 2 * reach + 2

    def choose(group, carry):
        for slot in range(slots):
            chosen[group * slots + slot] = groups + group
            limits[group * slots + slot] = 0
        limits[group * slots] = GROUP
        count = jnp.int32(1)
        for column in range(2 * reach):
            offset = column - reach if column < reach else column - reach + 1
            there = first_group + group + offset
            left = length - there * GROUP
            good = (there >= 0) & (there < total) & (band_ref[group, column] == 1) & (left > 0)
            chosen[group * slots + count] = jnp.where(good, groups + group + offset, groups + group)
            limits[group * slots + count] = jnp.where(good, jnp.minimum(left, GROUP), 0)
            count = count + good.astype(jnp.int32)

        def run(size):
            half_mask = lax.broadcasted_iota(jnp.int32, (GROUP, LANES), 1) < HD
            row_ids = lax.broadcasted_iota(jnp.int32, (GROUP, 2 * GROUP), 0)

            def one_pair(pair, inner):
                own = q_all[pair, pl.ds(pl.multiple_of(group * GROUP, GROUP), GROUP), :]
                zero = jnp.zeros_like(own)
                both = jnp.concatenate(
                    [jnp.where(half_mask, own, zero), jnp.where(half_mask, zero, own)], axis=0
                ).T
                best = None
                for slot in range(0, size, 2):
                    tiles = []
                    for one in (slot, slot + 1):
                        index = chosen[group * slots + one]
                        tiles.append(k_all[pair, pl.ds(pl.multiple_of(index * GROUP, GROUP), GROUP), :])
                    got = jnp.dot(jnp.concatenate(tiles, axis=0), both, preferred_element_type=jnp.float32)
                    for one in (slot, slot + 1):
                        part = got[(one - slot) * GROUP:(one - slot + 1) * GROUP]
                        if one > 0:
                            part = jnp.where(row_ids < limits[group * slots + one], part, -jnp.inf)
                        score[one * GROUP:(one + 1) * GROUP, :] = part
                        top = jnp.max(part.reshape(GROUP // 8, 8, 2 * GROUP), axis=0)
                        best = top if best is None else jnp.maximum(best, top)
                row_max = jnp.max(best, axis=0, keepdims=True)
                total_sum = jnp.zeros((8, 2 * GROUP), jnp.float32)
                mixed = jnp.zeros((LANES, 2 * GROUP), jnp.float32)
                for slot in range(0, size, 2):
                    weights = jnp.exp(score[slot * GROUP:(slot + 2) * GROUP, :] - row_max)
                    total_sum += jnp.sum(weights.reshape(2 * GROUP // 8, 8, 2 * GROUP), axis=0)
                    tiles = [vt_all[pair, chosen[group * slots + one]] for one in (slot, slot + 1)]
                    mixed += jnp.dot(
                        jnp.concatenate(tiles, axis=1),
                        weights.astype(jnp.bfloat16),
                        preferred_element_type=jnp.float32,
                    )
                mixed = mixed / jnp.sum(total_sum, axis=0, keepdims=True)
                both_heads = jnp.concatenate([mixed[:HD, :GROUP], mixed[HD:, GROUP:]], axis=0)
                ctx[pair, pl.ds(pl.multiple_of(group * GROUP, GROUP), GROUP), :] = both_heads.T.astype(jnp.bfloat16)
                return inner

            lax.fori_loop(0, pairs, one_pair, 0)

        sizes = [size for size in (4, 8, 10) if size < slots] + [slots]
        for place, size in enumerate(sizes):
            low = sizes[place - 1] if place > 0 else 0

            @pl.when((count > low) & (count <= size))
            def _():
                run(size)

        return carry

    lax.fori_loop(0, groups, choose, 0)
    for step in range(steps):
        at = pl.ds(pl.multiple_of(place_ref[4 + steps + step] * rows, 64), rows)
        for pair in range(pairs):
            outs[step][:, pair * LANES:(pair + 1) * LANES] = ctx[pair, at, :]


def attend(place, band, queries, owns, chip_side, link_side):
    steps = len(queries)
    rows, width = queries[0].shape
    groups, reach = band.shape[0], band.shape[1] // 2
    pairs, block = width // LANES, steps * rows
    slots = 2 * reach + 2
    work = block * (2 * reach + 1) * GROUP * (width // HD)
    return pl.pallas_call(
        functools.partial(attend_kernel, steps, groups, reach),
        out_shape=(jax.ShapeDtypeStruct((rows, width), jnp.bfloat16),) * steps,
        in_specs=[SMEM, SMEM] + [VMEM] * (4 * steps),
        out_specs=(VMEM,) * steps,
        scratch_shapes=[
            pltpu.VMEM((pairs, block, LANES), jnp.bfloat16),
            pltpu.VMEM((pairs, 3 * block, LANES), jnp.bfloat16),
            pltpu.VMEM((pairs, 3 * block, LANES), jnp.bfloat16),
            pltpu.VMEM((pairs, 3 * groups, LANES, GROUP), jnp.bfloat16),
            pltpu.VMEM((slots * GROUP, 2 * GROUP), jnp.float32),
            pltpu.VMEM((pairs, block, LANES), jnp.bfloat16),
            pltpu.SMEM((groups * slots,), jnp.int32),
            pltpu.SMEM((groups * slots,), jnp.int32),
        ],
        compiler_params=pltpu.CompilerParams(vmem_limit_bytes=LIMIT),
        cost_estimate=pl.CostEstimate(
            flops=8 * work * HD, bytes_accessed=2 * width * block * 8, transcendentals=work
        ),
        name="attend",
    )(place, band, *queries, *owns, *chip_side, *link_side)


def output_kernel(steps, place_ref, weight_ref, *refs):
    total = None
    for step in range(steps):
        part = jnp.dot(
            refs[step][...], weight_ref[place_ref[step]], preferred_element_type=jnp.float32
        )
        total = part if total is None else total + part
    refs[steps][0] = total.astype(jnp.bfloat16)


def output(place, weight, contexts):
    steps = len(contexts)
    rows, width = contexts[0].shape
    columns = weight.shape[2]
    return pl.pallas_call(
        functools.partial(output_kernel, steps),
        out_shape=jax.ShapeDtypeStruct((1, rows, columns), jnp.bfloat16),
        in_specs=[SMEM] + [VMEM] * (1 + steps),
        out_specs=VMEM,
        compiler_params=pltpu.CompilerParams(vmem_limit_bytes=LIMIT),
        cost_estimate=pl.CostEstimate(
            flops=2 * rows * width * steps * columns,
            bytes_accessed=2 * (width * steps * columns + 2 * rows * columns),
            transcendentals=0,
        ),
        name="output",
    )(place, weight, *contexts)


def local(frames, norm_gain, w_query, w_key, w_value, w_out, group_band, lengths):
    cores, seqs, layers = lax.axis_size("dp"), lax.axis_size("seq"), lax.axis_size("head")
    core, seq, layer = lax.axis_index("dp"), lax.axis_index("seq"), lax.axis_index("head")
    groups = group_band.shape[1]
    here = [(c, s) for c in range(cores) for s in range(seqs)]

    def home(c, s):
        return s % 2, s // 2 * 2 + c

    def flat(c, s, z=None):
        return c * seqs + s if z is None else (c * seqs + s) * layers + z

    def moved(value, shift):
        pairs = [(flat(c, s, z), flat(*home(c, s), shift(z))) for c, s in here for z in range(layers)]
        return lax.ppermute(value, ("dp", "seq", "head"), pairs)

    after = ring_successors(layers)
    before = {after[z]: z for z in after}
    swap = [(c, cores - 1 - c) for c in range(cores)]
    over_link = [(flat(1, s), flat(0, s + 2)) for s in range(seqs - 2)]
    over_link += [(flat(0, s + 2), flat(1, s)) for s in range(seqs - 2)]

    ring = [(z, after[z]) for z in range(layers)]
    rows = frames[0]
    blocks = [None, moved(rows, lambda z: after[z])]
    blocks[0] = moved(rows, lambda z: z)
    for _ in range(2, layers):
        blocks.append(lax.ppermute(blocks[-1], "head", ring))
    own = (w_query, w_key, w_value)
    other = lax.ppermute(own, "dp", swap)
    facts = jnp.concatenate([group_band[0], jnp.broadcast_to(lengths[:, None], (1, group_band.shape[2]))], axis=0)
    facts = lax.ppermute(facts, ("dp", "seq"), [(flat(c, s), flat(*home(c, s))) for c, s in here])

    share = 4 if seqs % 4 == 0 else (2 if seqs % 2 == 0 else 1)
    part = w_out.shape[0] // share
    piece = lax.dynamic_slice_in_dim(w_out, seq % share * part, part, 0)
    pieces = lax.all_gather(piece, "head", axis=0)
    sets = [list(range(s, s + share)) for s in range(0, seqs, share)]
    pieces = lax.all_gather(pieces, "seq", axis=0, axis_index_groups=sets)
    pieces = lax.all_gather(pieces, "dp", axis=0)
    weight = jnp.transpose(pieces, (2, 1, 3, 0, 4)).reshape(layers, w_out.shape[0], cores * w_out.shape[1])

    gain = norm_gain[None, :]
    core_at = core[None].astype(jnp.int32)
    queries, owns, chip_side, link_side = [], [], [], []
    for rows in blocks:
        query, pair = project(core_at, rows, gain, own, other)
        queries.append(query)
        owns.append(pair)
        link_side.append(lax.ppermute(pair, ("dp", "seq"), over_link))
        chip_side.append(lax.ppermute(pair, "dp", swap))

    ids = [layer]
    for _ in range(1, layers):
        ids.append(lookup([before[z] for z in range(layers)], ids[-1]))
    targets = [lax.rem(layer + shift, layers) for shift in range(layers)]
    place = [core, (seq // 2 * 2 + core) * groups, groups * seqs, facts[groups, 0]] + ids + targets
    place = jnp.stack([jnp.asarray(value, jnp.int32) for value in place])
    contexts = attend(place, facts[:groups], queries, owns, chip_side, link_side)
    arrived = [
        moved(context, lambda z, shift=shift: (z + shift) % layers) for shift, context in enumerate(contexts)
    ]
    sources = jnp.stack([lax.rem(layer + layers - shift, layers) for shift in range(layers)]).astype(jnp.int32)
    return output(sources, weight, arrived)


def solution(mesh):
    return jax.shard_map(
        local,
        mesh=mesh,
        in_specs=(
            P("dp", ("seq", "head"), None),
            P(),
            P("dp", "head"),
            P("dp", "head"),
            P("dp", "head"),
            P("head", "dp"),
            P("dp", "seq", None),
            P("dp"),
        ),
        out_specs=P("dp", ("seq", "head"), None),
        check_vma=False,
    )
```

```python
import functools

import jax
import jax.numpy as jnp
from jax import lax
from jax.experimental import pallas as pl
from jax.experimental.pallas import tpu as pltpu
from jax.sharding import PartitionSpec as P

HD = 64
GROUP = 128
LANES = 128

epsilon = 1e-05

VMEM = pl.BlockSpec(memory_space=pltpu.VMEM)
SMEM = pl.BlockSpec(memory_space=pltpu.SMEM)
MIB = 1024 * 1024


def ring_successors(count):
    order = [0] + list(range(1, count, 2)) + list(range(count - 2 + count % 2, 0, -2))
    return {order[i]: order[(i + 1) % count] for i in range(count)}


def lookup(table, index):
    value = jnp.int32(table[0])
    for place in range(1, len(table)):
        value = jnp.where(index == place, jnp.int32(table[place]), value)
    return value


def project_kernel(parts, place_ref, gain_ref, *refs):
    rows, own, other, (query_ref, pair_ref) = refs[:parts], refs[parts:parts + 3], refs[parts + 3:parts + 6], refs[parts + 6:]
    gain = gain_ref[...]
    pieces = []
    for part in rows:
        values = part[...].astype(jnp.float32)
        center = values - jnp.mean(values, axis=-1, keepdims=True)
        spread = jnp.mean(center * center, axis=-1, keepdims=True)
        pieces.append((center * lax.rsqrt(spread + epsilon) * gain).astype(jnp.bfloat16))
    normalized = pieces[0] if parts == 1 else jnp.concatenate(pieces, axis=0)
    depth, width = own[0].shape
    low, high = normalized[:, :depth], normalized[:, depth:]
    first = place_ref[0] == 0
    mine = jnp.where(first, low, high)
    theirs = jnp.where(first, high, low)
    sums = [
        jnp.dot(mine, a[...], preferred_element_type=jnp.float32)
        + jnp.dot(theirs, b[...], preferred_element_type=jnp.float32)
        for a, b in zip(own, other)
    ]
    query_ref[...] = (sums[0].astype(jnp.bfloat16).astype(jnp.float32) * (HD ** -0.5)).astype(jnp.bfloat16)
    pair_ref[:, :width] = sums[1].astype(jnp.bfloat16)
    pair_ref[:, width:] = sums[2].astype(jnp.bfloat16)


def project(place, rows, gain, own, other):
    count, depth, width = sum(part.shape[0] for part in rows), rows[0].shape[1], own[0].shape[1]
    return pl.pallas_call(
        functools.partial(project_kernel, len(rows)),
        out_shape=(
            jax.ShapeDtypeStruct((count, width), jnp.bfloat16),
            jax.ShapeDtypeStruct((count, 2 * width), jnp.bfloat16),
        ),
        in_specs=[SMEM] + [VMEM] * (7 + len(rows)),
        out_specs=(VMEM, VMEM),
        compiler_params=pltpu.CompilerParams(vmem_limit_bytes=16 * MIB),
        cost_estimate=pl.CostEstimate(
            flops=2 * count * depth * 3 * width,
            bytes_accessed=2 * (depth * 3 * width + count * (depth + 3 * width)),
            transcendentals=count,
        ),
        name="project",
    )(place, gain, *rows, *own, *other)


def window_kernel(steps, groups, place_ref, *refs):
    queries, owns, sides = refs[:steps], refs[steps:2 * steps], refs[2 * steps:4 * steps]
    q_all, k_all, vt_all, v_all = refs[4 * steps:]
    rows, width = queries[0].shape
    pairs, block = width // LANES, steps * rows
    core = place_ref[0]
    chip_base = jnp.where(core == 0, 2 * block, 0)
    link_base = jnp.where(core == 0, 0, 2 * block)
    for step in range(steps):
        at = place_ref[4 + step] * rows
        q_at = pl.ds(pl.multiple_of(at, 64), rows)
        for pair in range(pairs):
            q_all[pair, q_at, :] = queries[step][:, pair * LANES:(pair + 1) * LANES]
        for source, base in ((owns[step], block), (sides[step], chip_base), (sides[steps + step], link_base)):
            to = pl.ds(pl.multiple_of(base + at, 64), rows)
            for pair in range(pairs):
                k_all[pair, to, :] = source[:, pair * LANES:(pair + 1) * LANES]
                v_all[pair, to, :] = source[:, width + pair * LANES:width + (pair + 1) * LANES]
    for index in range(3 * groups):
        for pair in range(pairs):
            vt_all[pair, index] = v_all[pair, index * GROUP:(index + 1) * GROUP, :].T


def window(place, groups, queries, owns, chip_side, link_side):
    steps = len(queries)
    rows, width = queries[0].shape
    pairs, block = width // LANES, steps * rows
    return pl.pallas_call(
        functools.partial(window_kernel, steps, groups),
        out_shape=(
            jax.ShapeDtypeStruct((pairs, block, LANES), jnp.bfloat16),
            jax.ShapeDtypeStruct((pairs, 3 * block, LANES), jnp.bfloat16),
            jax.ShapeDtypeStruct((pairs, 3 * groups, LANES, GROUP), jnp.bfloat16),
        ),
        in_specs=[SMEM] + [VMEM] * (4 * steps),
        out_specs=(VMEM,) * 3,
        scratch_shapes=[pltpu.VMEM((pairs, 3 * block, LANES), jnp.bfloat16)],
        compiler_params=pltpu.CompilerParams(vmem_limit_bytes=16 * MIB),
        cost_estimate=pl.CostEstimate(flops=0, bytes_accessed=2 * 14 * block * width, transcendentals=0),
        name="window",
    )(place, *queries, *owns, *chip_side, *link_side)


def attend_kernel(groups, reach, count_rows, place_ref, band_ref, turn_ref, q_all, k_all, vt_all, *refs):
    outs, (score, ctx, chosen, limits) = refs[:-4], refs[-4:]
    pairs, rows = q_all.shape[0], outs[0].shape[0]
    first_group, total, length = (place_ref[i] for i in range(1, 4))
    first_row = turn_ref[0]
    slots = 2 * reach + 2
    half_mask = lax.broadcasted_iota(jnp.int32, (GROUP, LANES), 1) < HD
    row_ids = lax.broadcasted_iota(jnp.int32, (GROUP, 2 * GROUP), 0)
    part_group = lax.div(length, jnp.int32(GROUP))
    part_left = lax.rem(length, jnp.int32(GROUP))

    def one_group(place, carry):
        group = first_row // GROUP + place
        for slot in range(slots):
            chosen[slot] = groups + group
        offset = part_group - first_group - group
        column = jnp.clip(jnp.where(offset < 0, offset + reach, offset + reach - 1), 0, 2 * reach - 1)
        cut = (part_left > 0) & (offset != 0) & (jnp.abs(offset) <= reach) & (part_group < total)
        cut = cut & (band_ref[group, column] == 1)
        chosen[1] = jnp.where(cut, groups + group + offset, groups + group)
        limits[0] = jnp.where(cut, part_left, 0)
        count = 1 + cut.astype(jnp.int32)
        for column in range(2 * reach):
            offset = column - reach if column < reach else column - reach + 1
            there = first_group + group + offset
            good = (there >= 0) & (there < part_group) & (there < total) & (band_ref[group, column] == 1)
            chosen[count] = jnp.where(good, groups + group + offset, groups + group)
            limits[0] = jnp.where(good & (count == 1), GROUP, limits[0])
            count = count + good.astype(jnp.int32)
        query_at = pl.ds(pl.multiple_of(group * GROUP, GROUP), GROUP)
        out_at = pl.ds(pl.multiple_of(place * GROUP, GROUP), GROUP)

        def run(size):
            first_limit = limits[0]
            last_limit = jnp.where(count == size, GROUP, 0)
            indices = [chosen[slot] for slot in range(size)]
            best = []
            for pair in range(pairs):
                own = q_all[pair, query_at, :]
                zero = jnp.zeros_like(own)
                both = jnp.concatenate(
                    [jnp.where(half_mask, own, zero), jnp.where(half_mask, zero, own)], axis=0
                ).T
                top = None
                for slot in range(0, size, 2):
                    tiles = [
                        k_all[pair, pl.ds(pl.multiple_of(index * GROUP, GROUP), GROUP), :]
                        for index in indices[slot:slot + 2]
                    ]
                    got = jnp.dot(jnp.concatenate(tiles, axis=0), both, preferred_element_type=jnp.float32)
                    for one in (slot, slot + 1):
                        part = got[(one - slot) * GROUP:(one - slot + 1) * GROUP]
                        if one == 1:
                            part = jnp.where(row_ids < first_limit, part, -jnp.inf)
                        elif one == size - 1:
                            part = jnp.where(row_ids < last_limit, part, -jnp.inf)
                        score[pair, one * GROUP:(one + 1) * GROUP, :] = part
                        high = jnp.max(part.reshape(GROUP // 8, 8, 2 * GROUP), axis=0)
                        top = high if top is None else jnp.maximum(top, high)
                best.append(jnp.max(top, axis=0, keepdims=True))
            for pair in range(pairs):
                total_sum = jnp.zeros((8, 2 * GROUP), jnp.float32)
                mixed = jnp.zeros((LANES, 2 * GROUP), jnp.float32)
                for slot in range(0, size, 2):
                    weights = jnp.exp(score[pair, slot * GROUP:(slot + 2) * GROUP, :] - best[pair])
                    total_sum += jnp.sum(weights.reshape(2 * GROUP // 8, 8, 2 * GROUP), axis=0)
                    tiles = [vt_all[pair, index] for index in indices[slot:slot + 2]]
                    mixed += jnp.dot(
                        jnp.concatenate(tiles, axis=1),
                        weights.astype(jnp.bfloat16),
                        preferred_element_type=jnp.float32,
                    )
                mixed = mixed / jnp.sum(total_sum, axis=0, keepdims=True)
                both_heads = jnp.concatenate([mixed[:HD, :GROUP], mixed[HD:, GROUP:]], axis=0)
                ctx[pair, out_at, :] = both_heads.T.astype(jnp.bfloat16)

        for size in range(2, slots + 1, 2):
            @pl.when((count == size) | (count == size - 1))
            def _():
                run(size)

        return carry

    lax.fori_loop(0, count_rows // GROUP, one_group, 0)
    for place, out in enumerate(outs):
        at = pl.ds(pl.multiple_of(turn_ref[1 + place], 64), rows)
        for pair in range(pairs):
            out[:, pair * LANES:(pair + 1) * LANES] = ctx[pair, at, :]


def attend(place, band, turn, outs, q_all, k_all, vt_all):
    groups, reach = band.shape[0], band.shape[1] // 2
    pairs, block = q_all.shape[:2]
    rows = block // (2 * outs)
    slots = 2 * reach + 2
    work = block // 2 * (reach + 1) * GROUP * 2 * pairs
    return pl.pallas_call(
        functools.partial(attend_kernel, groups, reach, block // 2),
        out_shape=(jax.ShapeDtypeStruct((rows, pairs * LANES), jnp.bfloat16),) * outs,
        in_specs=[SMEM, SMEM, SMEM] + [VMEM] * 3,
        out_specs=(VMEM,) * outs,
        scratch_shapes=[
            pltpu.VMEM((pairs, slots * GROUP, 2 * GROUP), jnp.float32),
            pltpu.VMEM((pairs, block // 2, LANES), jnp.bfloat16),
            pltpu.SMEM((slots + 2,), jnp.int32),
            pltpu.SMEM((1,), jnp.int32),
        ],
        compiler_params=pltpu.CompilerParams(vmem_limit_bytes=20 * MIB),
        cost_estimate=pl.CostEstimate(
            flops=16 * work * HD, bytes_accessed=2 * 7 * block * pairs * LANES, transcendentals=work
        ),
        name="attend",
    )(place, band, turn, q_all, k_all, vt_all)


def output_kernel(share, layers, place_ref, own_ref, far_ref, *refs):
    mine, theirs, contexts, (out_ref, weight) = (
        refs[:share], refs[share:2 * share], refs[2 * share:2 * share + layers], refs[2 * share + layers:]
    )
    core, layer, sharer = (place_ref[i] for i in range(3))
    depth, columns = own_ref.shape
    part = depth // share
    weight[layer, core] = own_ref[...]
    weight[layer, 1 - core] = far_ref[...]
    for other in range(share):
        to = pl.ds(pl.multiple_of((sharer ^ other) * part, part), part)
        for step in range(1, layers):
            there = lax.rem(layer + layers - step, layers)
            weight[there, core, to, :] = mine[other][(step - 1) * part:step * part, :]
            weight[there, 1 - core, to, :] = theirs[other][(step - 1) * part:step * part, :]
    for side in range(2):
        total = None
        for step in range(layers):
            got = jnp.dot(
                contexts[step][...], weight[place_ref[3 + step], side], preferred_element_type=jnp.float32
            )
            total = got if total is None else total + got
        out_ref[0, :, side * columns:(side + 1) * columns] = total.astype(jnp.bfloat16)


def output(place, own, far, mine, theirs, contexts):
    layers = len(contexts)
    rows, width = contexts[0].shape
    depth, columns = own.shape
    return pl.pallas_call(
        functools.partial(output_kernel, len(mine), layers),
        out_shape=jax.ShapeDtypeStruct((1, rows, 2 * columns), jnp.bfloat16),
        in_specs=[SMEM] + [VMEM] * (2 + 2 * len(mine) + layers),
        out_specs=VMEM,
        scratch_shapes=[pltpu.VMEM((layers, 2, depth, columns), jnp.bfloat16)],
        compiler_params=pltpu.CompilerParams(vmem_limit_bytes=20 * MIB),
        cost_estimate=pl.CostEstimate(
            flops=2 * rows * width * layers * 2 * columns,
            bytes_accessed=2 * (width * layers * 2 * columns + 4 * rows * columns),
            transcendentals=0,
        ),
        name="output",
    )(place, own, far, *mine, *theirs, *contexts)


def local(frames, norm_gain, w_query, w_key, w_value, w_out, group_band, lengths):
    cores, seqs, layers = lax.axis_size("dp"), lax.axis_size("seq"), lax.axis_size("head")
    core, seq, layer = lax.axis_index("dp"), lax.axis_index("seq"), lax.axis_index("head")
    groups = group_band.shape[1]
    here = [(c, s) for c in range(cores) for s in range(seqs)]

    def home(c, s):
        return s % 2, s // 2 * 2 + c

    def flat(c, s, z=None):
        return c * seqs + s if z is None else (c * seqs + s) * layers + z

    def moved(value, shift):
        pairs = [(flat(c, s, z), flat(*home(c, s), shift(z))) for c, s in here for z in range(layers)]
        return lax.ppermute(value, ("dp", "seq", "head"), pairs)

    after = ring_successors(layers)
    before = {after[z]: z for z in after}
    swap = [(c, cores - 1 - c) for c in range(cores)]
    over_link = [(flat(1, s), flat(0, s + 2)) for s in range(seqs - 2)]
    over_link += [(flat(0, s + 2), flat(1, s)) for s in range(seqs - 2)]

    ring = [(z, after[z]) for z in range(layers)]
    rows = frames[0]
    middle = rows.shape[0] // 2
    hops = [[moved(part, lambda z: after[z]) for part in (rows[:middle], rows[middle:])]]
    whole = moved(rows, lambda z: z)
    own = (w_query, w_key, w_value)
    other = lax.ppermute(own, "dp", swap)
    facts = jnp.concatenate([group_band[0], jnp.broadcast_to(lengths[:, None], (1, group_band.shape[2]))], axis=0)
    facts = lax.ppermute(facts, ("dp", "seq"), [(flat(c, s), flat(*home(c, s))) for c, s in here])
    w_far = lax.ppermute(w_out, "dp", swap)
    for _ in range(2, layers):
        hops.append([lax.ppermute(part, "head", ring) for part in hops[-1]])

    share = 4 if seqs % 4 == 0 else 2
    part = w_out.shape[0] // share
    piece = lax.dynamic_slice_in_dim(w_out, seq % share * part, part, 0)
    piece, hops[-1][1] = lax.optimization_barrier((piece, hops[-1][1]))
    pieces = [
        lax.ppermute(piece, "head", [(z, (z + step) % layers) for z in range(layers)]) for step in range(1, layers)
    ]
    mine = [jnp.concatenate(pieces, axis=0)]
    for other_sharer in range(1, share):
        mine.append(lax.ppermute(mine[0], "seq", [(s, s ^ other_sharer) for s in range(seqs)]))
    theirs = [lax.ppermute(value, "dp", swap) for value in mine]

    gain = norm_gain[None, :]
    core_at = core[None].astype(jnp.int32)
    queries, owns, chip_side, link_side = [], [], [], []
    for parts in [[whole]] + hops:
        query, pair = project(core_at, parts, gain, own, other)
        queries.append(query)
        owns.append(pair)
        link_side.append(lax.ppermute(pair, ("dp", "seq"), over_link))
        chip_side.append(lax.ppermute(pair, "dp", swap))

    ids = [layer]
    for _ in range(1, layers):
        ids.append(lookup([before[z] for z in range(layers)], ids[-1]))
    place = [core, (seq // 2 * 2 + core) * groups, groups * seqs, facts[groups, 0]] + ids
    place = jnp.stack([jnp.asarray(value, jnp.int32) for value in place])
    band = facts[:groups]
    q_all, k_all, vt_all = window(place, groups, queries, owns, chip_side, link_side)

    half = layers // 2
    arrived, sources = [], []
    for near in (0, 1):
        side = layer // half if near else 1 - layer // half
        first_row = side * half * rows.shape[0]
        turn = [first_row] + [lax.rem(layer + e, half) * rows.shape[0] for e in range(half)]
        turn = jnp.stack([jnp.asarray(value, jnp.int32) for value in turn])
        for e, context in enumerate(attend(place, band, turn, half, q_all, k_all, vt_all)):
            def target(z, e=e):
                return (z // half if near else 1 - z // half) * half + (z + e) % half

            arrived.append(moved(context, target))
            sources.append(side * half + lax.rem(layer + half - e, half))
    last = jnp.stack([jnp.asarray(value, jnp.int32) for value in [core, layer, seq % share] + sources])
    return output(last, w_out, w_far, mine, theirs, arrived)


def solution(mesh):
    return jax.shard_map(
        local,
        mesh=mesh,
        in_specs=(
            P("dp", ("seq", "head"), None),
            P(),
            P("dp", "head"),
            P("dp", "head"),
            P("dp", "head"),
            P("head", "dp"),
            P("dp", "seq", None),
            P("dp"),
        ),
        out_specs=P("dp", ("seq", "head"), None),
        check_vma=False,
    )
```

```python
import functools

import jax
import jax.numpy as jnp
from jax import lax
from jax.experimental import pallas as pl
from jax.experimental.pallas import tpu as pltpu
from jax.sharding import PartitionSpec as P

HD = 64
GROUP = 128
LANES = 128

epsilon = 1e-05

VMEM = pl.BlockSpec(memory_space=pltpu.VMEM)
SMEM = pl.BlockSpec(memory_space=pltpu.SMEM)
ANY = pl.BlockSpec(memory_space=pl.ANY)
MIB = 1024 * 1024
LIGHT = pl.CostEstimate(flops=1, bytes_accessed=1, transcendentals=0)


def ring_successors(count):
    order = [0] + list(range(1, count, 2)) + list(range(count - 2 + count % 2, 0, -2))
    return {order[i]: order[(i + 1) % count] for i in range(count)}


def lookup(table, index):
    value = jnp.int32(table[0])
    for place in range(1, len(table)):
        value = jnp.where(index == place, jnp.int32(table[place]), value)
    return value


def copy_all(pairs, sems):
    copies = [pltpu.make_async_copy(source, target, sems.at[i]) for i, (source, target) in enumerate(pairs)]
    for copy in copies:
        copy.start()
    return copies


def pack_kernel(place_ref, rows_ref, w_out_ref, out_ref, sems):
    count = rows_ref.shape[0]
    part, columns = (out_ref.shape[0] - count), w_out_ref.shape[1]
    first = pl.multiple_of(place_ref[0] * 2 * part, 2 * part)
    pairs = [(rows_ref, out_ref.at[pl.ds(0, count), :])]
    for side in range(2):
        pairs.append((
            w_out_ref.at[pl.ds(first + side * part, part), :],
            out_ref.at[pl.ds(count, part), pl.ds(side * columns, columns)],
        ))
    for copy in copy_all(pairs, sems):
        copy.wait()


def pack(place, rows, w_out, share):
    part = w_out.shape[0] // share // 2
    return pl.pallas_call(
        pack_kernel,
        out_shape=jax.ShapeDtypeStruct((rows.shape[0] + part, rows.shape[1]), jnp.bfloat16),
        in_specs=[SMEM, ANY, ANY],
        out_specs=ANY,
        scratch_shapes=[pltpu.SemaphoreType.DMA((3,))],
        compiler_params=pltpu.CompilerParams(vmem_limit_bytes=MIB),
        cost_estimate=LIGHT,
        name="pack",
    )(place, rows, w_out)


def project_kernel(blocks, count, stacked, place_ref, gain_ref, *refs):
    rows, own, other = refs[:blocks], refs[blocks], refs[blocks + 1]
    extra = refs[blocks + 2:blocks + 2 + stacked]
    outs = refs[blocks + 2 + stacked:]
    query_ref, pair_ref = outs[:2]
    held, mine_ref, theirs_ref, sems = outs[-4:]
    depth, width = own.shape[0], query_ref.shape[1]
    loads = copy_all(
        [(rows[i].at[pl.ds(0, count), :], held.at[pl.ds(i * count, count), :]) for i in range(blocks)], sems
    )
    loads += copy_all(
        [(own.at[:, pl.ds(0, 3 * width)], mine_ref), (other.at[:, pl.ds(0, 3 * width)], theirs_ref)],
        sems.at[pl.ds(blocks, 2)],
    )
    sides = []
    for i, source in enumerate(extra):
        part = source.shape[0] - count
        sides.append((source.at[pl.ds(count, part), :], outs[2].at[pl.ds(i * part, part), :]))
    sides = copy_all(sides, sems.at[pl.ds(blocks + 2, max(1, stacked))])
    gain = gain_ref[...]
    first = place_ref[0] == 0
    mine, theirs = [], []
    for i in range(blocks):
        loads[i].wait()
        values = held[i * count:(i + 1) * count, :].astype(jnp.float32)
        center = values - jnp.mean(values, axis=-1, keepdims=True)
        spread = jnp.mean(center * center, axis=-1, keepdims=True)
        normalized = (center * lax.rsqrt(spread + epsilon) * gain).astype(jnp.bfloat16)
        low, high = normalized[:, :depth], normalized[:, depth:]
        mine.append(jnp.where(first, low, high))
        theirs.append(jnp.where(first, high, low))
    for load in loads[blocks:]:
        load.wait()
    mine = mine[0] if blocks == 1 else jnp.concatenate(mine, axis=0)
    theirs = theirs[0] if blocks == 1 else jnp.concatenate(theirs, axis=0)
    for place in range(3):
        columns = slice(place * width, (place + 1) * width)
        got = jnp.dot(mine, mine_ref[:, columns], preferred_element_type=jnp.float32)
        got = (got + jnp.dot(theirs, theirs_ref[:, columns], preferred_element_type=jnp.float32)).astype(jnp.bfloat16)
        if place == 0:
            query_ref[...] = (got.astype(jnp.float32) * (HD ** -0.5)).astype(jnp.bfloat16)
        else:
            pair_ref[:, (place - 1) * width:place * width] = got
    for copy in sides:
        copy.wait()


def project(place, rows, count, width, gain, own, other, extra=()):
    blocks, depth = len(rows), rows[0].shape[1]
    total = blocks * count
    part = extra[0].shape[0] - count if extra else 0
    out_shape = [
        jax.ShapeDtypeStruct((total, width), jnp.bfloat16),
        jax.ShapeDtypeStruct((total, 2 * width), jnp.bfloat16),
    ]
    if extra:
        out_shape.append(jax.ShapeDtypeStruct((len(extra) * part, depth), jnp.bfloat16))
    return pl.pallas_call(
        functools.partial(project_kernel, blocks, count, len(extra)),
        out_shape=out_shape,
        in_specs=[SMEM, VMEM] + [ANY] * (blocks + 2 + len(extra)),
        out_specs=[VMEM, VMEM] + [ANY] * (1 if extra else 0),
        scratch_shapes=[
            pltpu.VMEM((total, depth), jnp.bfloat16),
            pltpu.VMEM((own.shape[0], 3 * width), jnp.bfloat16),
            pltpu.VMEM((own.shape[0], 3 * width), jnp.bfloat16),
            pltpu.SemaphoreType.DMA((blocks + 2 + max(1, len(extra)),)),
        ],
        compiler_params=pltpu.CompilerParams(vmem_limit_bytes=20 * MIB),
        cost_estimate=pl.CostEstimate(
            flops=2 * total * depth * 3 * width,
            bytes_accessed=2 * (depth * 3 * width + total * (depth + 3 * width)),
            transcendentals=total,
        ),
        name="project",
    )(place, gain, *rows, own, other, *extra)


def window_kernel(shape, groups, place_ref, *refs):
    kinds = len(shape)
    queries, owns, sides = refs[:kinds], refs[kinds:2 * kinds], refs[2 * kinds:4 * kinds]
    q_all, kv_all, vt_all, sems = refs[4 * kinds:]
    block, width = q_all.shape
    rows = block // sum(shape)
    core = place_ref[0]
    chip_base = jnp.where(core == 0, 2 * block, 0)
    link_base = jnp.where(core == 0, 0, 2 * block)
    pairs, step = [], 0
    for kind in range(kinds):
        for inside in range(shape[kind]):
            at = place_ref[4 + step] * rows
            part = pl.ds(inside * rows, rows)
            pairs.append((queries[kind].at[part, :], q_all.at[pl.ds(pl.multiple_of(at, 64), rows), :]))
            for source, base in (
                (owns[kind], block), (sides[kind], chip_base), (sides[kinds + kind], link_base)
            ):
                to = pl.ds(pl.multiple_of(base + at, 64), rows)
                pairs.append((source.at[part, :], kv_all.at[to, :]))
            step += 1
    for copy in copy_all(pairs, sems):
        copy.wait()
    for index in range(3 * groups):
        for pair in range(width // LANES):
            columns = slice(width + pair * LANES, width + (pair + 1) * LANES)
            vt_all[pair, index] = kv_all[index * GROUP:(index + 1) * GROUP, columns].T


def window(place, groups, rows, queries, owns, chip_side, link_side):
    shape = [query.shape[0] // rows for query in queries]
    width, block = queries[0].shape[1], sum(shape) * rows
    pairs = width // LANES
    return pl.pallas_call(
        functools.partial(window_kernel, shape, groups),
        out_shape=(
            jax.ShapeDtypeStruct((block, width), jnp.bfloat16),
            jax.ShapeDtypeStruct((3 * block, 2 * width), jnp.bfloat16),
            jax.ShapeDtypeStruct((pairs, 3 * groups, LANES, GROUP), jnp.bfloat16),
        ),
        in_specs=[SMEM] + [ANY] * (4 * len(shape)),
        out_specs=(VMEM,) * 3,
        scratch_shapes=[pltpu.SemaphoreType.DMA((4 * sum(shape),))],
        compiler_params=pltpu.CompilerParams(vmem_limit_bytes=16 * MIB),
        cost_estimate=pl.CostEstimate(flops=0, bytes_accessed=2 * 14 * block * width, transcendentals=0),
        name="window",
    )(place, *queries, *owns, *chip_side, *link_side)


def attend_kernel(groups, reach, count_rows, place_ref, band_ref, turn_ref, q_all, kv_all, vt_all, *refs):
    outs, (score, ctx, chosen, limits) = refs[:-4], refs[-4:]
    pairs, rows = vt_all.shape[0], outs[0].shape[0]
    first_group, total, length = (place_ref[i] for i in range(1, 4))
    first_row = turn_ref[0]
    slots = 2 * reach + 2
    half_mask = lax.broadcasted_iota(jnp.int32, (GROUP, LANES), 1) < HD
    row_ids = lax.broadcasted_iota(jnp.int32, (GROUP, 2 * GROUP), 0)
    part_group = lax.div(length, jnp.int32(GROUP))
    part_left = lax.rem(length, jnp.int32(GROUP))

    def one_group(place, carry):
        group = first_row // GROUP + place
        for slot in range(slots):
            chosen[slot] = groups + group
        offset = part_group - first_group - group
        column = jnp.clip(jnp.where(offset < 0, offset + reach, offset + reach - 1), 0, 2 * reach - 1)
        cut = (part_left > 0) & (offset != 0) & (jnp.abs(offset) <= reach) & (part_group < total)
        cut = cut & (band_ref[group, column] == 1)
        chosen[1] = jnp.where(cut, groups + group + offset, groups + group)
        limits[0] = jnp.where(cut, part_left, 0)
        count = 1 + cut.astype(jnp.int32)
        for column in range(2 * reach):
            offset = column - reach if column < reach else column - reach + 1
            there = first_group + group + offset
            good = (there >= 0) & (there < part_group) & (there < total) & (band_ref[group, column] == 1)
            chosen[count] = jnp.where(good, groups + group + offset, groups + group)
            limits[0] = jnp.where(good & (count == 1), GROUP, limits[0])
            count = count + good.astype(jnp.int32)
        query_at = pl.ds(pl.multiple_of(group * GROUP, GROUP), GROUP)
        out_at = pl.ds(pl.multiple_of(place * GROUP, GROUP), GROUP)

        def run(size):
            first_limit = limits[0]
            last_limit = jnp.where(count == size, GROUP, 0)
            indices = [chosen[slot] for slot in range(size)]
            best = []
            for pair in range(pairs):
                own = q_all[query_at, pair * LANES:(pair + 1) * LANES]
                zero = jnp.zeros_like(own)
                both = jnp.concatenate(
                    [jnp.where(half_mask, own, zero), jnp.where(half_mask, zero, own)], axis=0
                ).T
                top = None
                for slot in range(0, size, 2):
                    tiles = [
                        kv_all[pl.ds(pl.multiple_of(index * GROUP, GROUP), GROUP), pair * LANES:(pair + 1) * LANES]
                        for index in indices[slot:slot + 2]
                    ]
                    got = jnp.dot(jnp.concatenate(tiles, axis=0), both, preferred_element_type=jnp.float32)
                    for one in (slot, slot + 1):
                        part = got[(one - slot) * GROUP:(one - slot + 1) * GROUP]
                        if one == 1:
                            part = jnp.where(row_ids < first_limit, part, -jnp.inf)
                        elif one == size - 1:
                            part = jnp.where(row_ids < last_limit, part, -jnp.inf)
                        score[pair, one * GROUP:(one + 1) * GROUP, :] = part
                        high = jnp.max(part.reshape(GROUP // 8, 8, 2 * GROUP), axis=0)
                        top = high if top is None else jnp.maximum(top, high)
                best.append(jnp.max(top, axis=0, keepdims=True))
            for pair in range(pairs):
                total_sum = jnp.zeros((8, 2 * GROUP), jnp.float32)
                mixed = jnp.zeros((LANES, 2 * GROUP), jnp.float32)
                for slot in range(0, size, 2):
                    weights = jnp.exp(score[pair, slot * GROUP:(slot + 2) * GROUP, :] - best[pair])
                    total_sum += jnp.sum(weights.reshape(2 * GROUP // 8, 8, 2 * GROUP), axis=0)
                    tiles = [vt_all[pair, index] for index in indices[slot:slot + 2]]
                    mixed += jnp.dot(
                        jnp.concatenate(tiles, axis=1),
                        weights.astype(jnp.bfloat16),
                        preferred_element_type=jnp.float32,
                    )
                mixed = mixed / jnp.sum(total_sum, axis=0, keepdims=True)
                both_heads = jnp.concatenate([mixed[:HD, :GROUP], mixed[HD:, GROUP:]], axis=0)
                ctx[pair, out_at, :] = both_heads.T.astype(jnp.bfloat16)

        for size in range(2, slots + 1, 2):
            @pl.when((count == size) | (count == size - 1))
            def _():
                run(size)

        return carry

    lax.fori_loop(0, count_rows // GROUP, one_group, 0)
    for place, out in enumerate(outs):
        at = pl.ds(pl.multiple_of(turn_ref[1 + place], 64), rows)
        for pair in range(pairs):
            out[:, pair * LANES:(pair + 1) * LANES] = ctx[pair, at, :]


def attend(place, band, turn, outs, q_all, kv_all, vt_all):
    groups, reach = band.shape[0], band.shape[1] // 2
    pairs, block = vt_all.shape[0], q_all.shape[0]
    rows = block // (2 * outs)
    slots = 2 * reach + 2
    return pl.pallas_call(
        functools.partial(attend_kernel, groups, reach, block // 2),
        out_shape=[jax.ShapeDtypeStruct((rows, pairs * LANES), jnp.bfloat16)] * outs,
        in_specs=[SMEM, SMEM, SMEM] + [VMEM] * 3,
        out_specs=[VMEM] * outs,
        scratch_shapes=[
            pltpu.VMEM((pairs, slots * GROUP, 2 * GROUP), jnp.float32),
            pltpu.VMEM((pairs, block // 2, LANES), jnp.bfloat16),
            pltpu.SMEM((slots + 2,), jnp.int32),
            pltpu.SMEM((1,), jnp.int32),
        ],
        compiler_params=pltpu.CompilerParams(vmem_limit_bytes=16 * MIB),
        cost_estimate=pl.CostEstimate(flops=1 << 32, bytes_accessed=1 << 20, transcendentals=0),
        name="attend",
    )(place, band, turn, q_all, kv_all, vt_all)


def join_kernel(*refs):
    sources, out, sems = refs[:-2], refs[-2], refs[-1]
    pairs, at = [], 0
    for source in sources:
        pairs.append((source, out.at[pl.ds(at, source.shape[0]), :]))
        at += source.shape[0]
    for copy in copy_all(pairs, sems):
        copy.wait()


def join(values):
    rows = sum(value.shape[0] for value in values)
    return pl.pallas_call(
        join_kernel,
        out_shape=jax.ShapeDtypeStruct((rows, values[0].shape[1]), jnp.bfloat16),
        in_specs=[ANY] * len(values),
        out_specs=ANY,
        scratch_shapes=[pltpu.SemaphoreType.DMA((len(values),))],
        compiler_params=pltpu.CompilerParams(vmem_limit_bytes=MIB),
        cost_estimate=LIGHT,
        name="join",
    )(*values)


def place_kernel(share, place_ref, own_ref, far_ref, mine_ref, theirs_ref, *refs):
    out_ref, sems = refs[-2:]
    core, layer, seq = (place_ref[i] for i in range(3))
    layers, _, depth, columns = out_ref.shape
    part = depth // share // 2
    half = columns // 2
    pairs = [(own_ref, out_ref.at[layer, core])]
    for side in range(2):
        pairs.append((
            far_ref.at[pl.ds(side * depth, depth), pl.ds(far_ref.shape[1] - half, half)],
            out_ref.at[layer, 1 - core, :, pl.ds(side * half, half)],
        ))
    for other in range(share):
        there = seq ^ other
        for source, source_core in ((mine_ref, core), (theirs_ref, 1 - core)):
            at = lax.rem(there // 2 * 2 + source_core, share) * 2 * part
            for step in range(layers - 1):
                row = (other * (layers - 1) + step) * part
                for side in range(2):
                    pairs.append((
                        source.at[pl.ds(row, part), pl.ds(side * columns, columns)],
                        out_ref.at[
                            place_ref[3 + step], lax.rem(there, 2),
                            pl.ds(pl.multiple_of(at + side * part, 16), part), :
                        ],
                    ))
    for copy in copy_all(pairs, sems):
        copy.wait()


def place_weights(place, share, layers, own, far, mine, theirs, held):
    depth, columns = own.shape
    return pl.pallas_call(
        functools.partial(place_kernel, share),
        out_shape=jax.ShapeDtypeStruct((layers, 2, depth, columns), jnp.bfloat16),
        in_specs=[SMEM] + [ANY] * (4 + len(held)),
        out_specs=VMEM,
        scratch_shapes=[pltpu.SemaphoreType.DMA((3 + 4 * share * (layers - 1),))],
        compiler_params=pltpu.CompilerParams(vmem_limit_bytes=8 * MIB),
        cost_estimate=LIGHT,
        name="place",
    )(place, own, far, mine, theirs, *held)


def output_kernel(layers, place_ref, weight, *refs):
    contexts, out_ref = refs[:layers], refs[layers]
    columns = weight.shape[3]
    for side in range(2):
        total = None
        for step in range(layers):
            got = jnp.dot(contexts[step][...], weight[place_ref[step], side], preferred_element_type=jnp.float32)
            total = got if total is None else total + got
        out_ref[0, :, side * columns:(side + 1) * columns] = total.astype(jnp.bfloat16)


def output(place, weight, contexts):
    layers, _, depth, columns = weight.shape
    rows, width = contexts[0].shape
    return pl.pallas_call(
        functools.partial(output_kernel, layers),
        out_shape=jax.ShapeDtypeStruct((1, rows, 2 * columns), jnp.bfloat16),
        in_specs=[SMEM] + [VMEM] * (1 + layers),
        out_specs=VMEM,
        compiler_params=pltpu.CompilerParams(vmem_limit_bytes=12 * MIB),
        cost_estimate=LIGHT,
        name="output",
    )(place, weight, *contexts)


def hold_kernel(*refs):
    del refs


def hold(values):
    return pl.pallas_call(
        hold_kernel,
        out_shape=[jax.ShapeDtypeStruct(value.shape, value.dtype) for value in values],
        in_specs=[ANY] * len(values),
        out_specs=[ANY] * len(values),
        input_output_aliases={i: i for i in range(len(values))},
        compiler_params=pltpu.CompilerParams(vmem_limit_bytes=MIB),
        cost_estimate=pl.CostEstimate(flops=1 << 30, bytes_accessed=1, transcendentals=0),
        name="hold",
    )(*values)


def together(*values):
    return lax.optimization_barrier(values)


def numbers(*values):
    return jnp.stack([jnp.asarray(value, jnp.int32) for value in values])


def local(frames, norm_gain, w_query, w_key, w_value, w_out, group_band, lengths):
    cores, seqs, layers = lax.axis_size("dp"), lax.axis_size("seq"), lax.axis_size("head")
    core, seq, layer = lax.axis_index("dp"), lax.axis_index("seq"), lax.axis_index("head")
    groups = group_band.shape[1]
    width = w_query.shape[1]
    here = [(c, s) for c in range(cores) for s in range(seqs)]

    def home(c, s):
        return s % 2, s // 2 * 2 + c

    def flat(c, s, z=None):
        return c * seqs + s if z is None else (c * seqs + s) * layers + z

    def moved(value, shift):
        pairs = [(flat(c, s, z), flat(*home(c, s), shift(z))) for c, s in here for z in range(layers)]
        return lax.ppermute(value, ("dp", "seq", "head"), pairs)

    after = ring_successors(layers)
    before = {after[z]: z for z in after}
    swap = [(c, cores - 1 - c) for c in range(cores)]
    over_link = [(flat(1, s), flat(0, s + 2)) for s in range(seqs - 2)]
    over_link += [(flat(0, s + 2), flat(1, s)) for s in range(seqs - 2)]
    share = 4 if seqs % 4 == 0 else 2

    def halos(pair):
        return lax.ppermute(pair, ("dp", "seq"), over_link), lax.ppermute(pair, "dp", swap)

    def shared(value):
        return [value] + [
            lax.ppermute(value, "seq", [(s, s ^ other) for s in range(seqs)]) for other in range(1, share)
        ]

    rows = frames[0]
    count = rows.shape[0]
    sent = pack(numbers(lax.rem(seq, share)), rows, w_out, share)
    first = moved(sent, lambda z: after[z])
    whole = moved(rows, lambda z: z)
    sent, w_query, w_key, w_value, weights_out = together(sent, w_query, w_key, w_value, w_out)
    half = w_out.shape[1] // 2
    own = jnp.concatenate(
        [w_query, w_key, w_value, jnp.concatenate([weights_out[:, :half], weights_out[:, half:]], axis=0)], axis=1
    )
    third = moved(sent, lambda z: before[z])
    facts = jnp.concatenate([group_band[0], jnp.broadcast_to(lengths[:, None], (1, group_band.shape[2]))], axis=0)
    facts = lax.ppermute(facts, ("dp", "seq"), [(flat(c, s), flat(*home(c, s))) for c, s in here])
    far = lax.ppermute(own, "dp", swap)
    second = lax.ppermute(first, "head", [(z, after[z]) for z in range(layers)])

    gain = norm_gain[None, :]
    far, facts = together(far, facts)
    core_at = numbers(core)
    query_a, pair_a = project(core_at, [whole, first], count, width, gain, own, far)
    link_a, chip_a = halos(pair_a)
    third, pair_a = together(third, pair_a)
    query_b, pair_b = project(core_at, [third], count, width, gain, own, far)
    link_b, chip_b = halos(pair_b)
    second, pair_b = together(second, pair_b)
    query_c, pair_c, stack = project(core_at, [second], count, width, gain, own, far, extra=(first, third, second))
    pair_c, link_a, chip_a, link_b, chip_b = together(pair_c, link_a, chip_a, link_b, chip_b)
    link_c, chip_c = halos(pair_c)
    shares = shared(stack)

    back = {z: before[z] for z in range(layers)}
    ids = [layer, lookup([back[z] for z in range(layers)], layer)]
    ids.append(lookup([after[z] for z in range(layers)], layer))
    ids.append(lookup([back[back[z]] for z in range(layers)], layer))
    place = numbers(core, (seq // 2 * 2 + core) * groups, groups * seqs, facts[groups, 0], *ids)
    band = facts[:groups]
    q_all, kv_all, vt_all = window(
        place, groups, count, [query_a, query_b, query_c], [pair_a, pair_b, pair_c],
        [chip_a, chip_b, chip_c], [link_a, link_b, link_c],
    )
    half = layers // 2
    arrived, sources = [], []
    for near in (0, 1):
        side = layer // half if near else 1 - layer // half
        turn = numbers(side * half * count, *[lax.rem(layer + e, half) * count for e in range(half)])
        contexts = list(attend(place, band, turn, half, q_all, kv_all, vt_all))
        if near:
            contexts[0], contexts[1], *shares = together(contexts[0], contexts[1], *shares)
            mine = join(shares)
            theirs = lax.ppermute(mine, "dp", swap)
        else:
            contexts[0], q_all = together(contexts[0], q_all)
        for e, context in enumerate(contexts):
            def target(z, e=e):
                return (z // half if near else 1 - z // half) * half + (z + e) % half

            arrived.append(moved(context, target))
            sources.append(side * half + lax.rem(layer + half - e, half))
    held = hold(arrived[:half])
    weight = place_weights(numbers(core, layer, seq, *ids[1:]), share, layers, w_out, far, mine, theirs, held)
    arrived = list(held) + arrived[half:]
    return output(numbers(*sources), weight, arrived)


def solution(mesh):
    return jax.shard_map(
        local,
        mesh=mesh,
        in_specs=(
            P("dp", ("seq", "head"), None),
            P(),
            P("dp", "head"),
            P("dp", "head"),
            P("dp", "head"),
            P("head", "dp"),
            P("dp", "seq", None),
            P("dp"),
        ),
        out_specs=P("dp", ("seq", "head"), None),
        check_vma=False,
    )
```

```python
import functools

import jax
import jax.numpy as jnp
from jax import lax
from jax.experimental import pallas as pl
from jax.experimental.pallas import tpu as pltpu
from jax.sharding import PartitionSpec as P

HD = 64
GROUP = 128
LANES = 128

epsilon = 1e-05

VMEM = pl.BlockSpec(memory_space=pltpu.VMEM)
SMEM = pl.BlockSpec(memory_space=pltpu.SMEM)
HBM = pl.BlockSpec(memory_space=pltpu.HBM)
MIB = 1024 * 1024
LIGHT = pl.CostEstimate(flops=1, bytes_accessed=1, transcendentals=0)


def ring_successors(count):
    order = [0] + list(range(1, count, 2)) + list(range(count - 2 + count % 2, 0, -2))
    return {order[i]: order[(i + 1) % count] for i in range(count)}


def lookup(table, index):
    value = jnp.int32(table[0])
    for place in range(1, len(table)):
        value = jnp.where(index == place, jnp.int32(table[place]), value)
    return value


def copy_all(pairs, sems):
    copies = [pltpu.make_async_copy(source, target, sems.at[i]) for i, (source, target) in enumerate(pairs)]
    for copy in copies:
        copy.start()
    return copies


def in_hbm(*values):
    return [pltpu.with_memory_space_constraint(value, pltpu.HBM) for value in values]


def pack_kernel(place_ref, rows_ref, query_ref, key_ref, value_ref, w_out_ref, sent_ref, piece_ref, all_ref, *refs):
    held_sent, held_piece, held, sems = refs
    depth, width = query_ref.shape
    count = rows_ref.shape[0]
    part, columns = piece_ref.shape
    first = pl.multiple_of(place_ref[0] * part, 16)
    pairs = [(rows_ref, held_sent.at[pl.ds(0, count), :]), (w_out_ref.at[pl.ds(first, part), :], held_piece)]
    for side in range(2):
        pairs.append((
            w_out_ref.at[pl.ds(first + side * part // 2, part // 2), :],
            held_sent.at[pl.ds(count, part // 2), pl.ds(side * columns, columns)],
        ))
    for place, source in enumerate((query_ref, key_ref, value_ref)):
        pairs.append((source, held.at[:, pl.ds(place * width, width)]))
    rows = w_out_ref.shape[0]
    for side in range(2):
        pairs.append((
            w_out_ref.at[:, pl.ds(side * width, width)],
            held.at[pl.ds(side * rows, rows), pl.ds(3 * width, width)],
        ))
    loads = copy_all(pairs, sems)
    for load in loads[:4]:
        load.wait()
    stores = copy_all([(held_sent, sent_ref), (held_piece, piece_ref)], sems.at[pl.ds(len(pairs), 2)])
    for load in loads[4:]:
        load.wait()
    stores += copy_all([(held, all_ref)], sems.at[pl.ds(len(pairs) + 2, 1)])
    for store in stores:
        store.wait()


def pack(place, rows, w_query, w_key, w_value, w_out, share):
    depth, width = w_query.shape
    part = w_out.shape[0] // share
    shapes = [
        (rows.shape[0] + part // 2, rows.shape[1]), (part, w_out.shape[1]), (depth, 4 * width)
    ]
    return pl.pallas_call(
        pack_kernel,
        out_shape=[pltpu.HBM(shape, jnp.bfloat16) for shape in shapes],
        in_specs=[SMEM] + [HBM] * 5,
        out_specs=[HBM] * 3,
        scratch_shapes=[pltpu.VMEM(shape, jnp.bfloat16) for shape in shapes] + [pltpu.SemaphoreType.DMA((12,))],
        compiler_params=pltpu.CompilerParams(vmem_limit_bytes=8 * MIB),
        cost_estimate=LIGHT,
        name="pack",
    )(place, *in_hbm(rows, w_query, w_key, w_value, w_out))


def join_kernel(skips, *refs):
    sources, (out, held, sems) = refs[:-3], refs[-3:]
    spans, parts, at = [], [], 0
    columns = held.shape[1]
    for skip, source in zip(skips, sources):
        rows = source.shape[0] - skip
        if source.shape[1] == columns:
            parts.append((source.at[pl.ds(skip, rows), :], held.at[pl.ds(at, rows), :]))
        else:
            rows //= 2
            for side in range(2):
                parts.append((
                    source.at[pl.ds(side * rows, rows), :],
                    held.at[pl.ds(at, rows), pl.ds(side * source.shape[1], source.shape[1])],
                ))
        spans.append(pl.ds(at, rows))
        at += rows
    for load in copy_all(parts, sems):
        load.wait()
    for store in copy_all([(held.at[span, :], out.at[span, :]) for span in spans], sems.at[pl.ds(len(parts), len(spans))]):
        store.wait()


def join(values, skips=None):
    skips = [0] * len(values) if skips is None else skips
    columns = max(value.shape[1] for value in values)
    rows = sum((value.shape[0] - skip) * value.shape[1] // columns for value, skip in zip(values, skips))
    return pl.pallas_call(
        functools.partial(join_kernel, tuple(skips)),
        out_shape=pltpu.HBM((rows, columns), jnp.bfloat16),
        in_specs=[HBM] * len(values),
        out_specs=HBM,
        scratch_shapes=[
            pltpu.VMEM((rows, columns), jnp.bfloat16), pltpu.SemaphoreType.DMA((3 * len(values),))
        ],
        compiler_params=pltpu.CompilerParams(vmem_limit_bytes=4 * MIB),
        cost_estimate=LIGHT,
        name="join",
    )(*values)


def project_kernel(blocks, count, gain_ref, weight_ref, *refs):
    rows = refs[:blocks]
    query_ref, pair_ref, held, weight, query_held, pair_held, sems = refs[blocks:]
    width = query_ref.shape[1]
    order = (1, 2, 0)
    loads = copy_all(
        [(rows[i].at[pl.ds(0, count), :], held.at[pl.ds(i * count, count), :]) for i in range(blocks)], sems
    )
    fetches = copy_all(
        [(weight_ref.at[:, pl.ds(place * width, width)], weight.at[place]) for place in order],
        sems.at[pl.ds(blocks, 3)],
    )
    gain = gain_ref[...]
    normalized = []
    for i in range(blocks):
        loads[i].wait()
        values = held[i * count:(i + 1) * count, :].astype(jnp.float32)
        center = values - jnp.mean(values, axis=-1, keepdims=True)
        spread = jnp.mean(center * center, axis=-1, keepdims=True)
        normalized.append((center * lax.rsqrt(spread + epsilon) * gain).astype(jnp.bfloat16))
    normalized = normalized[0] if blocks == 1 else jnp.concatenate(normalized, axis=0)
    stores = []
    for place, fetch in zip(order, fetches):
        fetch.wait()
        got = jnp.dot(normalized, weight[place], preferred_element_type=jnp.float32).astype(jnp.bfloat16)
        sem = sems.at[pl.ds(blocks + 3 + place, 1)]
        if place == 0:
            query_held[...] = (got.astype(jnp.float32) * (HD ** -0.5)).astype(jnp.bfloat16)
            stores += copy_all([(query_held, query_ref)], sem)
        else:
            part = pl.ds((place - 1) * width, width)
            pair_held[:, (place - 1) * width:place * width] = got
            stores += copy_all([(pair_held.at[:, part], pair_ref.at[:, part])], sem)
    for store in stores:
        store.wait()


def project(rows, count, width, gain, weight, cost):
    blocks, depth = len(rows), rows[0].shape[1]
    total = blocks * count
    return pl.pallas_call(
        functools.partial(project_kernel, blocks, count),
        out_shape=[pltpu.HBM((total, width), jnp.bfloat16), pltpu.HBM((total, 2 * width), jnp.bfloat16)],
        in_specs=[VMEM] + [HBM] * (blocks + 1),
        out_specs=[HBM, HBM],
        scratch_shapes=[
            pltpu.VMEM((total, depth), jnp.bfloat16),
            pltpu.VMEM((3, depth, width), jnp.bfloat16),
            pltpu.VMEM((total, width), jnp.bfloat16),
            pltpu.VMEM((total, 2 * width), jnp.bfloat16),
            pltpu.SemaphoreType.DMA((blocks + 6,)),
        ],
        compiler_params=pltpu.CompilerParams(vmem_limit_bytes=24 * MIB),
        cost_estimate=pl.CostEstimate(flops=cost, bytes_accessed=1, transcendentals=0),
        name="project",
    )(gain, *in_hbm(weight), *rows)


def window_kernel(shape, groups, place_ref, *refs):
    kinds = len(shape)
    queries, owns, sides = refs[:kinds], refs[kinds:2 * kinds], refs[2 * kinds:4 * kinds]
    q_all, kv_all, vt_all, sems = refs[4 * kinds:]
    block, width = q_all.shape
    rows = block // sum(shape)
    core = place_ref[0]
    chip_base = jnp.where(core == 0, 2 * block, 0)
    link_base = jnp.where(core == 0, 0, 2 * block)
    pairs, step = [], 0
    for kind in range(kinds):
        for inside in range(shape[kind]):
            at = place_ref[4 + step] * rows
            part = pl.ds(inside * rows, rows)
            pairs.append((queries[kind].at[part, :], q_all.at[pl.ds(pl.multiple_of(at, 64), rows), :]))
            for source, base in (
                (owns[kind], block), (sides[kind], chip_base), (sides[kinds + kind], link_base)
            ):
                to = pl.ds(pl.multiple_of(base + at, 64), rows)
                taken = source.at[1 - core, part, :] if len(source.shape) == 3 else source.at[part, :]
                pairs.append((taken, kv_all.at[to, :]))
            step += 1
    for copy in copy_all(pairs, sems):
        copy.wait()
    for index in range(3 * groups):
        for pair in range(width // LANES):
            columns = slice(width + pair * LANES, width + (pair + 1) * LANES)
            vt_all[pair, index] = kv_all[index * GROUP:(index + 1) * GROUP, columns].T


def window(place, groups, rows, queries, owns, chip_side, link_side):
    shape = [query.shape[0] // rows for query in queries]
    width, block = queries[0].shape[1], sum(shape) * rows
    pairs = width // LANES
    return pl.pallas_call(
        functools.partial(window_kernel, shape, groups),
        out_shape=(
            jax.ShapeDtypeStruct((block, width), jnp.bfloat16),
            jax.ShapeDtypeStruct((3 * block, 2 * width), jnp.bfloat16),
            jax.ShapeDtypeStruct((pairs, 3 * groups, LANES, GROUP), jnp.bfloat16),
        ),
        in_specs=[SMEM] + [HBM] * (4 * len(shape)),
        out_specs=(VMEM,) * 3,
        scratch_shapes=[pltpu.SemaphoreType.DMA((4 * sum(shape),))],
        compiler_params=pltpu.CompilerParams(vmem_limit_bytes=16 * MIB),
        cost_estimate=pl.CostEstimate(flops=0, bytes_accessed=2 * 14 * block * width, transcendentals=0),
        name="window",
    )(place, *in_hbm(*queries, *owns, *[side for side in chip_side if side.ndim == 3]),
      *[side for side in chip_side if side.ndim == 2], *link_side)


def attend_kernel(groups, reach, count_rows, place_ref, band_ref, turn_ref, q_all, kv_all, vt_all, *refs):
    outs, (score, ctx, chosen, limits, sems) = refs[:-5], refs[-5:]
    pairs, rows = vt_all.shape[0], outs[0].shape[0]
    first_group, total, length = (place_ref[i] for i in range(1, 4))
    first_row = turn_ref[0]
    slots = 2 * reach + 2
    half_mask = lax.broadcasted_iota(jnp.int32, (GROUP, LANES), 1) < HD
    row_ids = lax.broadcasted_iota(jnp.int32, (GROUP, 2 * GROUP), 0)
    part_group = lax.div(length, jnp.int32(GROUP))
    part_left = lax.rem(length, jnp.int32(GROUP))

    def one_group(place, carry):
        group = first_row // GROUP + place
        for slot in range(slots):
            chosen[slot] = groups + group
        offset = part_group - first_group - group
        column = jnp.clip(jnp.where(offset < 0, offset + reach, offset + reach - 1), 0, 2 * reach - 1)
        cut = (part_left > 0) & (offset != 0) & (jnp.abs(offset) <= reach) & (part_group < total)
        cut = cut & (band_ref[group, column] == 1)
        chosen[1] = jnp.where(cut, groups + group + offset, groups + group)
        limits[0] = jnp.where(cut, part_left, 0)
        count = 1 + cut.astype(jnp.int32)
        for column in range(2 * reach):
            offset = column - reach if column < reach else column - reach + 1
            there = first_group + group + offset
            good = (there >= 0) & (there < part_group) & (there < total) & (band_ref[group, column] == 1)
            chosen[count] = jnp.where(good, groups + group + offset, groups + group)
            limits[0] = jnp.where(good & (count == 1), GROUP, limits[0])
            count = count + good.astype(jnp.int32)
        query_at = pl.ds(pl.multiple_of(group * GROUP, GROUP), GROUP)
        out_at = pl.ds(pl.multiple_of(place * GROUP, GROUP), GROUP)

        def run(size):
            first_limit = limits[0]
            last_limit = jnp.where(count == size, GROUP, 0)
            indices = [chosen[slot] for slot in range(size)]
            best = []
            for pair in range(pairs):
                own = q_all[query_at, pair * LANES:(pair + 1) * LANES]
                zero = jnp.zeros_like(own)
                both = jnp.concatenate(
                    [jnp.where(half_mask, own, zero), jnp.where(half_mask, zero, own)], axis=0
                ).T
                top = None
                for slot in range(0, size, 2):
                    tiles = [
                        kv_all[pl.ds(pl.multiple_of(index * GROUP, GROUP), GROUP), pair * LANES:(pair + 1) * LANES]
                        for index in indices[slot:slot + 2]
                    ]
                    got = jnp.dot(jnp.concatenate(tiles, axis=0), both, preferred_element_type=jnp.float32)
                    for one in (slot, slot + 1):
                        part = got[(one - slot) * GROUP:(one - slot + 1) * GROUP]
                        if one == 1:
                            part = jnp.where(row_ids < first_limit, part, -jnp.inf)
                        elif one == size - 1:
                            part = jnp.where(row_ids < last_limit, part, -jnp.inf)
                        score[pair, one * GROUP:(one + 1) * GROUP, :] = part
                        high = jnp.max(part.reshape(GROUP // 8, 8, 2 * GROUP), axis=0)
                        top = high if top is None else jnp.maximum(top, high)
                best.append(jnp.max(top, axis=0, keepdims=True))
            for pair in range(pairs):
                total_sum = jnp.zeros((8, 2 * GROUP), jnp.float32)
                mixed = jnp.zeros((LANES, 2 * GROUP), jnp.float32)
                for slot in range(0, size, 2):
                    weights = jnp.exp(score[pair, slot * GROUP:(slot + 2) * GROUP, :] - best[pair])
                    total_sum += jnp.sum(weights.reshape(2 * GROUP // 8, 8, 2 * GROUP), axis=0)
                    tiles = [vt_all[pair, index] for index in indices[slot:slot + 2]]
                    mixed += jnp.dot(
                        jnp.concatenate(tiles, axis=1),
                        weights.astype(jnp.bfloat16),
                        preferred_element_type=jnp.float32,
                    )
                mixed = mixed / jnp.sum(total_sum, axis=0, keepdims=True)
                both_heads = jnp.concatenate([mixed[:HD, :GROUP], mixed[HD:, GROUP:]], axis=0)
                ctx[out_at, pair * LANES:(pair + 1) * LANES] = both_heads.T.astype(jnp.bfloat16)

        for size in range(2, slots + 1, 2):
            @pl.when((count == size) | (count == size - 1))
            def _():
                run(size)

        return carry

    lax.fori_loop(0, count_rows // GROUP, one_group, 0)
    stores = copy_all(
        [(ctx.at[pl.ds(pl.multiple_of(turn_ref[1 + i], 64), rows), :], out) for i, out in enumerate(outs)], sems
    )
    for store in stores:
        store.wait()


def attend(place, band, turn, outs, q_all, kv_all, vt_all):
    groups, reach = band.shape[0], band.shape[1] // 2
    pairs, block = vt_all.shape[0], q_all.shape[0]
    rows = block // (2 * outs)
    slots = 2 * reach + 2
    return pl.pallas_call(
        functools.partial(attend_kernel, groups, reach, block // 2),
        out_shape=[pltpu.HBM((rows, pairs * LANES), jnp.bfloat16)] * outs,
        in_specs=[SMEM, SMEM, SMEM] + [VMEM] * 3,
        out_specs=[HBM] * outs,
        scratch_shapes=[
            pltpu.VMEM((pairs, slots * GROUP, 2 * GROUP), jnp.float32),
            pltpu.VMEM((block // 2, pairs * LANES), jnp.bfloat16),
            pltpu.SMEM((slots + 2,), jnp.int32),
            pltpu.SMEM((1,), jnp.int32),
            pltpu.SemaphoreType.DMA((outs,)),
        ],
        compiler_params=pltpu.CompilerParams(vmem_limit_bytes=16 * MIB),
        cost_estimate=pl.CostEstimate(flops=1 << 32, bytes_accessed=1 << 20, transcendentals=0),
        name="attend",
    )(place, band, turn, q_all, kv_all, vt_all)


def place_kernel(share, place_ref, own_ref, far_ref, pieces_ref, out_ref, held, sems):
    core, layer, seq = (place_ref[i] for i in range(3))
    layers, _, depth, columns = out_ref.shape
    part = depth // share // 2
    half = columns // 2
    pairs = [(own_ref, held.at[layer, core])]
    far_rows = far_ref.shape[0] // 2
    for side in range(2):
        pairs.append((
            far_ref.at[
                pl.ds(pl.multiple_of((1 - core) * far_rows + side * depth, 16), depth),
                pl.ds(far_ref.shape[1] - half, half),
            ],
            held.at[layer, 1 - core, :, pl.ds(side * half, half)],
        ))
    for other in range(share):
        there = seq ^ other
        for holder in range(2):
            at = lax.rem(there // 2 * 2 + holder, share) * 2 * part
            for step in range(layers - 1):
                row = (other * (layers - 1) + step) * part
                for side in range(2):
                    to = pl.ds(pl.multiple_of(at + side * part, 16), part)
                    pairs.append((
                        pieces_ref.at[holder, pl.ds(row, part), pl.ds(side * columns, columns)],
                        held.at[place_ref[3 + step], lax.rem(there, 2), to, :],
                    ))
    for load in copy_all(pairs, sems):
        load.wait()
    store = pltpu.make_async_copy(held, out_ref, sems.at[len(pairs)])
    store.start()
    store.wait()


def place_weights(place, share, layers, own, far, pieces):
    shape = (layers, 2) + own.shape
    return pl.pallas_call(
        functools.partial(place_kernel, share),
        out_shape=pltpu.HBM(shape, jnp.bfloat16),
        in_specs=[SMEM] + [HBM] * 3,
        out_specs=HBM,
        scratch_shapes=[
            pltpu.VMEM(shape, jnp.bfloat16), pltpu.SemaphoreType.DMA((4 + 4 * share * (layers - 1),))
        ],
        compiler_params=pltpu.CompilerParams(vmem_limit_bytes=8 * MIB),
        cost_estimate=LIGHT,
        name="place",
    )(place, *in_hbm(own, far, pieces))


def output_kernel(layers, place_ref, weight_ref, *refs):
    contexts, out_ref, held, weight, sems = refs[:layers], *refs[layers:]
    columns = weight.shape[3]
    rows = contexts[0].shape[0]
    loads = []
    for step in range(layers):
        there = place_ref[step]
        loads.append(copy_all(
            [(contexts[step], held.at[pl.ds(step * rows, rows), :]), (weight_ref.at[there], weight.at[step])],
            sems.at[pl.ds(2 * step, 2)],
        ))
    totals = [None, None]
    for step in range(layers):
        for load in loads[step]:
            load.wait()
        for side in range(2):
            got = jnp.dot(
                held[step * rows:(step + 1) * rows, :], weight[step, side], preferred_element_type=jnp.float32
            )
            totals[side] = got if step == 0 else totals[side] + got
    for side in range(2):
        out_ref[0, :, side * columns:(side + 1) * columns] = totals[side].astype(jnp.bfloat16)


def output(place, weight, contexts):
    layers, _, depth, columns = weight.shape
    rows, width = contexts[0].shape
    return pl.pallas_call(
        functools.partial(output_kernel, layers),
        out_shape=jax.ShapeDtypeStruct((1, rows, 2 * columns), jnp.bfloat16),
        in_specs=[SMEM] + [HBM] * (1 + layers),
        out_specs=VMEM,
        scratch_shapes=[
            pltpu.VMEM((layers * rows, width), jnp.bfloat16),
            pltpu.VMEM(weight.shape, jnp.bfloat16),
            pltpu.SemaphoreType.DMA((2 * layers,)),
        ],
        compiler_params=pltpu.CompilerParams(vmem_limit_bytes=16 * MIB),
        cost_estimate=LIGHT,
        name="output",
    )(place, *in_hbm(weight), *contexts)


def hold_kernel(*refs):
    del refs


def hold(values):
    return pl.pallas_call(
        hold_kernel,
        out_shape=[jax.ShapeDtypeStruct(value.shape, value.dtype) for value in values],
        in_specs=[HBM] * len(values),
        out_specs=[HBM] * len(values),
        input_output_aliases={i: i for i in range(len(values))},
        compiler_params=pltpu.CompilerParams(vmem_limit_bytes=MIB),
        cost_estimate=pl.CostEstimate(flops=1 << 34, bytes_accessed=1, transcendentals=0),
        name="hold",
    )(*values)


def together(*values):
    return lax.optimization_barrier(values)


def numbers(*values):
    return jnp.stack([jnp.asarray(value, jnp.int32) for value in values])


def local(frames, norm_gain, w_query, w_key, w_value, w_out, group_band, lengths):
    cores, seqs, layers = lax.axis_size("dp"), lax.axis_size("seq"), lax.axis_size("head")
    core, seq, layer = lax.axis_index("dp"), lax.axis_index("seq"), lax.axis_index("head")
    groups = group_band.shape[1]
    width = w_query.shape[1]
    here = [(c, s) for c in range(cores) for s in range(seqs)]

    def home(c, s):
        return s % 2, s // 2 * 2 + c

    def flat(c, s, z=None):
        return c * seqs + s if z is None else (c * seqs + s) * layers + z

    def moved(value, shift):
        pairs = [(flat(c, s, z), flat(*home(c, s), shift(z))) for c, s in here for z in range(layers)]
        return lax.ppermute(value, ("dp", "seq", "head"), pairs)

    after = ring_successors(layers)
    before = {after[z]: z for z in after}
    swap = [(c, cores - 1 - c) for c in range(cores)]
    over_link = [(flat(1, s), flat(0, s + 2)) for s in range(seqs - 2)]
    over_link += [(flat(0, s + 2), flat(1, s)) for s in range(seqs - 2)]
    share = 4 if seqs % 4 == 0 else 2

    def shared(value):
        return [value] + [
            lax.ppermute(value, "seq", [(s, s ^ other) for s in range(seqs)]) for other in range(1, share)
        ]

    rows = frames[0]
    count = rows.shape[0]
    gain = norm_gain[None, :]

    sent, piece, own = pack(numbers(lax.rem(seq, share)), rows, w_query, w_key, w_value, w_out, share)
    first = moved(sent, lambda z: after[z])
    whole = moved(rows, lambda z: z)
    third = moved(sent, lambda z: before[z])
    piece = moved(piece, lambda z: after[after[z]])
    weights = lax.all_gather(own, "dp", axis=0, tiled=True)
    facts = jnp.concatenate([group_band[0], jnp.broadcast_to(lengths[:, None], (1, group_band.shape[2]))], axis=0)
    facts = lax.ppermute(facts, ("dp", "seq"), [(flat(c, s), flat(*home(c, s))) for c, s in here])
    first, whole, piece, facts = together(first, whole, piece, facts)
    second = lax.ppermute(first, "head", [(z, after[z]) for z in range(layers)])

    query_a, pair_a = project([whole, first, third], count, width, gain, weights, 1)
    link_a = lax.ppermute(pair_a, ("dp", "seq"), over_link)
    chip_a = lax.all_gather(pair_a, "dp", axis=0)
    shares = shared(join([first, third, piece], [count, count, 0]))
    query_c, pair_c = project([second], count, width, gain, weights, 1 << 33)
    pair_c, link_a = together(pair_c, link_a)
    link_c, chip_c = lax.ppermute(pair_c, ("dp", "seq"), over_link), lax.ppermute(pair_c, "dp", swap)

    back = {z: before[z] for z in range(layers)}
    ids = [layer, lookup([back[z] for z in range(layers)], layer)]
    ids.append(lookup([after[z] for z in range(layers)], layer))
    ids.append(lookup([back[back[z]] for z in range(layers)], layer))
    place = numbers(core, (seq // 2 * 2 + core) * groups, groups * seqs, facts[groups, 0], *ids)
    band = facts[:groups]
    q_all, kv_all, vt_all = window(
        place, groups, count, [query_a, query_c], [pair_a, pair_c], [chip_a, chip_c], [link_a, link_c]
    )
    *shares, q_all = together(*shares, q_all)
    pieces = join(shares)
    pieces, q_all = together(pieces, q_all)
    pieces = lax.all_gather(pieces, "dp", axis=0)
    half = layers // 2
    arrived, sources = [], []
    for near in (0, 1):
        side = layer // half if near else 1 - layer // half
        turn = numbers(side * half * count, *[lax.rem(layer + e, half) * count for e in range(half)])
        contexts = list(attend(place, band, turn, half, q_all, kv_all, vt_all))
        if not near:
            contexts[0], q_all = together(contexts[0], q_all)
        for e, context in enumerate(contexts):
            def target(z, e=e):
                return (z // half if near else 1 - z // half) * half + (z + e) % half

            arrived.append(moved(context, target))
            sources.append(side * half + lax.rem(layer + half - e, half))
    arrived = list(hold(arrived[:half])) + arrived[half:]
    froms = [before[z] for z in range(layers)], [after[z] for z in range(layers)], [back[back[z]] for z in range(layers)]
    weight = place_weights(
        numbers(core, layer, seq, *[lookup(table, layer) for table in froms]), share, layers, w_out, weights, pieces
    )
    return output(numbers(*sources), weight, arrived)


def solution(mesh):
    return jax.shard_map(
        local,
        mesh=mesh,
        in_specs=(
            P("dp", ("seq", "head"), None),
            P(),
            P("dp", "head"),
            P("dp", "head"),
            P("dp", "head"),
            P("head", "dp"),
            P("dp", "seq", None),
            P("dp"),
        ),
        out_specs=P("dp", ("seq", "head"), None),
        check_vma=False,
    )
```

```python
import functools

import jax
import jax.numpy as jnp
from jax import lax
from jax.experimental import pallas as pl
from jax.experimental.pallas import tpu as pltpu
from jax.sharding import PartitionSpec as P

HD = 64
GROUP = 128
LANES = 128

epsilon = 1e-05

VMEM = pl.BlockSpec(memory_space=pltpu.VMEM)
SMEM = pl.BlockSpec(memory_space=pltpu.SMEM)
HBM = pl.BlockSpec(memory_space=pltpu.HBM)
MIB = 1024 * 1024
LIGHT = pl.CostEstimate(flops=1, bytes_accessed=1, transcendentals=0)


def ring_successors(count):
    order = [0] + list(range(1, count, 2)) + list(range(count - 2 + count % 2, 0, -2))
    return {order[i]: order[(i + 1) % count] for i in range(count)}


def lookup(table, index):
    value = jnp.int32(table[0])
    for place in range(1, len(table)):
        value = jnp.where(index == place, jnp.int32(table[place]), value)
    return value


def copy_all(pairs, sems):
    copies = [pltpu.make_async_copy(source, target, sems.at[i]) for i, (source, target) in enumerate(pairs)]
    for copy in copies:
        copy.start()
    return copies


def in_hbm(*values):
    return [pltpu.with_memory_space_constraint(value, pltpu.HBM) for value in values]


def bundle_kernel(place_ref, query_ref, key_ref, value_ref, w_out_ref, all_ref, piece_ref, held, held_piece, sems):
    depth, width = query_ref.shape
    part = piece_ref.shape[0]
    first = pl.multiple_of(place_ref[0] * part, 16)
    pairs = [(w_out_ref.at[pl.ds(first, part), :], held_piece)]
    for place, source in enumerate((query_ref, key_ref, value_ref)):
        pairs.append((source, held.at[:, pl.ds(place * width, width)]))
    rows = w_out_ref.shape[0]
    for side in range(2):
        pairs.append((
            w_out_ref.at[:, pl.ds(side * width, width)],
            held.at[pl.ds(side * rows, rows), pl.ds(3 * width, width)],
        ))
    loads = copy_all(pairs, sems)
    loads[0].wait()
    stores = copy_all([(held_piece, piece_ref)], sems.at[pl.ds(len(pairs), 1)])
    for load in loads[1:]:
        load.wait()
    stores += copy_all([(held, all_ref)], sems.at[pl.ds(len(pairs) + 1, 1)])
    for store in stores:
        store.wait()


def bundle(place, w_query, w_key, w_value, w_out, share):
    depth, width = w_query.shape
    shapes = [(depth, 4 * width), (w_out.shape[0] // share, w_out.shape[1])]
    return pl.pallas_call(
        bundle_kernel,
        out_shape=[pltpu.HBM(shape, jnp.bfloat16) for shape in shapes],
        in_specs=[SMEM] + [HBM] * 4,
        out_specs=[HBM] * 2,
        scratch_shapes=[pltpu.VMEM(shape, jnp.bfloat16) for shape in shapes] + [pltpu.SemaphoreType.DMA((8,))],
        compiler_params=pltpu.CompilerParams(vmem_limit_bytes=4 * MIB),
        cost_estimate=LIGHT,
        name="bundle",
    )(place, *in_hbm(w_query, w_key, w_value, w_out))


def join_kernel(*refs):
    sources, (out, held, sems) = refs[:-3], refs[-3:]
    spans, at = [], 0
    for source in sources:
        spans.append(pl.ds(at, source.shape[0]))
        at += source.shape[0]
    loads = copy_all([(source, held.at[span, :]) for source, span in zip(sources, spans)], sems)
    stores = []
    for place, (load, span) in enumerate(zip(loads, spans)):
        load.wait()
        stores += copy_all([(held.at[span, :], out.at[span, :])], sems.at[pl.ds(len(loads) + place, 1)])
    for store in stores:
        store.wait()


def join(values, cost=1):
    rows, columns = sum(value.shape[0] for value in values), values[0].shape[1]
    return pl.pallas_call(
        join_kernel,
        out_shape=pltpu.HBM((rows, columns), jnp.bfloat16),
        in_specs=[HBM] * len(values),
        out_specs=HBM,
        scratch_shapes=[
            pltpu.VMEM((rows, columns), jnp.bfloat16), pltpu.SemaphoreType.DMA((2 * len(values),))
        ],
        compiler_params=pltpu.CompilerParams(vmem_limit_bytes=4 * MIB),
        cost_estimate=pl.CostEstimate(flops=cost, bytes_accessed=1, transcendentals=0),
        name="join",
    )(*values)


def project_kernel(blocks, place_ref, gain_ref, own_ref, far_ref, *refs):
    rows = refs[:blocks]
    query_ref, pair_ref, held, weight, query_held, pair_held, sems = refs[blocks:]
    count, (depth, width) = rows[0].shape[0], (own_ref.shape[0], query_ref.shape[1])
    core = place_ref[0]
    order = (1, 2, 0)
    loads = copy_all([(rows[i], held.at[pl.ds(i * count, count), :]) for i in range(blocks)], sems)
    fetches = []
    for place in order:
        for source, owner in ((own_ref, core), (far_ref, 1 - core)):
            to = weight.at[place, pl.ds(pl.multiple_of(owner * depth, 16), depth), :]
            fetches.append((source.at[:, pl.ds(place * width, width)], to))
    fetches = copy_all(fetches, sems.at[pl.ds(blocks, len(fetches))])
    gain = gain_ref[...]
    normalized = []
    for i in range(blocks):
        loads[i].wait()
        values = held[i * count:(i + 1) * count, :].astype(jnp.float32)
        center = values - jnp.mean(values, axis=-1, keepdims=True)
        spread = jnp.mean(center * center, axis=-1, keepdims=True)
        normalized.append((center * lax.rsqrt(spread + epsilon) * gain).astype(jnp.bfloat16))
    normalized = normalized[0] if blocks == 1 else jnp.concatenate(normalized, axis=0)
    stores = []
    for turn, place in enumerate(order):
        for fetch in fetches[2 * turn:2 * turn + 2]:
            fetch.wait()
        got = jnp.dot(normalized, weight[place], preferred_element_type=jnp.float32).astype(jnp.bfloat16)
        sem = sems.at[pl.ds(blocks + len(fetches) + place, 1)]
        if place == 0:
            query_held[...] = (got.astype(jnp.float32) * (HD ** -0.5)).astype(jnp.bfloat16)
            stores += copy_all([(query_held, query_ref)], sem)
        else:
            part = pl.ds((place - 1) * width, width)
            pair_held[:, (place - 1) * width:place * width] = got
            stores += copy_all([(pair_held.at[:, part], pair_ref.at[:, part])], sem)
    for store in stores:
        store.wait()


def project(place, rows, width, gain, own, far, cost):
    blocks, (count, depth) = len(rows), rows[0].shape
    total = blocks * count
    return pl.pallas_call(
        functools.partial(project_kernel, blocks),
        out_shape=[pltpu.HBM((total, width), jnp.bfloat16), pltpu.HBM((total, 2 * width), jnp.bfloat16)],
        in_specs=[SMEM, VMEM] + [HBM] * (blocks + 2),
        out_specs=[HBM, HBM],
        scratch_shapes=[
            pltpu.VMEM((total, depth), jnp.bfloat16),
            pltpu.VMEM((3, depth, width), jnp.bfloat16),
            pltpu.VMEM((total, width), jnp.bfloat16),
            pltpu.VMEM((total, 2 * width), jnp.bfloat16),
            pltpu.SemaphoreType.DMA((blocks + 9,)),
        ],
        compiler_params=pltpu.CompilerParams(vmem_limit_bytes=24 * MIB),
        cost_estimate=pl.CostEstimate(flops=cost, bytes_accessed=1, transcendentals=0),
        name="project",
    )(place, gain, *in_hbm(own), far, *rows)


def window_kernel(shape, groups, place_ref, *refs):
    kinds = len(shape)
    queries, owns, sides = refs[:kinds], refs[kinds:2 * kinds], refs[2 * kinds:4 * kinds]
    q_all, kv_all, vt_all, sems = refs[4 * kinds:]
    block, width = q_all.shape
    rows = block // sum(shape)
    core = place_ref[0]
    chip_base = jnp.where(core == 0, 2 * block, 0)
    link_base = jnp.where(core == 0, 0, 2 * block)
    pairs, step = [], 0
    for kind in range(kinds):
        for inside in range(shape[kind]):
            at = place_ref[4 + step] * rows
            part = pl.ds(inside * rows, rows)
            pairs.append((queries[kind].at[part, :], q_all.at[pl.ds(pl.multiple_of(at, 64), rows), :]))
            for source, base in (
                (owns[kind], block), (sides[kind], chip_base), (sides[kinds + kind], link_base)
            ):
                to = pl.ds(pl.multiple_of(base + at, 64), rows)
                pairs.append((source.at[part, :], kv_all.at[to, :]))
            step += 1
    for copy in copy_all(pairs, sems):
        copy.wait()
    for index in range(3 * groups):
        for pair in range(width // LANES):
            columns = slice(width + pair * LANES, width + (pair + 1) * LANES)
            vt_all[pair, index] = kv_all[index * GROUP:(index + 1) * GROUP, columns].T


def window(place, groups, rows, queries, owns, chip_side, link_side):
    shape = [query.shape[0] // rows for query in queries]
    width, block = queries[0].shape[1], sum(shape) * rows
    pairs = width // LANES
    return pl.pallas_call(
        functools.partial(window_kernel, shape, groups),
        out_shape=(
            jax.ShapeDtypeStruct((block, width), jnp.bfloat16),
            jax.ShapeDtypeStruct((3 * block, 2 * width), jnp.bfloat16),
            jax.ShapeDtypeStruct((pairs, 3 * groups, LANES, GROUP), jnp.bfloat16),
        ),
        in_specs=[SMEM] + [HBM] * (4 * len(shape)),
        out_specs=(VMEM,) * 3,
        scratch_shapes=[pltpu.SemaphoreType.DMA((4 * sum(shape),))],
        compiler_params=pltpu.CompilerParams(vmem_limit_bytes=16 * MIB),
        cost_estimate=pl.CostEstimate(flops=0, bytes_accessed=2 * 14 * block * width, transcendentals=0),
        name="window",
    )(place, *in_hbm(*queries, *owns), *chip_side, *link_side)


def attend_kernel(groups, reach, count_rows, place_ref, band_ref, turn_ref, q_all, kv_all, vt_all, *refs):
    outs, (score, ctx, chosen, limits, sems) = refs[:-5], refs[-5:]
    pairs, rows = vt_all.shape[0], outs[0].shape[0]
    first_group, total, length = (place_ref[i] for i in range(1, 4))
    first_row = turn_ref[0]
    slots = 2 * reach + 2
    half_mask = lax.broadcasted_iota(jnp.int32, (GROUP, LANES), 1) < HD
    row_ids = lax.broadcasted_iota(jnp.int32, (GROUP, 2 * GROUP), 0)
    part_group = lax.div(length, jnp.int32(GROUP))
    part_left = lax.rem(length, jnp.int32(GROUP))

    def one_group(place, carry):
        group = first_row // GROUP + place
        for slot in range(slots):
            chosen[slot] = groups + group
        offset = part_group - first_group - group
        column = jnp.clip(jnp.where(offset < 0, offset + reach, offset + reach - 1), 0, 2 * reach - 1)
        cut = (part_left > 0) & (offset != 0) & (jnp.abs(offset) <= reach) & (part_group < total)
        cut = cut & (band_ref[group, column] == 1)
        chosen[1] = jnp.where(cut, groups + group + offset, groups + group)
        limits[0] = jnp.where(cut, part_left, 0)
        count = 1 + cut.astype(jnp.int32)
        for column in range(2 * reach):
            offset = column - reach if column < reach else column - reach + 1
            there = first_group + group + offset
            good = (there >= 0) & (there < part_group) & (there < total) & (band_ref[group, column] == 1)
            chosen[count] = jnp.where(good, groups + group + offset, groups + group)
            limits[0] = jnp.where(good & (count == 1), GROUP, limits[0])
            count = count + good.astype(jnp.int32)
        query_at = pl.ds(pl.multiple_of(group * GROUP, GROUP), GROUP)
        out_at = pl.ds(pl.multiple_of(place * GROUP, GROUP), GROUP)

        def run(size):
            first_limit = limits[0]
            last_limit = jnp.where(count == size, GROUP, 0)
            indices = [chosen[slot] for slot in range(size)]
            best = []
            for pair in range(pairs):
                own = q_all[query_at, pair * LANES:(pair + 1) * LANES]
                zero = jnp.zeros_like(own)
                both = jnp.concatenate(
                    [jnp.where(half_mask, own, zero), jnp.where(half_mask, zero, own)], axis=0
                ).T
                top = None
                for slot in range(0, size, 2):
                    tiles = [
                        kv_all[pl.ds(pl.multiple_of(index * GROUP, GROUP), GROUP), pair * LANES:(pair + 1) * LANES]
                        for index in indices[slot:slot + 2]
                    ]
                    got = jnp.dot(jnp.concatenate(tiles, axis=0), both, preferred_element_type=jnp.float32)
                    for one in (slot, slot + 1):
                        part = got[(one - slot) * GROUP:(one - slot + 1) * GROUP]
                        if one == 1:
                            part = jnp.where(row_ids < first_limit, part, -jnp.inf)
                        elif one == size - 1:
                            part = jnp.where(row_ids < last_limit, part, -jnp.inf)
                        score[pair, one * GROUP:(one + 1) * GROUP, :] = part
                        high = jnp.max(part.reshape(GROUP // 8, 8, 2 * GROUP), axis=0)
                        top = high if top is None else jnp.maximum(top, high)
                best.append(jnp.max(top, axis=0, keepdims=True))
            for pair in range(pairs):
                total_sum = jnp.zeros((8, 2 * GROUP), jnp.float32)
                mixed = jnp.zeros((LANES, 2 * GROUP), jnp.float32)
                for slot in range(0, size, 2):
                    weights = jnp.exp(score[pair, slot * GROUP:(slot + 2) * GROUP, :] - best[pair])
                    total_sum += jnp.sum(weights.reshape(2 * GROUP // 8, 8, 2 * GROUP), axis=0)
                    tiles = [vt_all[pair, index] for index in indices[slot:slot + 2]]
                    mixed += jnp.dot(
                        jnp.concatenate(tiles, axis=1),
                        weights.astype(jnp.bfloat16),
                        preferred_element_type=jnp.float32,
                    )
                mixed = mixed / jnp.sum(total_sum, axis=0, keepdims=True)
                both_heads = jnp.concatenate([mixed[:HD, :GROUP], mixed[HD:, GROUP:]], axis=0)
                ctx[out_at, pair * LANES:(pair + 1) * LANES] = both_heads.T.astype(jnp.bfloat16)

        for size in range(2, slots + 1, 2):
            @pl.when((count == size) | (count == size - 1))
            def _():
                run(size)

        return carry

    lax.fori_loop(0, count_rows // GROUP, one_group, 0)
    stores = copy_all(
        [(ctx.at[pl.ds(pl.multiple_of(turn_ref[1 + i], 64), rows), :], out) for i, out in enumerate(outs)], sems
    )
    for store in stores:
        store.wait()


def attend(place, band, turn, outs, q_all, kv_all, vt_all):
    groups, reach = band.shape[0], band.shape[1] // 2
    pairs, block = vt_all.shape[0], q_all.shape[0]
    rows = block // (2 * outs)
    slots = 2 * reach + 2
    return pl.pallas_call(
        functools.partial(attend_kernel, groups, reach, block // 2),
        out_shape=[pltpu.HBM((rows, pairs * LANES), jnp.bfloat16)] * outs,
        in_specs=[SMEM, SMEM, SMEM] + [VMEM] * 3,
        out_specs=[HBM] * outs,
        scratch_shapes=[
            pltpu.VMEM((pairs, slots * GROUP, 2 * GROUP), jnp.float32),
            pltpu.VMEM((block // 2, pairs * LANES), jnp.bfloat16),
            pltpu.SMEM((slots + 2,), jnp.int32),
            pltpu.SMEM((1,), jnp.int32),
            pltpu.SemaphoreType.DMA((outs,)),
        ],
        compiler_params=pltpu.CompilerParams(vmem_limit_bytes=16 * MIB),
        cost_estimate=pl.CostEstimate(flops=1 << 32, bytes_accessed=1 << 20, transcendentals=0),
        name="attend",
    )(place, band, turn, q_all, kv_all, vt_all)


def place_kernel(share, place_ref, own_ref, far_ref, pieces_ref, theirs_ref, out_ref, mark_ref, held, sems):
    mark_ref[...] = jnp.zeros_like(mark_ref)
    core, layer, seq = (place_ref[i] for i in range(3))
    layers, _, depth, columns = out_ref.shape
    part = depth // share
    half = columns // 2
    pairs = [(own_ref, held.at[layer, core])]
    for side in range(2):
        pairs.append((
            far_ref.at[pl.ds(side * depth, depth), pl.ds(far_ref.shape[1] - half, half)],
            held.at[layer, 1 - core, :, pl.ds(side * half, half)],
        ))
    for other in range(share):
        at = pl.ds(pl.multiple_of(lax.rem(seq ^ other, share) * part, 16), part)
        for source, source_core in ((pieces_ref, core), (theirs_ref, 1 - core)):
            for step in range(layers - 1):
                row = (other * (layers - 1) + step) * part
                pairs.append((source.at[pl.ds(row, part), :], held.at[place_ref[3 + step], source_core, at, :]))
    for load in copy_all(pairs, sems):
        load.wait()
    store = pltpu.make_async_copy(held, out_ref, sems.at[len(pairs)])
    store.start()
    store.wait()


def place_weights(place, share, layers, own, far, mine, theirs):
    shape = (layers, 2) + own.shape
    return pl.pallas_call(
        functools.partial(place_kernel, share),
        out_shape=[pltpu.HBM(shape, jnp.bfloat16), jax.ShapeDtypeStruct((8, LANES), jnp.float32)],
        in_specs=[SMEM] + [HBM] * 4,
        out_specs=[HBM, VMEM],
        scratch_shapes=[
            pltpu.VMEM(shape, jnp.bfloat16), pltpu.SemaphoreType.DMA((4 + 2 * share * (layers - 1),))
        ],
        compiler_params=pltpu.CompilerParams(vmem_limit_bytes=8 * MIB),
        cost_estimate=LIGHT,
        name="place",
    )(place, *in_hbm(own), far, *in_hbm(mine), theirs)


def output_kernel(layers, place_ref, weight_ref, *refs):
    contexts, out_ref, held, weight, sems = refs[:layers], *refs[layers:]
    columns = weight.shape[3]
    rows = contexts[0].shape[0]
    loads = []
    for step in range(layers):
        there = place_ref[step]
        loads.append(copy_all(
            [(contexts[step], held.at[pl.ds(step * rows, rows), :]), (weight_ref.at[there], weight.at[step])],
            sems.at[pl.ds(2 * step, 2)],
        ))
    totals = [None, None]
    for step in range(layers):
        for load in loads[step]:
            load.wait()
        for side in range(2):
            got = jnp.dot(
                held[step * rows:(step + 1) * rows, :], weight[step, side], preferred_element_type=jnp.float32
            )
            totals[side] = got if step == 0 else totals[side] + got
    for side in range(2):
        out_ref[0, :, side * columns:(side + 1) * columns] = totals[side].astype(jnp.bfloat16)


def output(place, weight, contexts):
    layers, _, depth, columns = weight.shape
    rows, width = contexts[0].shape
    return pl.pallas_call(
        functools.partial(output_kernel, layers),
        out_shape=jax.ShapeDtypeStruct((1, rows, 2 * columns), jnp.bfloat16),
        in_specs=[SMEM] + [HBM] * (1 + layers),
        out_specs=VMEM,
        scratch_shapes=[
            pltpu.VMEM((layers * rows, width), jnp.bfloat16),
            pltpu.VMEM(weight.shape, jnp.bfloat16),
            pltpu.SemaphoreType.DMA((2 * layers,)),
        ],
        compiler_params=pltpu.CompilerParams(vmem_limit_bytes=16 * MIB),
        cost_estimate=LIGHT,
        name="output",
    )(place, *in_hbm(weight), *contexts)


def hold_kernel(*refs):
    del refs


def hold(values):
    return pl.pallas_call(
        hold_kernel,
        out_shape=[jax.ShapeDtypeStruct(value.shape, value.dtype) for value in values],
        in_specs=[HBM] * len(values),
        out_specs=[HBM] * len(values),
        input_output_aliases={i: i for i in range(len(values))},
        compiler_params=pltpu.CompilerParams(vmem_limit_bytes=MIB),
        cost_estimate=pl.CostEstimate(flops=1 << 34, bytes_accessed=1, transcendentals=0),
        name="hold",
    )(*values)


def together(*values):
    return lax.optimization_barrier(values)


def numbers(*values):
    return jnp.stack([jnp.asarray(value, jnp.int32) for value in values])


def local(frames, norm_gain, w_query, w_key, w_value, w_out, group_band, lengths):
    cores, seqs, layers = lax.axis_size("dp"), lax.axis_size("seq"), lax.axis_size("head")
    core, seq, layer = lax.axis_index("dp"), lax.axis_index("seq"), lax.axis_index("head")
    groups = group_band.shape[1]
    width = w_query.shape[1]
    here = [(c, s) for c in range(cores) for s in range(seqs)]

    def home(c, s):
        return s % 2, s // 2 * 2 + c

    def flat(c, s, z=None):
        return c * seqs + s if z is None else (c * seqs + s) * layers + z

    def moved(value, shift):
        pairs = [(flat(c, s, z), flat(*home(c, s), shift(z))) for c, s in here for z in range(layers)]
        return lax.ppermute(value, ("dp", "seq", "head"), pairs)

    after = ring_successors(layers)
    before = {after[z]: z for z in after}
    swap = [(c, cores - 1 - c) for c in range(cores)]
    over_link = [(flat(1, s), flat(0, s + 2)) for s in range(seqs - 2)]
    over_link += [(flat(0, s + 2), flat(1, s)) for s in range(seqs - 2)]
    share = 4

    def shared(value):
        near = [lax.ppermute(value, "seq", [(s, s ^ step) for s in range(seqs)]) for step in (1, 2)]
        middle = value.shape[0] // 2
        halves = (near[1][:middle], near[0][middle:])
        opposite = [
            lax.ppermute(half, "seq", [(s, s ^ step) for s in range(seqs)]) for half, step in zip(halves, (1, 2))
        ]
        return [value] + near + opposite

    rows = frames[0]
    count = rows.shape[0]
    gain = norm_gain[None, :]

    def ringed(value):
        return lax.ppermute(value, "head", [(z, after[z]) for z in range(layers)])

    first = moved(rows, lambda z: after[z])
    second = ringed(first)
    third = ringed(second)
    own, piece = bundle(numbers(lax.rem(seq, share)), w_query, w_key, w_value, w_out, share)
    far = lax.ppermute(own, "dp", swap)
    whole = moved(rows, lambda z: z)
    facts = jnp.concatenate([group_band[0], jnp.broadcast_to(lengths[:, None], (1, group_band.shape[2]))], axis=0)
    facts = lax.ppermute(facts, ("dp", "seq"), [(flat(c, s), flat(*home(c, s))) for c, s in here])
    pieces, held = [], piece
    step = 1
    while step < layers:
        pieces.append(lax.ppermute(held, "head", [(z, z ^ step) for z in range(layers)]))
        held = join([held, pieces[-1]], 1 << 33) if 2 * step < layers else held
        step *= 2
    shares = shared(join(pieces, 1 << 32))
    whole, facts = together(whole, facts)

    core_at = numbers(core)
    query_a, pair_a = project(core_at, [whole, first, second], width, gain, own, far, 1)
    link_a, chip_a = lax.ppermute(pair_a, ("dp", "seq"), over_link), lax.ppermute(pair_a, "dp", swap)
    query_c, pair_c = project(core_at, [third], width, gain, own, far, 1 << 33)
    link_c, chip_c = lax.ppermute(pair_c, ("dp", "seq"), over_link), lax.ppermute(pair_c, "dp", swap)
    _, *shares = together(query_a, *shares)
    mine = join(shares)
    theirs = lax.ppermute(mine, "dp", swap)

    back = {z: before[z] for z in range(layers)}
    ids = [layer, lookup([back[z] for z in range(layers)], layer)]
    ids.append(lookup([back[back[z]] for z in range(layers)], layer))
    ids.append(lookup([after[z] for z in range(layers)], layer))
    place = numbers(core, (seq // 2 * 2 + core) * groups, groups * seqs, facts[groups, 0], *ids)
    band = facts[:groups]
    q_all, kv_all, vt_all = window(
        place, groups, count, [query_a, query_c], [pair_a, pair_c], [chip_a, chip_c], [link_a, link_c]
    )
    half = layers // 2
    arrived, sources = [], []
    for near in (0, 1):
        side = layer // half if near else 1 - layer // half
        turn = numbers(side * half * count, *[lax.rem(layer + e, half) * count for e in range(half)])
        contexts = list(attend(place, band, turn, half, q_all, kv_all, vt_all))
        if not near:
            contexts[0], q_all = together(contexts[0], q_all)
        if near:
            contexts[0], theirs = together(contexts[0], theirs)
        for e, context in enumerate(contexts):
            def target(z, e=e):
                return (z // half if near else 1 - z // half) * half + (z + e) % half

            arrived.append(moved(context, target))
            sources.append(side * half + lax.rem(layer + half - e, half))
    weight, mark = place_weights(
        numbers(core, layer, seq, *[layer ^ step for step in range(1, layers)]),
        share, layers, w_out, far, mine, theirs,
    )
    *held, _ = hold(arrived[:half] + [mark])
    return output(numbers(*sources), weight, held + arrived[half:])


def solution(mesh):
    return jax.shard_map(
        local,
        mesh=mesh,
        in_specs=(
            P("dp", ("seq", "head"), None),
            P(),
            P("dp", "head"),
            P("dp", "head"),
            P("dp", "head"),
            P("head", "dp"),
            P("dp", "seq", None),
            P("dp"),
        ),
        out_specs=P("dp", ("seq", "head"), None),
        check_vma=False,
    )
```

```python
import functools

import jax
import jax.numpy as jnp
from jax import lax
from jax.experimental import pallas as pl
from jax.experimental.pallas import tpu as pltpu
from jax.sharding import PartitionSpec as P

HD = 64
GROUP = 128
LANES = 128

epsilon = 1e-05

VMEM = pl.BlockSpec(memory_space=pltpu.VMEM)
SMEM = pl.BlockSpec(memory_space=pltpu.SMEM)
HBM = pl.BlockSpec(memory_space=pltpu.HBM)
MIB = 1024 * 1024
LIGHT = pl.CostEstimate(flops=1, bytes_accessed=1, transcendentals=0)


def ring_successors(count):
    order = [0] + list(range(1, count, 2)) + list(range(count - 2 + count % 2, 0, -2))
    return {order[i]: order[(i + 1) % count] for i in range(count)}


def lookup(table, index):
    value = jnp.int32(table[0])
    for place in range(1, len(table)):
        value = jnp.where(index == place, jnp.int32(table[place]), value)
    return value


def copy_all(pairs, sems):
    copies = [pltpu.make_async_copy(source, target, sems.at[i]) for i, (source, target) in enumerate(pairs)]
    for copy in copies:
        copy.start()
    return copies


def in_hbm(*values):
    return [pltpu.with_memory_space_constraint(value, pltpu.HBM) for value in values]


def run_copies(loads, stores, sems):
    for copy in copy_all(loads, sems):
        copy.wait()
    for copy in copy_all(stores, sems):
        copy.wait()


def pack_kernel(place_ref, rows_ref, w_out_ref, sent_ref, piece_ref, held, held_piece, sems):
    count = rows_ref.shape[0]
    part, columns = piece_ref.shape
    first = pl.multiple_of(place_ref[0] * part, 16)
    loads = [(w_out_ref.at[pl.ds(first, part), :], held_piece), (rows_ref, held.at[pl.ds(0, count), :])]
    for side in range(2):
        loads.append((
            w_out_ref.at[pl.ds(first + side * (part // 2), part // 2), :],
            held.at[pl.ds(count, part // 2), pl.ds(side * columns, columns)],
        ))
    run_copies(loads, [(held, sent_ref), (held_piece, piece_ref)], sems)


def pack(place, rows, w_out, share):
    part = w_out.shape[0] // share
    shapes = [(rows.shape[0] + part // 2, rows.shape[1]), (part, w_out.shape[1])]
    return pl.pallas_call(
        pack_kernel,
        out_shape=[pltpu.HBM(shape, jnp.bfloat16) for shape in shapes],
        in_specs=[SMEM] + [HBM] * 2,
        out_specs=[HBM] * 2,
        scratch_shapes=[pltpu.VMEM(shape, jnp.bfloat16) for shape in shapes] + [pltpu.SemaphoreType.DMA((4,))],
        compiler_params=pltpu.CompilerParams(vmem_limit_bytes=4 * MIB),
        cost_estimate=LIGHT,
        name="pack",
    )(place, *in_hbm(rows, w_out))


def bundle_kernel(query_ref, key_ref, value_ref, w_out_ref, front_ref, back_ref, held, held_back, sems):
    width, rows = query_ref.shape[1], w_out_ref.shape[0]
    loads = [
        (query_ref, held.at[:, pl.ds(0, width)]),
        (key_ref, held.at[:, pl.ds(width, width)]),
        (value_ref, held_back.at[:, pl.ds(0, width)]),
    ]
    for side in range(2):
        loads.append((
            w_out_ref.at[:, pl.ds(side * width, width)],
            held_back.at[pl.ds(side * rows, rows), pl.ds(width, width)],
        ))
    run_copies(loads, [(held, front_ref), (held_back, back_ref)], sems)


def bundle(w_query, w_key, w_value, w_out):
    shape = (w_query.shape[0], 2 * w_query.shape[1])
    return pl.pallas_call(
        bundle_kernel,
        out_shape=[pltpu.HBM(shape, jnp.bfloat16)] * 2,
        in_specs=[HBM] * 4,
        out_specs=[HBM] * 2,
        scratch_shapes=[pltpu.VMEM(shape, jnp.bfloat16)] * 2 + [pltpu.SemaphoreType.DMA((5,))],
        compiler_params=pltpu.CompilerParams(vmem_limit_bytes=4 * MIB),
        cost_estimate=LIGHT,
        name="bundle",
    )(*in_hbm(w_query, w_key, w_value, w_out))


def join_kernel(count, first_ref, second_ref, piece_ref, out_ref, held, sems):
    part, columns = piece_ref.shape[0] // 2, piece_ref.shape[1]
    loads = [
        (source.at[pl.ds(count, part), :], held.at[pl.ds(place * part, part), :])
        for place, source in enumerate((first_ref, second_ref))
    ]
    for side in range(2):
        loads.append((
            piece_ref.at[pl.ds(side * part, part), :],
            held.at[pl.ds(2 * part, part), pl.ds(side * columns, columns)],
        ))
    run_copies(loads, [(held, out_ref)], sems)


def join(count, first, second, piece):
    shape = (3 * piece.shape[0] // 2, first.shape[1])
    return pl.pallas_call(
        functools.partial(join_kernel, count),
        out_shape=pltpu.HBM(shape, jnp.bfloat16),
        in_specs=[HBM] * 3,
        out_specs=HBM,
        scratch_shapes=[pltpu.VMEM(shape, jnp.bfloat16), pltpu.SemaphoreType.DMA((4,))],
        compiler_params=pltpu.CompilerParams(vmem_limit_bytes=4 * MIB),
        cost_estimate=LIGHT,
        name="join",
    )(first, second, piece)


def project_kernel(blocks, joined, count, place_ref, gain_ref, own_front, own_back, far_front, far_back, *refs):
    rows, sources = refs[:blocks], refs[blocks:blocks + joined]
    refs = refs[blocks + joined:]
    if joined:
        query_ref, pair_ref, join_ref, held, weight, query_held, pair_held, join_held, sems = refs
    else:
        query_ref, pair_ref, held, weight, query_held, pair_held, sems = refs[-7:]
    depth, width = own_front.shape[0], query_ref.shape[1]
    to_rows = pl.ds(query_ref.shape[0] - blocks * count if len(refs) > 8 and not joined else 0, blocks * count)
    core = place_ref[0]
    order = (1, 2, 0)
    loads = copy_all(
        [(rows[i].at[pl.ds(0, count), :], held.at[pl.ds(i * count, count), :]) for i in range(blocks)], sems
    )
    fetches = []
    for place in order:
        for pair, owner in (((own_front, own_back), core), ((far_front, far_back), 1 - core)):
            to = weight.at[place, pl.ds(pl.multiple_of(owner * depth, 16), depth), :]
            fetches.append((pair[place // 2].at[:, pl.ds(place % 2 * width, width)], to))
    fetches = copy_all(fetches, sems.at[pl.ds(blocks, len(fetches))])
    parts, at = [], 0
    for source in sources:
        parts.append((source, join_held.at[pl.ds(at, source.shape[0]), :]))
        at += source.shape[0]
    used = blocks + len(fetches) + 3
    parts = copy_all(parts, sems.at[pl.ds(used, max(1, joined))])
    gain = gain_ref[...]
    normalized = []
    for i in range(blocks):
        loads[i].wait()
        values = held[i * count:(i + 1) * count, :].astype(jnp.float32)
        center = values - jnp.mean(values, axis=-1, keepdims=True)
        spread = jnp.mean(center * center, axis=-1, keepdims=True)
        normalized.append((center * lax.rsqrt(spread + epsilon) * gain).astype(jnp.bfloat16))
    normalized = normalized[0] if blocks == 1 else jnp.concatenate(normalized, axis=0)
    stores = []
    for turn, place in enumerate(order):
        for fetch in fetches[2 * turn:2 * turn + 2]:
            fetch.wait()
        got = jnp.dot(normalized, weight[place], preferred_element_type=jnp.float32).astype(jnp.bfloat16)
        sem = sems.at[pl.ds(blocks + len(fetches) + place, 1)]
        if place == 0:
            query_held[...] = (got.astype(jnp.float32) * (HD ** -0.5)).astype(jnp.bfloat16)
            stores += copy_all([(query_held, query_ref.at[to_rows, :])], sem)
        else:
            part = pl.ds((place - 1) * width, width)
            pair_held[:, (place - 1) * width:place * width] = got
            stores += copy_all([(pair_held.at[:, part], pair_ref.at[to_rows, part])], sem)
        if turn == 0 and joined:
            for part in parts:
                part.wait()
            stores += copy_all([(join_held, join_ref)], sems.at[pl.ds(used + joined, 1)])
    for store in stores:
        store.wait()


def project(place, rows, count, width, gain, own, far, cost, room=0, into=(), joined=()):
    blocks, depth = len(rows), rows[0].shape[1]
    total = blocks * count
    full = into[0].shape[0] if into else total + room
    out_shape = [pltpu.HBM((full, width), jnp.bfloat16), pltpu.HBM((full, 2 * width), jnp.bfloat16)]
    scratch = [
        pltpu.VMEM((total, depth), jnp.bfloat16),
        pltpu.VMEM((3, depth, width), jnp.bfloat16),
        pltpu.VMEM((total, width), jnp.bfloat16),
        pltpu.VMEM((total, 2 * width), jnp.bfloat16),
    ]
    if joined:
        shape = (sum(value.shape[0] for value in joined), joined[0].shape[1])
        out_shape.append(pltpu.HBM(shape, jnp.bfloat16))
        scratch.append(pltpu.VMEM(shape, jnp.bfloat16))
    inputs = 6 + blocks + len(joined)
    return pl.pallas_call(
        functools.partial(project_kernel, blocks, len(joined), count),
        out_shape=out_shape,
        in_specs=[SMEM, VMEM] + [HBM] * (inputs - 2 + len(into)),
        out_specs=[HBM] * len(out_shape),
        scratch_shapes=scratch + [pltpu.SemaphoreType.DMA((blocks + 10 + max(1, len(joined)),))],
        input_output_aliases={inputs + i: i for i in range(len(into))},
        compiler_params=pltpu.CompilerParams(vmem_limit_bytes=24 * MIB),
        cost_estimate=pl.CostEstimate(flops=cost, bytes_accessed=1, transcendentals=0),
        name="project",
    )(place, gain, *in_hbm(*own), *far, *rows, *joined, *in_hbm(*into))


def window_kernel(shape, groups, place_ref, *refs):
    kinds = len(shape)
    queries, owns, sides = refs[:kinds], refs[kinds:2 * kinds], refs[2 * kinds:4 * kinds]
    q_all, kv_all, vt_all, sems = refs[4 * kinds:]
    block, width = q_all.shape
    rows = block // sum(shape)
    core = place_ref[0]
    chip_base = jnp.where(core == 0, 2 * block, 0)
    link_base = jnp.where(core == 0, 0, 2 * block)
    pairs, step = [], 0
    for kind in range(kinds):
        for inside in range(shape[kind]):
            at = place_ref[4 + step] * rows
            part = pl.ds(inside * rows, rows)
            pairs.append((queries[kind].at[part, :], q_all.at[pl.ds(pl.multiple_of(at, 64), rows), :]))
            for source, base in (
                (owns[kind], block), (sides[kind], chip_base), (sides[kinds + kind], link_base)
            ):
                to = pl.ds(pl.multiple_of(base + at, 64), rows)
                pairs.append((source.at[part, :], kv_all.at[to, :]))
            step += 1
    for copy in copy_all(pairs, sems):
        copy.wait()
    for index in range(3 * groups):
        for pair in range(width // LANES):
            columns = slice(width + pair * LANES, width + (pair + 1) * LANES)
            vt_all[pair, index] = kv_all[index * GROUP:(index + 1) * GROUP, columns].T


def window(place, groups, rows, queries, owns, chip_side, link_side):
    shape = [query.shape[0] // rows for query in queries]
    width, block = queries[0].shape[1], sum(shape) * rows
    pairs = width // LANES
    return pl.pallas_call(
        functools.partial(window_kernel, shape, groups),
        out_shape=(
            jax.ShapeDtypeStruct((block, width), jnp.bfloat16),
            jax.ShapeDtypeStruct((3 * block, 2 * width), jnp.bfloat16),
            jax.ShapeDtypeStruct((pairs, 3 * groups, LANES, GROUP), jnp.bfloat16),
        ),
        in_specs=[SMEM] + [HBM] * (4 * len(shape)),
        out_specs=(VMEM,) * 3,
        scratch_shapes=[pltpu.SemaphoreType.DMA((4 * sum(shape),))],
        compiler_params=pltpu.CompilerParams(vmem_limit_bytes=16 * MIB),
        cost_estimate=pl.CostEstimate(flops=0, bytes_accessed=2 * 14 * block * width, transcendentals=0),
        name="window",
    )(place, *in_hbm(*queries, *owns), *chip_side, *link_side)


def weight_copies(share, place_ref, own_ref, far_ref, pieces_ref, theirs_ref, weight_ref):
    core, layer, seq = (place_ref[i] for i in range(3))
    layers, _, depth, columns = weight_ref.shape
    part = depth // share // 2
    half = columns // 2
    pairs = [(own_ref, weight_ref.at[layer, core])]
    for side in range(2):
        pairs.append((
            far_ref.at[pl.ds(side * depth, depth), pl.ds(far_ref.shape[1] - half, half)],
            weight_ref.at[layer, 1 - core, :, pl.ds(side * half, half)],
        ))
    for other in range(share):
        there = seq ^ other
        for source, holder in ((pieces_ref, core), (theirs_ref, 1 - core)):
            at = lax.rem(there // 2 * 2 + holder, share) * 2 * part
            for step in range(layers - 1):
                row = (other * (layers - 1) + step) * part
                for side in range(2):
                    to = pl.ds(pl.multiple_of(at + side * part, 16), part)
                    pairs.append((
                        source.at[pl.ds(row, part), pl.ds(side * columns, columns)],
                        weight_ref.at[place_ref[3 + step], lax.rem(there, 2), to, :],
                    ))
    return pairs


def attend_kernel(groups, reach, count_rows, share, place_ref, band_ref, turn_ref, q_all, kv_all, vt_all, *refs):
    loads = []
    if share:
        sources, refs = refs[:5], refs[5:]
        weight, load_sems, refs = refs[-7], refs[-1], refs[:-7] + refs[-6:-1]
        loads = copy_all(weight_copies(share, *sources, weight), load_sems)
    outs, (score, ctx, chosen, limits, sems) = refs[:-5], refs[-5:]
    pairs, rows = vt_all.shape[0], outs[0].shape[0]
    first_group, total, length = (place_ref[i] for i in range(1, 4))
    first_row = turn_ref[0]
    slots = 2 * reach + 2
    half_mask = lax.broadcasted_iota(jnp.int32, (GROUP, LANES), 1) < HD
    row_ids = lax.broadcasted_iota(jnp.int32, (GROUP, 2 * GROUP), 0)
    part_group = lax.div(length, jnp.int32(GROUP))
    part_left = lax.rem(length, jnp.int32(GROUP))

    def one_group(place, carry):
        group = first_row // GROUP + place
        for slot in range(slots):
            chosen[slot] = groups + group
        offset = part_group - first_group - group
        column = jnp.clip(jnp.where(offset < 0, offset + reach, offset + reach - 1), 0, 2 * reach - 1)
        cut = (part_left > 0) & (offset != 0) & (jnp.abs(offset) <= reach) & (part_group < total)
        cut = cut & (band_ref[group, column] == 1)
        chosen[1] = jnp.where(cut, groups + group + offset, groups + group)
        limits[0] = jnp.where(cut, part_left, 0)
        count = 1 + cut.astype(jnp.int32)
        for column in range(2 * reach):
            offset = column - reach if column < reach else column - reach + 1
            there = first_group + group + offset
            good = (there >= 0) & (there < part_group) & (there < total) & (band_ref[group, column] == 1)
            chosen[count] = jnp.where(good, groups + group + offset, groups + group)
            limits[0] = jnp.where(good & (count == 1), GROUP, limits[0])
            count = count + good.astype(jnp.int32)
        query_at = pl.ds(pl.multiple_of(group * GROUP, GROUP), GROUP)
        out_at = pl.ds(pl.multiple_of(place * GROUP, GROUP), GROUP)

        def run(size):
            first_limit = limits[0]
            last_limit = jnp.where(count == size, GROUP, 0)
            indices = [chosen[slot] for slot in range(size)]
            best = []
            for pair in range(pairs):
                own = q_all[query_at, pair * LANES:(pair + 1) * LANES]
                zero = jnp.zeros_like(own)
                both = jnp.concatenate(
                    [jnp.where(half_mask, own, zero), jnp.where(half_mask, zero, own)], axis=0
                ).T
                top = None
                for slot in range(0, size, 2):
                    tiles = [
                        kv_all[pl.ds(pl.multiple_of(index * GROUP, GROUP), GROUP), pair * LANES:(pair + 1) * LANES]
                        for index in indices[slot:slot + 2]
                    ]
                    got = jnp.dot(jnp.concatenate(tiles, axis=0), both, preferred_element_type=jnp.float32)
                    for one in (slot, slot + 1):
                        part = got[(one - slot) * GROUP:(one - slot + 1) * GROUP]
                        if one == 1:
                            part = jnp.where(row_ids < first_limit, part, -jnp.inf)
                        elif one == size - 1:
                            part = jnp.where(row_ids < last_limit, part, -jnp.inf)
                        score[pair, one * GROUP:(one + 1) * GROUP, :] = part
                        high = jnp.max(part.reshape(GROUP // 8, 8, 2 * GROUP), axis=0)
                        top = high if top is None else jnp.maximum(top, high)
                best.append(jnp.max(top, axis=0, keepdims=True))
            for pair in range(pairs):
                total_sum = jnp.zeros((8, 2 * GROUP), jnp.float32)
                mixed = jnp.zeros((LANES, 2 * GROUP), jnp.float32)
                for slot in range(0, size, 2):
                    weights = jnp.exp(score[pair, slot * GROUP:(slot + 2) * GROUP, :] - best[pair])
                    total_sum += jnp.sum(weights.reshape(2 * GROUP // 8, 8, 2 * GROUP), axis=0)
                    tiles = [vt_all[pair, index] for index in indices[slot:slot + 2]]
                    mixed += jnp.dot(
                        jnp.concatenate(tiles, axis=1),
                        weights.astype(jnp.bfloat16),
                        preferred_element_type=jnp.float32,
                    )
                mixed = mixed / jnp.sum(total_sum, axis=0, keepdims=True)
                both_heads = jnp.concatenate([mixed[:HD, :GROUP], mixed[HD:, GROUP:]], axis=0)
                ctx[out_at, pair * LANES:(pair + 1) * LANES] = both_heads.T.astype(jnp.bfloat16)

        for size in range(2, slots + 1, 2):
            @pl.when((count == size) | (count == size - 1))
            def _():
                run(size)

        return carry

    lax.fori_loop(0, count_rows // GROUP, one_group, 0)
    stores = copy_all(
        [(ctx.at[pl.ds(pl.multiple_of(turn_ref[1 + i], 64), rows), :], out) for i, out in enumerate(outs)], sems
    )
    for copy in stores + loads:
        copy.wait()


def attend(place, band, turn, outs, q_all, kv_all, vt_all, share=0, layers=0, parts=()):
    groups, reach = band.shape[0], band.shape[1] // 2
    pairs, block = vt_all.shape[0], q_all.shape[0]
    rows = block // (2 * outs)
    slots = 2 * reach + 2
    out_shape = [pltpu.HBM((rows, pairs * LANES), jnp.bfloat16)] * outs
    scratch = [
        pltpu.VMEM((pairs, slots * GROUP, 2 * GROUP), jnp.float32),
        pltpu.VMEM((block // 2, pairs * LANES), jnp.bfloat16),
        pltpu.SMEM((slots + 2,), jnp.int32),
        pltpu.SMEM((1,), jnp.int32),
        pltpu.SemaphoreType.DMA((outs,)),
    ]
    if parts:
        depth, columns = parts[1].shape
        out_shape.append(jax.ShapeDtypeStruct((layers, 2, depth, columns), jnp.bfloat16))
        scratch.append(pltpu.SemaphoreType.DMA((3 + 4 * share * (layers - 1),)))
        parts = [parts[0], *in_hbm(parts[1]), parts[2], *in_hbm(parts[3]), parts[4]]
    return pl.pallas_call(
        functools.partial(attend_kernel, groups, reach, block // 2, share),
        out_shape=out_shape,
        in_specs=[SMEM, SMEM, SMEM] + [VMEM] * 3 + ([SMEM] + [HBM] * 4 if parts else []),
        out_specs=[HBM] * outs + ([VMEM] if parts else []),
        scratch_shapes=scratch,
        compiler_params=pltpu.CompilerParams(vmem_limit_bytes=16 * MIB),
        cost_estimate=pl.CostEstimate(flops=1 << 34, bytes_accessed=1 << 20, transcendentals=0),
        name="attend",
    )(place, band, turn, q_all, kv_all, vt_all, *parts)


def output_kernel(layers, place_ref, weight, *refs):
    contexts, out_ref, held, sems = refs[:layers], *refs[layers:]
    columns = weight.shape[3]
    rows = contexts[0].shape[0]
    loads = copy_all([(contexts[step], held.at[pl.ds(step * rows, rows), :]) for step in range(layers)], sems)
    for load in loads:
        load.wait()
    for side in range(2):
        total = None
        for step in range(layers):
            got = jnp.dot(
                held[step * rows:(step + 1) * rows, :], weight[place_ref[step], side],
                preferred_element_type=jnp.float32,
            )
            total = got if step == 0 else total + got
        out_ref[0, :, side * columns:(side + 1) * columns] = total.astype(jnp.bfloat16)


def output(place, weight, contexts):
    layers, _, depth, columns = weight.shape
    rows, width = contexts[0].shape
    return pl.pallas_call(
        functools.partial(output_kernel, layers),
        out_shape=jax.ShapeDtypeStruct((1, rows, 2 * columns), jnp.bfloat16),
        in_specs=[SMEM, VMEM] + [HBM] * layers,
        out_specs=VMEM,
        scratch_shapes=[pltpu.VMEM((layers * rows, width), jnp.bfloat16), pltpu.SemaphoreType.DMA((layers,))],
        compiler_params=pltpu.CompilerParams(vmem_limit_bytes=8 * MIB),
        cost_estimate=LIGHT,
        name="output",
    )(place, weight, *contexts)


def hold_kernel(*refs):
    del refs


def hold(values, cost=1 << 34):
    return pl.pallas_call(
        hold_kernel,
        out_shape=[jax.ShapeDtypeStruct(value.shape, value.dtype) for value in values],
        in_specs=[HBM] * len(values),
        out_specs=[HBM] * len(values),
        input_output_aliases={i: i for i in range(len(values))},
        compiler_params=pltpu.CompilerParams(vmem_limit_bytes=MIB),
        cost_estimate=pl.CostEstimate(flops=cost, bytes_accessed=1, transcendentals=0),
        name="hold",
    )(*values)


def together(*values):
    return lax.optimization_barrier(values)


def numbers(*values):
    return jnp.stack([jnp.asarray(value, jnp.int32) for value in values])


def local(frames, norm_gain, w_query, w_key, w_value, w_out, group_band, lengths):
    cores, seqs, layers = lax.axis_size("dp"), lax.axis_size("seq"), lax.axis_size("head")
    core, seq, layer = lax.axis_index("dp"), lax.axis_index("seq"), lax.axis_index("head")
    groups = group_band.shape[1]
    width = w_query.shape[1]
    here = [(c, s) for c in range(cores) for s in range(seqs)]

    def home(c, s):
        return s % 2, s // 2 * 2 + c

    def flat(c, s, z=None):
        return c * seqs + s if z is None else (c * seqs + s) * layers + z

    def moved(value, shift):
        pairs = [(flat(c, s, z), flat(*home(c, s), shift(z))) for c, s in here for z in range(layers)]
        return lax.ppermute(value, ("dp", "seq", "head"), pairs)

    after = ring_successors(layers)
    before = {after[z]: z for z in after}
    swap = [(c, cores - 1 - c) for c in range(cores)]
    over_link = [(flat(1, s), flat(0, s + 2)) for s in range(seqs - 2)]
    over_link += [(flat(0, s + 2), flat(1, s)) for s in range(seqs - 2)]
    share = 4

    def shared(value):
        near = [lax.ppermute(value, "seq", [(s, s ^ step) for s in range(seqs)]) for step in (1, 2)]
        middle = (value.shape[0] // 2 + 15) // 16 * 16
        halves = (near[1][:middle], near[0][middle:])
        opposite = [
            lax.ppermute(half, "seq", [(s, s ^ step) for s in range(seqs)]) for half, step in zip(halves, (1, 2))
        ]
        return [value] + near + opposite

    rows = frames[0]
    count = rows.shape[0]
    gain = norm_gain[None, :]

    def ringed(value):
        return lax.ppermute(value, "head", [(z, after[z]) for z in range(layers)])

    sent, piece = pack(numbers(lax.rem(seq, share)), rows, w_out, share)
    piece = moved(piece, lambda z: before[z])
    first = moved(sent, lambda z: after[z])
    second = ringed(first)
    own = bundle(w_query, w_key, w_value, w_out)
    whole = moved(rows, lambda z: z)
    facts = jnp.concatenate([group_band[0], jnp.broadcast_to(lengths[:, None], (1, group_band.shape[2]))], axis=0)
    facts = lax.ppermute(facts, ("dp", "seq"), [(flat(c, s), flat(*home(c, s))) for c, s in here])
    *own, facts = together(*own, facts)
    far = [lax.ppermute(value, "dp", swap) for value in own]
    back = {z: before[z] for z in range(layers)}
    ids = [layer, lookup([back[z] for z in range(layers)], layer)]
    ids.append(lookup([back[back[z]] for z in range(layers)], layer))
    ids.append(lookup([after[z] for z in range(layers)], layer))
    place = numbers(core, (seq // 2 * 2 + core) * groups, groups * seqs, facts[groups, 0], *ids)
    band = facts[:groups]
    piece, = hold([piece], 1 << 33)
    whole, place, band, piece = together(whole, place, band, piece)

    core_at = numbers(core)
    done = project(core_at, [whole, first], count, width, gain, own, far, 1, room=count)
    *done, second = together(*done, second)
    third = ringed(second)
    shares = shared(join(count, first, second, piece))
    done = project(core_at, [second], count, width, gain, own, far, 1, into=done)
    query_a, pair_a = done
    link_a, chip_a = lax.ppermute(pair_a, ("dp", "seq"), over_link), lax.ppermute(pair_a, "dp", swap)
    query_c, pair_c, mine = project(core_at, [third], count, width, gain, own, far, 1 << 33, joined=shares)
    link_c, chip_c = lax.ppermute(pair_c, ("dp", "seq"), over_link), lax.ppermute(pair_c, "dp", swap)
    theirs = lax.ppermute(mine, "dp", swap)
    q_all, kv_all, vt_all = window(
        place, groups, count, [query_a, query_c], [pair_a, pair_c], [chip_a, chip_c], [link_a, link_c]
    )

    half = layers // 2
    arrived, sources = [], []
    for near in (0, 1):
        side = layer // half if near else 1 - layer // half
        turn = numbers(side * half * count, *[lax.rem(layer + e, half) * count for e in range(half)])
        if near:
            weight_place = numbers(core, layer, seq, ids[1], ids[2], ids[3])
            *contexts, weight = attend(
                place, band, turn, half, q_all, kv_all, vt_all, share, layers,
                [weight_place, w_out, far[1], mine, theirs],
            )
        else:
            contexts = list(attend(place, band, turn, half, q_all, kv_all, vt_all))
            contexts[0], q_all = together(contexts[0], q_all)
        for e, context in enumerate(contexts):
            def target(z, e=e):
                return (z // half if near else 1 - z // half) * half + (z + e) % half

            arrived.append(moved(context, target))
            sources.append(side * half + lax.rem(layer + half - e, half))
    arrived = list(hold(arrived[:half])) + arrived[half:]
    return output(numbers(*sources), weight, arrived)


def solution(mesh):
    return jax.shard_map(
        local,
        mesh=mesh,
        in_specs=(
            P("dp", ("seq", "head"), None),
            P(),
            P("dp", "head"),
            P("dp", "head"),
            P("dp", "head"),
            P("head", "dp"),
            P("dp", "seq", None),
            P("dp"),
        ),
        out_specs=P("dp", ("seq", "head"), None),
        check_vma=False,
    )
```

```python
import functools

import jax
import jax.numpy as jnp
from jax import lax
from jax.experimental import pallas as pl
from jax.experimental.pallas import tpu as pltpu
from jax.sharding import PartitionSpec as P

HD = 64
GROUP = 128
LANES = 128

epsilon = 1e-05

VMEM = pl.BlockSpec(memory_space=pltpu.VMEM)
SMEM = pl.BlockSpec(memory_space=pltpu.SMEM)
HBM = pl.BlockSpec(memory_space=pltpu.HBM)
MIB = 1024 * 1024
LIGHT = pl.CostEstimate(flops=1, bytes_accessed=1, transcendentals=0)


def ring_successors(count):
    order = [0] + list(range(1, count, 2)) + list(range(count - 2 + count % 2, 0, -2))
    return {order[i]: order[(i + 1) % count] for i in range(count)}


def lookup(table, index):
    value = jnp.int32(table[0])
    for place in range(1, len(table)):
        value = jnp.where(index == place, jnp.int32(table[place]), value)
    return value


def copy_all(pairs, sems):
    copies = [pltpu.make_async_copy(source, target, sems.at[i]) for i, (source, target) in enumerate(pairs)]
    for copy in copies:
        copy.start()
    return copies


def in_hbm(*values):
    return [pltpu.with_memory_space_constraint(value, pltpu.HBM) for value in values]


def run_copies(loads, stores, sems):
    for copy in copy_all(loads, sems):
        copy.wait()
    for copy in copy_all(stores, sems):
        copy.wait()


def pack_kernel(place_ref, rows_ref, w_out_ref, sent_ref, piece_ref, held, held_piece, sems):
    count = rows_ref.shape[0]
    part, columns = piece_ref.shape
    first = pl.multiple_of(place_ref[0] * part, 16)
    loads = [(w_out_ref.at[pl.ds(first, part), :], held_piece), (rows_ref, held.at[pl.ds(0, count), :])]
    for side in range(2):
        loads.append((
            w_out_ref.at[pl.ds(first + side * (part // 2), part // 2), :],
            held.at[pl.ds(count, part // 2), pl.ds(side * columns, columns)],
        ))
    run_copies(loads, [(held, sent_ref), (held_piece, piece_ref)], sems)


def pack(place, rows, w_out, share):
    part = w_out.shape[0] // share
    shapes = [(rows.shape[0] + part // 2, rows.shape[1]), (part, w_out.shape[1])]
    return pl.pallas_call(
        pack_kernel,
        out_shape=[pltpu.HBM(shape, jnp.bfloat16) for shape in shapes],
        in_specs=[SMEM] + [HBM] * 2,
        out_specs=[HBM] * 2,
        scratch_shapes=[pltpu.VMEM(shape, jnp.bfloat16) for shape in shapes] + [pltpu.SemaphoreType.DMA((4,))],
        compiler_params=pltpu.CompilerParams(vmem_limit_bytes=4 * MIB),
        cost_estimate=LIGHT,
        name="pack",
    )(place, *in_hbm(rows, w_out))


def bundle_kernel(query_ref, key_ref, value_ref, w_out_ref, front_ref, back_ref, held, held_back, sems):
    width, rows = query_ref.shape[1], w_out_ref.shape[0]
    loads = [
        (query_ref, held.at[:, pl.ds(0, width)]),
        (key_ref, held.at[:, pl.ds(width, width)]),
        (value_ref, held_back.at[:, pl.ds(0, width)]),
    ]
    for side in range(2):
        loads.append((
            w_out_ref.at[:, pl.ds(side * width, width)],
            held_back.at[pl.ds(side * rows, rows), pl.ds(width, width)],
        ))
    run_copies(loads, [(held, front_ref), (held_back, back_ref)], sems)


def bundle(w_query, w_key, w_value, w_out):
    shape = (w_query.shape[0], 2 * w_query.shape[1])
    return pl.pallas_call(
        bundle_kernel,
        out_shape=[pltpu.HBM(shape, jnp.bfloat16)] * 2,
        in_specs=[HBM] * 4,
        out_specs=[HBM] * 2,
        scratch_shapes=[pltpu.VMEM(shape, jnp.bfloat16)] * 2 + [pltpu.SemaphoreType.DMA((5,))],
        compiler_params=pltpu.CompilerParams(vmem_limit_bytes=4 * MIB),
        cost_estimate=LIGHT,
        name="bundle",
    )(*in_hbm(w_query, w_key, w_value, w_out))


def join_kernel(count, first_ref, second_ref, piece_ref, out_ref, held, sems):
    part, columns = piece_ref.shape[0] // 2, piece_ref.shape[1]
    loads = [
        (source.at[pl.ds(count, part), :], held.at[pl.ds(place * part, part), :])
        for place, source in enumerate((first_ref, second_ref))
    ]
    for side in range(2):
        loads.append((
            piece_ref.at[pl.ds(side * part, part), :],
            held.at[pl.ds(2 * part, part), pl.ds(side * columns, columns)],
        ))
    run_copies(loads, [(held, out_ref)], sems)


def join(count, first, second, piece):
    shape = (3 * piece.shape[0] // 2, first.shape[1])
    return pl.pallas_call(
        functools.partial(join_kernel, count),
        out_shape=pltpu.HBM(shape, jnp.bfloat16),
        in_specs=[HBM] * 3,
        out_specs=HBM,
        scratch_shapes=[pltpu.VMEM(shape, jnp.bfloat16), pltpu.SemaphoreType.DMA((4,))],
        compiler_params=pltpu.CompilerParams(vmem_limit_bytes=4 * MIB),
        cost_estimate=LIGHT,
        name="join",
    )(first, second, piece)


def project_kernel(blocks, count, place_ref, gain_ref, own_front, own_back, far_front, far_back, *refs):
    rows = refs[:blocks]
    query_ref, pair_ref, held, weight, query_held, pair_held, sems = refs[blocks:]
    depth, width = own_front.shape[0], query_ref.shape[1]
    core = place_ref[0]
    order = (1, 2, 0)
    loads = copy_all(
        [(rows[i].at[pl.ds(0, count), :], held.at[pl.ds(i * count, count), :]) for i in range(blocks)], sems
    )
    fetches = []
    for place in order:
        for pair, owner in (((own_front, own_back), core), ((far_front, far_back), 1 - core)):
            to = weight.at[place, pl.ds(pl.multiple_of(owner * depth, 16), depth), :]
            fetches.append((pair[place // 2].at[:, pl.ds(place % 2 * width, width)], to))
    fetches = copy_all(fetches, sems.at[pl.ds(blocks, len(fetches))])
    gain = gain_ref[...]
    normalized = []
    for i in range(blocks):
        loads[i].wait()
        values = held[i * count:(i + 1) * count, :].astype(jnp.float32)
        center = values - jnp.mean(values, axis=-1, keepdims=True)
        spread = jnp.mean(center * center, axis=-1, keepdims=True)
        normalized.append((center * lax.rsqrt(spread + epsilon) * gain).astype(jnp.bfloat16))
    normalized = normalized[0] if blocks == 1 else jnp.concatenate(normalized, axis=0)
    stores = []
    for turn, place in enumerate(order):
        for fetch in fetches[2 * turn:2 * turn + 2]:
            fetch.wait()
        got = jnp.dot(normalized, weight[place], preferred_element_type=jnp.float32).astype(jnp.bfloat16)
        sem = sems.at[pl.ds(blocks + len(fetches) + place, 1)]
        if place == 0:
            query_held[...] = (got.astype(jnp.float32) * (HD ** -0.5)).astype(jnp.bfloat16)
            stores += copy_all([(query_held, query_ref)], sem)
        else:
            part = pl.ds((place - 1) * width, width)
            pair_held[:, (place - 1) * width:place * width] = got
            stores += copy_all([(pair_held.at[:, part], pair_ref.at[:, part])], sem)
    for store in stores:
        store.wait()


def project(place, rows, count, width, gain, own, far, cost):
    blocks, depth = len(rows), rows[0].shape[1]
    total = blocks * count
    return pl.pallas_call(
        functools.partial(project_kernel, blocks, count),
        out_shape=[pltpu.HBM((total, width), jnp.bfloat16), pltpu.HBM((total, 2 * width), jnp.bfloat16)],
        in_specs=[SMEM, VMEM] + [HBM] * (4 + blocks),
        out_specs=[HBM, HBM],
        scratch_shapes=[
            pltpu.VMEM((total, depth), jnp.bfloat16),
            pltpu.VMEM((3, depth, width), jnp.bfloat16),
            pltpu.VMEM((total, width), jnp.bfloat16),
            pltpu.VMEM((total, 2 * width), jnp.bfloat16),
            pltpu.SemaphoreType.DMA((blocks + 9,)),
        ],
        compiler_params=pltpu.CompilerParams(vmem_limit_bytes=16 * MIB),
        cost_estimate=pl.CostEstimate(flops=cost, bytes_accessed=1, transcendentals=0),
        name="project",
    )(place, gain, *in_hbm(*own), *far, *rows)


def window_kernel(shape, groups, joined, place_ref, *refs):
    kinds = len(shape)
    queries, owns, sides = refs[:kinds], refs[kinds:2 * kinds], refs[2 * kinds:4 * kinds]
    sources = refs[4 * kinds:4 * kinds + joined]
    q_all, kv_all, vt_all, join_ref, join_held, sems = refs[4 * kinds + joined:]
    block, width = q_all.shape
    rows = block // sum(shape)
    core = place_ref[0]
    chip_base = jnp.where(core == 0, 2 * block, 0)
    link_base = jnp.where(core == 0, 0, 2 * block)
    pairs, step = [], 0
    for kind in range(kinds):
        for inside in range(shape[kind]):
            at = place_ref[4 + step] * rows
            part = pl.ds(inside * rows, rows)
            pairs.append((queries[kind].at[part, :], q_all.at[pl.ds(pl.multiple_of(at, 64), rows), :]))
            for source, base in (
                (owns[kind], block), (sides[kind], chip_base), (sides[kinds + kind], link_base)
            ):
                to = pl.ds(pl.multiple_of(base + at, 64), rows)
                pairs.append((source.at[part, :], kv_all.at[to, :]))
            step += 1
    loads = copy_all(pairs, sems)
    parts, at = [], 0
    for source in sources:
        parts.append((source, join_held.at[pl.ds(at, source.shape[0]), :]))
        at += source.shape[0]
    parts = copy_all(parts, sems.at[pl.ds(len(loads), joined)])
    for load in loads + parts:
        load.wait()
    stores = copy_all([(join_held, join_ref)], sems.at[pl.ds(len(loads) + joined, 1)])
    for index in range(3 * groups):
        for pair in range(width // LANES):
            columns = slice(width + pair * LANES, width + (pair + 1) * LANES)
            vt_all[pair, index] = kv_all[index * GROUP:(index + 1) * GROUP, columns].T
    for store in stores:
        store.wait()


def window(place, groups, rows, queries, owns, chip_side, link_side, joined):
    shape = [query.shape[0] // rows for query in queries]
    width, block = queries[0].shape[1], sum(shape) * rows
    pairs = width // LANES
    join_shape = (sum(value.shape[0] for value in joined), joined[0].shape[1])
    return pl.pallas_call(
        functools.partial(window_kernel, shape, groups, len(joined)),
        out_shape=(
            jax.ShapeDtypeStruct((block, width), jnp.bfloat16),
            jax.ShapeDtypeStruct((3 * block, 2 * width), jnp.bfloat16),
            jax.ShapeDtypeStruct((pairs, 3 * groups, LANES, GROUP), jnp.bfloat16),
            pltpu.HBM(join_shape, jnp.bfloat16),
        ),
        in_specs=[SMEM] + [HBM] * (4 * len(shape) + len(joined)),
        out_specs=(VMEM,) * 3 + (HBM,),
        scratch_shapes=[
            pltpu.VMEM(join_shape, jnp.bfloat16), pltpu.SemaphoreType.DMA((4 * sum(shape) + len(joined) + 1,))
        ],
        compiler_params=pltpu.CompilerParams(vmem_limit_bytes=16 * MIB),
        cost_estimate=pl.CostEstimate(flops=0, bytes_accessed=2 * 14 * block * width, transcendentals=0),
        name="window",
    )(place, *in_hbm(*queries, *owns), *chip_side, *link_side, *in_hbm(joined[0]), *joined[1:])


def weight_copies(share, place_ref, own_ref, far_ref, pieces_ref, theirs_ref, weight_ref):
    core, layer, seq = (place_ref[i] for i in range(3))
    layers, _, depth, columns = weight_ref.shape
    part = depth // share // 2
    half = columns // 2
    pairs = [(own_ref, weight_ref.at[layer, core])]
    for side in range(2):
        pairs.append((
            far_ref.at[pl.ds(side * depth, depth), pl.ds(far_ref.shape[1] - half, half)],
            weight_ref.at[layer, 1 - core, :, pl.ds(side * half, half)],
        ))
    for other in range(share):
        there = seq ^ other
        for source, holder in ((pieces_ref, core), (theirs_ref, 1 - core)):
            at = lax.rem(there // 2 * 2 + holder, share) * 2 * part
            for step in range(layers - 1):
                row = (other * (layers - 1) + step) * part
                for side in range(2):
                    to = pl.ds(pl.multiple_of(at + side * part, 16), part)
                    pairs.append((
                        source.at[pl.ds(row, part), pl.ds(side * columns, columns)],
                        weight_ref.at[place_ref[3 + step], lax.rem(there, 2), to, :],
                    ))
    return pairs


def attend_kernel(groups, reach, count_rows, share, place_ref, band_ref, turn_ref, q_all, kv_all, vt_all, *refs):
    loads = []
    if share:
        sources, refs = refs[:5], refs[5:]
        weight, load_sems, refs = refs[-7], refs[-1], refs[:-7] + refs[-6:-1]
        loads = copy_all(weight_copies(share, *sources, weight), load_sems)
    outs, (score, ctx, chosen, limits, sems) = refs[:-5], refs[-5:]
    pairs, rows = vt_all.shape[0], outs[0].shape[0]
    first_group, total, length = (place_ref[i] for i in range(1, 4))
    first_row = turn_ref[0]
    slots = 2 * reach + 2
    half_mask = lax.broadcasted_iota(jnp.int32, (GROUP, LANES), 1) < HD
    row_ids = lax.broadcasted_iota(jnp.int32, (GROUP, 2 * GROUP), 0)
    part_group = lax.div(length, jnp.int32(GROUP))
    part_left = lax.rem(length, jnp.int32(GROUP))

    def one_group(place, carry):
        group = first_row // GROUP + place
        for slot in range(slots):
            chosen[slot] = groups + group
        offset = part_group - first_group - group
        column = jnp.clip(jnp.where(offset < 0, offset + reach, offset + reach - 1), 0, 2 * reach - 1)
        cut = (part_left > 0) & (offset != 0) & (jnp.abs(offset) <= reach) & (part_group < total)
        cut = cut & (band_ref[group, column] == 1)
        chosen[1] = jnp.where(cut, groups + group + offset, groups + group)
        limits[0] = jnp.where(cut, part_left, 0)
        count = 1 + cut.astype(jnp.int32)
        for column in range(2 * reach):
            offset = column - reach if column < reach else column - reach + 1
            there = first_group + group + offset
            good = (there >= 0) & (there < part_group) & (there < total) & (band_ref[group, column] == 1)
            chosen[count] = jnp.where(good, groups + group + offset, groups + group)
            limits[0] = jnp.where(good & (count == 1), GROUP, limits[0])
            count = count + good.astype(jnp.int32)
        query_at = pl.ds(pl.multiple_of(group * GROUP, GROUP), GROUP)
        out_at = pl.ds(pl.multiple_of(place * GROUP, GROUP), GROUP)

        def run(size):
            first_limit = limits[0]
            last_limit = jnp.where(count == size, GROUP, 0)
            indices = [chosen[slot] for slot in range(size)]
            best = []
            for pair in range(pairs):
                own = q_all[query_at, pair * LANES:(pair + 1) * LANES]
                zero = jnp.zeros_like(own)
                both = jnp.concatenate(
                    [jnp.where(half_mask, own, zero), jnp.where(half_mask, zero, own)], axis=0
                ).T
                top = None
                for slot in range(0, size, 2):
                    tiles = [
                        kv_all[pl.ds(pl.multiple_of(index * GROUP, GROUP), GROUP), pair * LANES:(pair + 1) * LANES]
                        for index in indices[slot:slot + 2]
                    ]
                    got = jnp.dot(jnp.concatenate(tiles, axis=0), both, preferred_element_type=jnp.float32)
                    for one in (slot, slot + 1):
                        part = got[(one - slot) * GROUP:(one - slot + 1) * GROUP]
                        if one == 1:
                            part = jnp.where(row_ids < first_limit, part, -jnp.inf)
                        elif one == size - 1:
                            part = jnp.where(row_ids < last_limit, part, -jnp.inf)
                        score[pair, one * GROUP:(one + 1) * GROUP, :] = part
                        high = jnp.max(part.reshape(GROUP // 8, 8, 2 * GROUP), axis=0)
                        top = high if top is None else jnp.maximum(top, high)
                best.append(jnp.max(top, axis=0, keepdims=True))
            for pair in range(pairs):
                total_sum = jnp.zeros((8, 2 * GROUP), jnp.float32)
                mixed = jnp.zeros((LANES, 2 * GROUP), jnp.float32)
                for slot in range(0, size, 2):
                    weights = jnp.exp(score[pair, slot * GROUP:(slot + 2) * GROUP, :] - best[pair])
                    total_sum += jnp.sum(weights.reshape(2 * GROUP // 8, 8, 2 * GROUP), axis=0)
                    tiles = [vt_all[pair, index] for index in indices[slot:slot + 2]]
                    mixed += jnp.dot(
                        jnp.concatenate(tiles, axis=1),
                        weights.astype(jnp.bfloat16),
                        preferred_element_type=jnp.float32,
                    )
                mixed = mixed / jnp.sum(total_sum, axis=0, keepdims=True)
                both_heads = jnp.concatenate([mixed[:HD, :GROUP], mixed[HD:, GROUP:]], axis=0)
                ctx[out_at, pair * LANES:(pair + 1) * LANES] = both_heads.T.astype(jnp.bfloat16)

        for size in range(2, slots + 1, 2):
            @pl.when((count == size) | (count == size - 1))
            def _():
                run(size)

        return carry

    lax.fori_loop(0, count_rows // GROUP, one_group, 0)
    stores = copy_all(
        [(ctx.at[pl.ds(pl.multiple_of(turn_ref[1 + i], 64), rows), :], out) for i, out in enumerate(outs)], sems
    )
    for copy in stores + loads:
        copy.wait()


def attend(place, band, turn, outs, q_all, kv_all, vt_all, share=0, layers=0, parts=()):
    groups, reach = band.shape[0], band.shape[1] // 2
    pairs, block = vt_all.shape[0], q_all.shape[0]
    rows = block // (2 * outs)
    slots = 2 * reach + 2
    out_shape = [pltpu.HBM((rows, pairs * LANES), jnp.bfloat16)] * outs
    scratch = [
        pltpu.VMEM((pairs, slots * GROUP, 2 * GROUP), jnp.float32),
        pltpu.VMEM((block // 2, pairs * LANES), jnp.bfloat16),
        pltpu.SMEM((slots + 2,), jnp.int32),
        pltpu.SMEM((1,), jnp.int32),
        pltpu.SemaphoreType.DMA((outs,)),
    ]
    if parts:
        depth, columns = parts[1].shape
        out_shape.append(jax.ShapeDtypeStruct((layers, 2, depth, columns), jnp.bfloat16))
        scratch.append(pltpu.SemaphoreType.DMA((3 + 4 * share * (layers - 1),)))
        parts = [parts[0], *in_hbm(parts[1]), parts[2], *in_hbm(parts[3]), parts[4]]
    return pl.pallas_call(
        functools.partial(attend_kernel, groups, reach, block // 2, share),
        out_shape=out_shape,
        in_specs=[SMEM, SMEM, SMEM] + [VMEM] * 3 + ([SMEM] + [HBM] * 4 if parts else []),
        out_specs=[HBM] * outs + ([VMEM] if parts else []),
        scratch_shapes=scratch,
        compiler_params=pltpu.CompilerParams(vmem_limit_bytes=16 * MIB),
        cost_estimate=pl.CostEstimate(flops=1 << 34, bytes_accessed=1 << 20, transcendentals=0),
        name="attend",
    )(place, band, turn, q_all, kv_all, vt_all, *parts)


def output_kernel(layers, place_ref, weight, *refs):
    contexts, out_ref, held, sems = refs[:layers], *refs[layers:]
    columns = weight.shape[3]
    rows = contexts[0].shape[0]
    loads = copy_all([(contexts[step], held.at[pl.ds(step * rows, rows), :]) for step in range(layers)], sems)
    for load in loads:
        load.wait()
    for side in range(2):
        total = None
        for step in range(layers):
            got = jnp.dot(
                held[step * rows:(step + 1) * rows, :], weight[place_ref[step], side],
                preferred_element_type=jnp.float32,
            )
            total = got if step == 0 else total + got
        out_ref[0, :, side * columns:(side + 1) * columns] = total.astype(jnp.bfloat16)


def output(place, weight, contexts):
    layers, _, depth, columns = weight.shape
    rows, width = contexts[0].shape
    return pl.pallas_call(
        functools.partial(output_kernel, layers),
        out_shape=jax.ShapeDtypeStruct((1, rows, 2 * columns), jnp.bfloat16),
        in_specs=[SMEM, VMEM] + [HBM] * layers,
        out_specs=VMEM,
        scratch_shapes=[pltpu.VMEM((layers * rows, width), jnp.bfloat16), pltpu.SemaphoreType.DMA((layers,))],
        compiler_params=pltpu.CompilerParams(vmem_limit_bytes=8 * MIB),
        cost_estimate=LIGHT,
        name="output",
    )(place, weight, *contexts)


def hold_kernel(*refs):
    del refs


def hold(values, cost=1 << 34):
    return pl.pallas_call(
        hold_kernel,
        out_shape=[jax.ShapeDtypeStruct(value.shape, value.dtype) for value in values],
        in_specs=[HBM] * len(values),
        out_specs=[HBM] * len(values),
        input_output_aliases={i: i for i in range(len(values))},
        compiler_params=pltpu.CompilerParams(vmem_limit_bytes=MIB),
        cost_estimate=pl.CostEstimate(flops=cost, bytes_accessed=1, transcendentals=0),
        name="hold",
    )(*values)


def together(*values):
    return lax.optimization_barrier(values)


def numbers(*values):
    return jnp.stack([jnp.asarray(value, jnp.int32) for value in values])


def local(frames, norm_gain, w_query, w_key, w_value, w_out, group_band, lengths):
    cores, seqs, layers = lax.axis_size("dp"), lax.axis_size("seq"), lax.axis_size("head")
    core, seq, layer = lax.axis_index("dp"), lax.axis_index("seq"), lax.axis_index("head")
    groups = group_band.shape[1]
    width = w_query.shape[1]
    here = [(c, s) for c in range(cores) for s in range(seqs)]

    def home(c, s):
        return s % 2, s // 2 * 2 + c

    def flat(c, s, z=None):
        return c * seqs + s if z is None else (c * seqs + s) * layers + z

    def moved(value, shift):
        pairs = [(flat(c, s, z), flat(*home(c, s), shift(z))) for c, s in here for z in range(layers)]
        return lax.ppermute(value, ("dp", "seq", "head"), pairs)

    after = ring_successors(layers)
    before = {after[z]: z for z in after}
    swap = [(c, cores - 1 - c) for c in range(cores)]
    over_link = [(flat(1, s), flat(0, s + 2)) for s in range(seqs - 2)]
    over_link += [(flat(0, s + 2), flat(1, s)) for s in range(seqs - 2)]
    share = 4

    def shared(value, behind):
        near = [lax.ppermute(value, "seq", [(s, s ^ step) for s in range(seqs)]) for step in (1, 2)]
        *near, _ = together(*near, behind)
        return [value] + near + [lax.ppermute(near[1], "seq", [(s, s ^ 1) for s in range(seqs)])]

    rows = frames[0]
    count = rows.shape[0]
    gain = norm_gain[None, :]

    def halos(pair):
        return lax.ppermute(pair, ("dp", "seq"), over_link), lax.ppermute(pair, "dp", swap)

    def ringed(value):
        return lax.ppermute(value, "head", [(z, after[z]) for z in range(layers)])

    sent, piece = pack(numbers(lax.rem(seq, share)), rows, w_out, share)
    piece = moved(piece, lambda z: before[z])
    first = moved(sent, lambda z: after[z])
    second = ringed(first)
    own = bundle(w_query, w_key, w_value, w_out)
    whole = moved(rows, lambda z: z)
    facts = jnp.concatenate([group_band[0], jnp.broadcast_to(lengths[:, None], (1, group_band.shape[2]))], axis=0)
    facts = lax.ppermute(facts, ("dp", "seq"), [(flat(c, s), flat(*home(c, s))) for c, s in here])
    *own, facts = together(*own, facts)
    far = [lax.ppermute(value, "dp", swap) for value in own]
    back = {z: before[z] for z in range(layers)}
    ids = [layer, lookup([back[z] for z in range(layers)], layer)]
    ids.append(lookup([back[back[z]] for z in range(layers)], layer))
    ids.append(lookup([after[z] for z in range(layers)], layer))
    place = numbers(core, (seq // 2 * 2 + core) * groups, groups * seqs, facts[groups, 0], *ids)
    band = facts[:groups]
    piece, = hold([piece], 1 << 33)
    whole, place, band, piece = together(whole, place, band, piece)

    core_at = numbers(core)
    query_a, pair_a = project(core_at, [whole, first], count, width, gain, own, far, 1)
    link_a, chip_a = halos(pair_a)
    second, link_a, chip_a = together(second, link_a, chip_a)
    third = ringed(second)
    query_b, pair_b = project(core_at, [second], count, width, gain, own, far, 1)
    shares = shared(join(count, first, second, piece), query_b)
    link_b, chip_b = halos(pair_b)
    third, link_b, chip_b = together(third, link_b, chip_b)
    query_c, pair_c = project(core_at, [third], count, width, gain, own, far, 1)
    link_c, chip_c = halos(pair_c)
    q_all, kv_all, vt_all, mine = window(
        place, groups, count, [query_a, query_b, query_c], [pair_a, pair_b, pair_c],
        [chip_a, chip_b, chip_c], [link_a, link_b, link_c], shares,
    )
    theirs = lax.ppermute(mine, "dp", swap)

    half = layers // 2
    contexts, arrived, sources = [], [], []
    for near in (0, 1):
        side = layer // half if near else 1 - layer // half
        turn = numbers(side * half * count, *[lax.rem(layer + e, half) * count for e in range(half)])
        if near:
            weight_place = numbers(core, layer, seq, ids[1], ids[2], ids[3])
            *got, weight = attend(
                place, band, turn, half, q_all, kv_all, vt_all, share, layers,
                [weight_place, w_out, far[1], mine, theirs],
            )
        else:
            got = list(attend(place, band, turn, half, q_all, kv_all, vt_all))
            got[0], q_all = together(got[0], q_all)
        contexts += got
    *contexts[1:half], contexts[half] = together(*contexts[1:half], contexts[half])
    for index, context in enumerate(contexts):
        near, e = divmod(index, half)

        def target(z, near=near, e=e):
            return (z // half if near else 1 - z // half) * half + (z + e) % half

        side = layer // half if near else 1 - layer // half
        arrived.append(moved(context, target))
        sources.append(side * half + lax.rem(layer + half - e, half))
    arrived = list(hold(arrived[:1])) + arrived[1:]
    return output(numbers(*sources), weight, arrived)


def solution(mesh):
    return jax.shard_map(
        local,
        mesh=mesh,
        in_specs=(
            P("dp", ("seq", "head"), None),
            P(),
            P("dp", "head"),
            P("dp", "head"),
            P("dp", "head"),
            P("head", "dp"),
            P("dp", "seq", None),
            P("dp"),
        ),
        out_specs=P("dp", ("seq", "head"), None),
        check_vma=False,
    )
```

```python
import functools

import jax
import jax.numpy as jnp
from jax import lax
from jax.experimental import pallas as pl
from jax.experimental.pallas import tpu as pltpu
from jax.sharding import PartitionSpec as P

HD = 64
GROUP = 128
LANES = 128

epsilon = 1e-05

VMEM = pl.BlockSpec(memory_space=pltpu.VMEM)
SMEM = pl.BlockSpec(memory_space=pltpu.SMEM)
HBM = pl.BlockSpec(memory_space=pltpu.HBM)
MIB = 1024 * 1024
LIGHT = pl.CostEstimate(flops=1, bytes_accessed=1, transcendentals=0)


def ring_successors(count):
    order = [0] + list(range(1, count, 2)) + list(range(count - 2 + count % 2, 0, -2))
    return {order[i]: order[(i + 1) % count] for i in range(count)}


def lookup(table, index):
    value = jnp.int32(table[0])
    for place in range(1, len(table)):
        value = jnp.where(index == place, jnp.int32(table[place]), value)
    return value


def copy_all(pairs, sems):
    copies = [pltpu.make_async_copy(source, target, sems.at[i]) for i, (source, target) in enumerate(pairs)]
    for copy in copies:
        copy.start()
    return copies


def in_hbm(*values):
    return [pltpu.with_memory_space_constraint(value, pltpu.HBM) for value in values]


def run_copies(loads, stores, sems):
    for copy in copy_all(loads, sems):
        copy.wait()
    for copy in copy_all(stores, sems):
        copy.wait()


def pack_kernel(place_ref, rows_ref, w_out_ref, sent_ref, piece_ref, held, held_piece, sems):
    count = rows_ref.shape[0]
    part, columns = piece_ref.shape
    first = pl.multiple_of(place_ref[0] * part, 16)
    loads = [(w_out_ref.at[pl.ds(first, part), :], held_piece), (rows_ref, held.at[pl.ds(0, count), :])]
    for side in range(2):
        loads.append((
            w_out_ref.at[pl.ds(first + side * (part // 2), part // 2), :],
            held.at[pl.ds(count, part // 2), pl.ds(side * columns, columns)],
        ))
    run_copies(loads, [(held, sent_ref), (held_piece, piece_ref)], sems)


def pack(place, rows, w_out, share):
    part = w_out.shape[0] // share
    shapes = [(rows.shape[0] + part // 2, rows.shape[1]), (part, w_out.shape[1])]
    return pl.pallas_call(
        pack_kernel,
        out_shape=[pltpu.HBM(shape, jnp.bfloat16) for shape in shapes],
        in_specs=[SMEM] + [HBM] * 2,
        out_specs=[HBM] * 2,
        scratch_shapes=[pltpu.VMEM(shape, jnp.bfloat16) for shape in shapes] + [pltpu.SemaphoreType.DMA((4,))],
        compiler_params=pltpu.CompilerParams(vmem_limit_bytes=4 * MIB),
        cost_estimate=LIGHT,
        name="pack",
    )(place, *in_hbm(rows, w_out))


def bundle_kernel(query_ref, key_ref, value_ref, w_out_ref, front_ref, back_ref, held, held_back, sems):
    width, rows = query_ref.shape[1], w_out_ref.shape[0]
    loads = [
        (query_ref, held.at[:, pl.ds(0, width)]),
        (key_ref, held.at[:, pl.ds(width, width)]),
        (value_ref, held_back.at[:, pl.ds(0, width)]),
    ]
    for side in range(2):
        loads.append((
            w_out_ref.at[:, pl.ds(side * width, width)],
            held_back.at[pl.ds(side * rows, rows), pl.ds(width, width)],
        ))
    run_copies(loads, [(held, front_ref), (held_back, back_ref)], sems)


def bundle(w_query, w_key, w_value, w_out):
    shape = (w_query.shape[0], 2 * w_query.shape[1])
    return pl.pallas_call(
        bundle_kernel,
        out_shape=[pltpu.HBM(shape, jnp.bfloat16)] * 2,
        in_specs=[HBM] * 4,
        out_specs=[HBM] * 2,
        scratch_shapes=[pltpu.VMEM(shape, jnp.bfloat16)] * 2 + [pltpu.SemaphoreType.DMA((5,))],
        compiler_params=pltpu.CompilerParams(vmem_limit_bytes=4 * MIB),
        cost_estimate=LIGHT,
        name="bundle",
    )(*in_hbm(w_query, w_key, w_value, w_out))


def join_kernel(count, first_ref, second_ref, piece_ref, out_ref, held, sems):
    part, columns = piece_ref.shape[0] // 2, piece_ref.shape[1]
    loads = [
        (source.at[pl.ds(count, part), :], held.at[pl.ds(place * part, part), :])
        for place, source in enumerate((first_ref, second_ref))
    ]
    for side in range(2):
        loads.append((
            piece_ref.at[pl.ds(side * part, part), :],
            held.at[pl.ds(2 * part, part), pl.ds(side * columns, columns)],
        ))
    run_copies(loads, [(held, out_ref)], sems)


def join(count, first, second, piece):
    shape = (3 * piece.shape[0] // 2, first.shape[1])
    return pl.pallas_call(
        functools.partial(join_kernel, count),
        out_shape=pltpu.HBM(shape, jnp.bfloat16),
        in_specs=[HBM] * 3,
        out_specs=HBM,
        scratch_shapes=[pltpu.VMEM(shape, jnp.bfloat16), pltpu.SemaphoreType.DMA((4,))],
        compiler_params=pltpu.CompilerParams(vmem_limit_bytes=4 * MIB),
        cost_estimate=LIGHT,
        name="join",
    )(first, second, piece)


def project_kernel(blocks, count, place_ref, gain_ref, own_front, own_back, far_front, far_back, *refs):
    rows = refs[:blocks]
    query_ref, pair_ref, held, weight, query_held, pair_held, sems = refs[blocks:]
    depth, width = own_front.shape[0], query_ref.shape[1]
    core = place_ref[0]
    order = (1, 2, 0)
    loads = copy_all(
        [(rows[i].at[pl.ds(0, count), :], held.at[pl.ds(i * count, count), :]) for i in range(blocks)], sems
    )
    fetches = []
    for place in order:
        for pair, owner in (((own_front, own_back), core), ((far_front, far_back), 1 - core)):
            to = weight.at[place, pl.ds(pl.multiple_of(owner * depth, 16), depth), :]
            fetches.append((pair[place // 2].at[:, pl.ds(place % 2 * width, width)], to))
    fetches = copy_all(fetches, sems.at[pl.ds(blocks, len(fetches))])
    gain = gain_ref[...]
    normalized = []
    for i in range(blocks):
        loads[i].wait()
        values = held[i * count:(i + 1) * count, :].astype(jnp.float32)
        center = values - jnp.mean(values, axis=-1, keepdims=True)
        spread = jnp.mean(center * center, axis=-1, keepdims=True)
        normalized.append((center * lax.rsqrt(spread + epsilon) * gain).astype(jnp.bfloat16))
    normalized = normalized[0] if blocks == 1 else jnp.concatenate(normalized, axis=0)
    stores = []
    for turn, place in enumerate(order):
        for fetch in fetches[2 * turn:2 * turn + 2]:
            fetch.wait()
        got = jnp.dot(normalized, weight[place], preferred_element_type=jnp.float32).astype(jnp.bfloat16)
        sem = sems.at[pl.ds(blocks + len(fetches) + place, 1)]
        if place == 0:
            query_held[...] = (got.astype(jnp.float32) * (HD ** -0.5)).astype(jnp.bfloat16)
            stores += copy_all([(query_held, query_ref)], sem)
        else:
            part = pl.ds((place - 1) * width, width)
            pair_held[:, (place - 1) * width:place * width] = got
            stores += copy_all([(pair_held.at[:, part], pair_ref.at[:, part])], sem)
    for store in stores:
        store.wait()


def project(place, rows, count, width, gain, own, far, cost):
    blocks, depth = len(rows), rows[0].shape[1]
    total = blocks * count
    return pl.pallas_call(
        functools.partial(project_kernel, blocks, count),
        out_shape=[pltpu.HBM((total, width), jnp.bfloat16), pltpu.HBM((total, 2 * width), jnp.bfloat16)],
        in_specs=[SMEM, VMEM] + [HBM] * (4 + blocks),
        out_specs=[HBM, HBM],
        scratch_shapes=[
            pltpu.VMEM((total, depth), jnp.bfloat16),
            pltpu.VMEM((3, depth, width), jnp.bfloat16),
            pltpu.VMEM((total, width), jnp.bfloat16),
            pltpu.VMEM((total, 2 * width), jnp.bfloat16),
            pltpu.SemaphoreType.DMA((blocks + 9,)),
        ],
        compiler_params=pltpu.CompilerParams(vmem_limit_bytes=16 * MIB),
        cost_estimate=pl.CostEstimate(flops=cost, bytes_accessed=1, transcendentals=0),
        name="project",
    )(place, gain, *in_hbm(*own), *far, *rows)


def window_kernel(shape, groups, joined, place_ref, *refs):
    kinds = len(shape)
    queries, owns, sides = refs[:kinds], refs[kinds:2 * kinds], refs[2 * kinds:4 * kinds]
    sources = refs[4 * kinds:4 * kinds + joined]
    q_all, kv_all, vt_all, join_ref, join_held, sems = refs[4 * kinds + joined:]
    block, width = q_all.shape
    rows = block // sum(shape)
    core = place_ref[0]
    chip_base = jnp.where(core == 0, 2 * block, 0)
    link_base = jnp.where(core == 0, 0, 2 * block)
    pairs, step = [], 0
    for kind in range(kinds):
        for inside in range(shape[kind]):
            at = place_ref[4 + step] * rows
            part = pl.ds(inside * rows, rows)
            pairs.append((queries[kind].at[part, :], q_all.at[pl.ds(pl.multiple_of(at, 64), rows), :]))
            for source, base in (
                (owns[kind], block), (sides[kind], chip_base), (sides[kinds + kind], link_base)
            ):
                to = pl.ds(pl.multiple_of(base + at, 64), rows)
                pairs.append((source.at[part, :], kv_all.at[to, :]))
            step += 1
    loads = copy_all(pairs, sems)
    parts, at = [], 0
    for source in sources:
        parts.append((source, join_held.at[pl.ds(at, source.shape[0]), :]))
        at += source.shape[0]
    parts = copy_all(parts, sems.at[pl.ds(len(loads), joined)])
    for load in loads + parts:
        load.wait()
    stores = copy_all([(join_held, join_ref)], sems.at[pl.ds(len(loads) + joined, 1)])
    for index in range(3 * groups):
        for pair in range(width // LANES):
            columns = slice(width + pair * LANES, width + (pair + 1) * LANES)
            vt_all[pair, index] = kv_all[index * GROUP:(index + 1) * GROUP, columns].T
    for store in stores:
        store.wait()


def window(place, groups, rows, queries, owns, chip_side, link_side, joined):
    shape = [query.shape[0] // rows for query in queries]
    width, block = queries[0].shape[1], sum(shape) * rows
    pairs = width // LANES
    join_shape = (sum(value.shape[0] for value in joined), joined[0].shape[1])
    return pl.pallas_call(
        functools.partial(window_kernel, shape, groups, len(joined)),
        out_shape=(
            jax.ShapeDtypeStruct((block, width), jnp.bfloat16),
            jax.ShapeDtypeStruct((3 * block, 2 * width), jnp.bfloat16),
            jax.ShapeDtypeStruct((pairs, 3 * groups, LANES, GROUP), jnp.bfloat16),
            pltpu.HBM(join_shape, jnp.bfloat16),
        ),
        in_specs=[SMEM] + [HBM] * (4 * len(shape) + len(joined)),
        out_specs=(VMEM,) * 3 + (HBM,),
        scratch_shapes=[
            pltpu.VMEM(join_shape, jnp.bfloat16), pltpu.SemaphoreType.DMA((4 * sum(shape) + len(joined) + 1,))
        ],
        compiler_params=pltpu.CompilerParams(vmem_limit_bytes=16 * MIB),
        cost_estimate=pl.CostEstimate(flops=0, bytes_accessed=2 * 14 * block * width, transcendentals=0),
        name="window",
    )(place, *in_hbm(*queries, *owns), *chip_side, *link_side, *in_hbm(joined[0]), *joined[1:])


def weight_copies(share, place_ref, own_ref, far_ref, pieces_ref, theirs_ref, weight_ref):
    core, layer, seq = (place_ref[i] for i in range(3))
    layers, _, depth, columns = weight_ref.shape
    part = depth // share // 2
    half = columns // 2
    pairs = [(own_ref, weight_ref.at[layer, core])]
    for side in range(2):
        pairs.append((
            far_ref.at[pl.ds(side * depth, depth), pl.ds(far_ref.shape[1] - half, half)],
            weight_ref.at[layer, 1 - core, :, pl.ds(side * half, half)],
        ))
    for other in range(share):
        there = seq ^ other
        for source, holder in ((pieces_ref, core), (theirs_ref, 1 - core)):
            at = lax.rem(there // 2 * 2 + holder, share) * 2 * part
            for step in range(layers - 1):
                row = (other * (layers - 1) + step) * part
                for side in range(2):
                    to = pl.ds(pl.multiple_of(at + side * part, 16), part)
                    pairs.append((
                        source.at[pl.ds(row, part), pl.ds(side * columns, columns)],
                        weight_ref.at[place_ref[3 + step], lax.rem(there, 2), to, :],
                    ))
    return pairs


def attend_kernel(groups, reach, count_rows, share, place_ref, band_ref, turn_ref, q_all, kv_all, vt_all, *refs):
    loads = []
    if share:
        sources, refs = refs[:5], refs[5:]
        weight, load_sems, refs = refs[-7], refs[-1], refs[:-7] + refs[-6:-1]
        loads = copy_all(weight_copies(share, *sources, weight), load_sems)
    outs, (score, ctx, chosen, limits, sems) = refs[:-5], refs[-5:]
    pairs, rows = vt_all.shape[0], outs[0].shape[0]
    first_group, total, length = (place_ref[i] for i in range(1, 4))
    first_row = turn_ref[0]
    slots = 2 * reach + 2
    half_mask = lax.broadcasted_iota(jnp.int32, (GROUP, LANES), 1) < HD
    row_ids = lax.broadcasted_iota(jnp.int32, (GROUP, 2 * GROUP), 0)
    part_group = lax.div(length, jnp.int32(GROUP))
    part_left = lax.rem(length, jnp.int32(GROUP))

    def one_group(place, carry):
        group = first_row // GROUP + place
        for slot in range(slots):
            chosen[slot] = groups + group
        offset = part_group - first_group - group
        column = jnp.clip(jnp.where(offset < 0, offset + reach, offset + reach - 1), 0, 2 * reach - 1)
        cut = (part_left > 0) & (offset != 0) & (jnp.abs(offset) <= reach) & (part_group < total)
        cut = cut & (band_ref[group, column] == 1)
        chosen[1] = jnp.where(cut, groups + group + offset, groups + group)
        limits[0] = jnp.where(cut, part_left, 0)
        count = 1 + cut.astype(jnp.int32)
        for column in range(2 * reach):
            offset = column - reach if column < reach else column - reach + 1
            there = first_group + group + offset
            good = (there >= 0) & (there < part_group) & (there < total) & (band_ref[group, column] == 1)
            chosen[count] = jnp.where(good, groups + group + offset, groups + group)
            limits[0] = jnp.where(good & (count == 1), GROUP, limits[0])
            count = count + good.astype(jnp.int32)
        query_at = pl.ds(pl.multiple_of(group * GROUP, GROUP), GROUP)
        out_at = pl.ds(pl.multiple_of(place * GROUP, GROUP), GROUP)

        def run(size):
            first_limit = limits[0]
            last_limit = jnp.where(count == size, GROUP, 0)
            indices = [chosen[slot] for slot in range(size)]
            best = []
            for pair in range(pairs):
                own = q_all[query_at, pair * LANES:(pair + 1) * LANES]
                zero = jnp.zeros_like(own)
                both = jnp.concatenate(
                    [jnp.where(half_mask, own, zero), jnp.where(half_mask, zero, own)], axis=0
                ).T
                top = None
                for slot in range(0, size, 2):
                    tiles = [
                        kv_all[pl.ds(pl.multiple_of(index * GROUP, GROUP), GROUP), pair * LANES:(pair + 1) * LANES]
                        for index in indices[slot:slot + 2]
                    ]
                    got = jnp.dot(jnp.concatenate(tiles, axis=0), both, preferred_element_type=jnp.float32)
                    for one in (slot, slot + 1):
                        part = got[(one - slot) * GROUP:(one - slot + 1) * GROUP]
                        if one == 1:
                            part = jnp.where(row_ids < first_limit, part, -jnp.inf)
                        elif one == size - 1:
                            part = jnp.where(row_ids < last_limit, part, -jnp.inf)
                        score[pair, one * GROUP:(one + 1) * GROUP, :] = part
                        high = jnp.max(part.reshape(GROUP // 8, 8, 2 * GROUP), axis=0)
                        top = high if top is None else jnp.maximum(top, high)
                best.append(jnp.max(top, axis=0, keepdims=True))
            for pair in range(pairs):
                total_sum = jnp.zeros((8, 2 * GROUP), jnp.float32)
                mixed = jnp.zeros((LANES, 2 * GROUP), jnp.float32)
                for slot in range(0, size, 2):
                    weights = jnp.exp(score[pair, slot * GROUP:(slot + 2) * GROUP, :] - best[pair])
                    total_sum += jnp.sum(weights.reshape(2 * GROUP // 8, 8, 2 * GROUP), axis=0)
                    tiles = [vt_all[pair, index] for index in indices[slot:slot + 2]]
                    mixed += jnp.dot(
                        jnp.concatenate(tiles, axis=1),
                        weights.astype(jnp.bfloat16),
                        preferred_element_type=jnp.float32,
                    )
                mixed = mixed / jnp.sum(total_sum, axis=0, keepdims=True)
                both_heads = jnp.concatenate([mixed[:HD, :GROUP], mixed[HD:, GROUP:]], axis=0)
                ctx[out_at, pair * LANES:(pair + 1) * LANES] = both_heads.T.astype(jnp.bfloat16)

        for size in range(2, slots + 1, 2):
            @pl.when((count == size) | (count == size - 1))
            def _():
                run(size)

        return carry

    lax.fori_loop(0, count_rows // GROUP, one_group, 0)
    stores = copy_all(
        [(ctx.at[pl.ds(pl.multiple_of(turn_ref[1 + i], 64), rows), :], out) for i, out in enumerate(outs)], sems
    )
    for copy in stores + loads:
        copy.wait()


def attend(place, band, turn, outs, q_all, kv_all, vt_all, share=0, layers=0, parts=()):
    groups, reach = band.shape[0], band.shape[1] // 2
    pairs, block = vt_all.shape[0], q_all.shape[0]
    rows = block // (2 * outs)
    slots = 2 * reach + 2
    out_shape = [pltpu.HBM((rows, pairs * LANES), jnp.bfloat16)] * outs
    scratch = [
        pltpu.VMEM((pairs, slots * GROUP, 2 * GROUP), jnp.float32),
        pltpu.VMEM((block // 2, pairs * LANES), jnp.bfloat16),
        pltpu.SMEM((slots + 2,), jnp.int32),
        pltpu.SMEM((1,), jnp.int32),
        pltpu.SemaphoreType.DMA((outs,)),
    ]
    if parts:
        depth, columns = parts[1].shape
        out_shape.append(jax.ShapeDtypeStruct((layers, 2, depth, columns), jnp.bfloat16))
        scratch.append(pltpu.SemaphoreType.DMA((3 + 4 * share * (layers - 1),)))
        parts = [parts[0], *in_hbm(parts[1]), parts[2], *in_hbm(parts[3]), parts[4]]
    return pl.pallas_call(
        functools.partial(attend_kernel, groups, reach, block // 2, share),
        out_shape=out_shape,
        in_specs=[SMEM, SMEM, SMEM] + [VMEM] * 3 + ([SMEM] + [HBM] * 4 if parts else []),
        out_specs=[HBM] * outs + ([VMEM] if parts else []),
        scratch_shapes=scratch,
        compiler_params=pltpu.CompilerParams(vmem_limit_bytes=16 * MIB),
        cost_estimate=pl.CostEstimate(flops=1 << 34, bytes_accessed=1 << 20, transcendentals=0),
        name="attend",
    )(place, band, turn, q_all, kv_all, vt_all, *parts)


def output_kernel(layers, place_ref, weight, *refs):
    contexts, out_ref, held, sems = refs[:layers], *refs[layers:]
    columns = weight.shape[3]
    rows = contexts[0].shape[0]
    loads = copy_all([(contexts[step], held.at[pl.ds(step * rows, rows), :]) for step in range(layers)], sems)
    for load in loads:
        load.wait()
    for side in range(2):
        total = None
        for step in range(layers):
            got = jnp.dot(
                held[step * rows:(step + 1) * rows, :], weight[place_ref[step], side],
                preferred_element_type=jnp.float32,
            )
            total = got if step == 0 else total + got
        out_ref[0, :, side * columns:(side + 1) * columns] = total.astype(jnp.bfloat16)


def output(place, weight, contexts):
    layers, _, depth, columns = weight.shape
    rows, width = contexts[0].shape
    return pl.pallas_call(
        functools.partial(output_kernel, layers),
        out_shape=jax.ShapeDtypeStruct((1, rows, 2 * columns), jnp.bfloat16),
        in_specs=[SMEM, VMEM] + [HBM] * layers,
        out_specs=VMEM,
        scratch_shapes=[pltpu.VMEM((layers * rows, width), jnp.bfloat16), pltpu.SemaphoreType.DMA((layers,))],
        compiler_params=pltpu.CompilerParams(vmem_limit_bytes=8 * MIB),
        cost_estimate=LIGHT,
        name="output",
    )(place, weight, *contexts)


def hold_kernel(*refs):
    del refs


def hold(values, cost=1 << 34):
    return pl.pallas_call(
        hold_kernel,
        out_shape=[jax.ShapeDtypeStruct(value.shape, value.dtype) for value in values],
        in_specs=[HBM] * len(values),
        out_specs=[HBM] * len(values),
        input_output_aliases={i: i for i in range(len(values))},
        compiler_params=pltpu.CompilerParams(vmem_limit_bytes=MIB),
        cost_estimate=pl.CostEstimate(flops=cost, bytes_accessed=1, transcendentals=0),
        name="hold",
    )(*values)


def together(*values):
    return lax.optimization_barrier(values)


def numbers(*values):
    return jnp.stack([jnp.asarray(value, jnp.int32) for value in values])


def local(frames, norm_gain, w_query, w_key, w_value, w_out, group_band, lengths):
    cores, seqs, layers = lax.axis_size("dp"), lax.axis_size("seq"), lax.axis_size("head")
    core, seq, layer = lax.axis_index("dp"), lax.axis_index("seq"), lax.axis_index("head")
    groups = group_band.shape[1]
    width = w_query.shape[1]
    here = [(c, s) for c in range(cores) for s in range(seqs)]

    def home(c, s):
        return s % 2, s // 2 * 2 + c

    def flat(c, s, z=None):
        return c * seqs + s if z is None else (c * seqs + s) * layers + z

    def moved(value, shift):
        pairs = [(flat(c, s, z), flat(*home(c, s), shift(z))) for c, s in here for z in range(layers)]
        return lax.ppermute(value, ("dp", "seq", "head"), pairs)

    after = ring_successors(layers)
    before = {after[z]: z for z in after}
    swap = [(c, cores - 1 - c) for c in range(cores)]
    over_link = [(flat(1, s), flat(0, s + 2)) for s in range(seqs - 2)]
    over_link += [(flat(0, s + 2), flat(1, s)) for s in range(seqs - 2)]
    share = 4

    def shared(value, behind):
        near = [lax.ppermute(value, "seq", [(s, s ^ step) for s in range(seqs)]) for step in (1, 2)]
        *near, _ = together(*near, behind)
        return [value] + near + [lax.ppermute(near[1], "seq", [(s, s ^ 1) for s in range(seqs)])]

    rows = frames[0]
    count = rows.shape[0]
    gain = norm_gain[None, :]

    def halos(pair):
        return lax.ppermute(pair, ("dp", "seq"), over_link), lax.ppermute(pair, "dp", swap)

    def ringed(value):
        return lax.ppermute(value, "head", [(z, after[z]) for z in range(layers)])

    sent, piece = pack(numbers(lax.rem(seq, share)), rows, w_out, share)
    piece = moved(piece, lambda z: before[z])
    first = moved(sent, lambda z: after[z])
    second = ringed(first)
    own = bundle(w_query, w_key, w_value, w_out)
    whole = moved(rows, lambda z: z)
    facts = jnp.concatenate([group_band[0], jnp.broadcast_to(lengths[:, None], (1, group_band.shape[2]))], axis=0)
    facts = lax.ppermute(facts, ("dp", "seq"), [(flat(c, s), flat(*home(c, s))) for c, s in here])
    *own, facts = together(*own, facts)
    far = [lax.ppermute(value, "dp", swap) for value in own]
    back = {z: before[z] for z in range(layers)}
    ids = [layer, lookup([back[z] for z in range(layers)], layer)]
    ids.append(lookup([back[back[z]] for z in range(layers)], layer))
    ids.append(lookup([after[z] for z in range(layers)], layer))
    place = numbers(core, (seq // 2 * 2 + core) * groups, groups * seqs, facts[groups, 0], *ids)
    band = facts[:groups]
    piece, = hold([piece], 1 << 33)
    half = layers // 2
    sides = (1 - layer // half, layer // half)
    turns = [
        numbers(side * half * count, *[lax.rem(layer + e, half) * count for e in range(half)]) for side in sides
    ]
    weight_place = numbers(core, layer, seq, ids[1], ids[2], ids[3])
    sources = numbers(*[side * half + lax.rem(layer + half - e, half) for side in sides for e in range(half)])
    core_at = numbers(core)
    whole, place, band, piece, weight_place, sources, core_at, *turns = together(
        whole, place, band, piece, weight_place, sources, core_at, *turns
    )

    query_a, pair_a = project(core_at, [whole, first], count, width, gain, own, far, 1)
    link_a, chip_a = halos(pair_a)
    second, link_a, chip_a = together(second, link_a, chip_a)
    third = ringed(second)
    query_b, pair_b = project(core_at, [second], count, width, gain, own, far, 1)
    shares = shared(join(count, first, second, piece), query_b)
    link_b, chip_b = halos(pair_b)
    third, link_b, chip_b = together(third, link_b, chip_b)
    query_c, pair_c = project(core_at, [third], count, width, gain, own, far, 1)
    link_c, chip_c = halos(pair_c)
    q_all, kv_all, vt_all, mine = window(
        place, groups, count, [query_a, query_b, query_c], [pair_a, pair_b, pair_c],
        [chip_a, chip_b, chip_c], [link_a, link_b, link_c], shares,
    )
    theirs = lax.ppermute(mine, "dp", swap)

    contexts, arrived = [], []
    for near in (0, 1):
        if near:
            *got, weight = attend(
                place, band, turns[near], half, q_all, kv_all, vt_all, share, layers,
                [weight_place, w_out, far[1], mine, theirs],
            )
        else:
            got = list(attend(place, band, turns[near], half, q_all, kv_all, vt_all))
            got[0], q_all = together(got[0], q_all)
        contexts += got
    *contexts[1:half], contexts[half] = together(*contexts[1:half], contexts[half])
    for index, context in enumerate(contexts):
        near, e = divmod(index, half)

        def target(z, near=near, e=e):
            return (z // half if near else 1 - z // half) * half + (z + e) % half

        arrived.append(moved(context, target))
    arrived = list(hold(arrived[:1])) + arrived[1:]
    return output(sources, weight, arrived)


def solution(mesh):
    return jax.shard_map(
        local,
        mesh=mesh,
        in_specs=(
            P("dp", ("seq", "head"), None),
            P(),
            P("dp", "head"),
            P("dp", "head"),
            P("dp", "head"),
            P("head", "dp"),
            P("dp", "seq", None),
            P("dp"),
        ),
        out_specs=P("dp", ("seq", "head"), None),
        check_vma=False,
    )
```

```python
import functools

import jax
import jax.numpy as jnp
from jax import lax
from jax.experimental import pallas as pl
from jax.experimental.pallas import tpu as pltpu
from jax.sharding import PartitionSpec as P

HD = 64
GROUP = 128
LANES = 128

epsilon = 1e-05

VMEM = pl.BlockSpec(memory_space=pltpu.VMEM)
SMEM = pl.BlockSpec(memory_space=pltpu.SMEM)
HBM = pl.BlockSpec(memory_space=pltpu.HBM)
MIB = 1024 * 1024
LIGHT = pl.CostEstimate(flops=1, bytes_accessed=1, transcendentals=0)


def ring_successors(count):
    order = [0] + list(range(1, count, 2)) + list(range(count - 2 + count % 2, 0, -2))
    return {order[i]: order[(i + 1) % count] for i in range(count)}


def lookup(table, index):
    value = jnp.int32(table[0])
    for place in range(1, len(table)):
        value = jnp.where(index == place, jnp.int32(table[place]), value)
    return value


def copy_all(pairs, sems):
    copies = [pltpu.make_async_copy(source, target, sems.at[i]) for i, (source, target) in enumerate(pairs)]
    for copy in copies:
        copy.start()
    return copies


def in_hbm(*values):
    return [pltpu.with_memory_space_constraint(value, pltpu.HBM) for value in values]


def run_copies(loads, stores, sems):
    for copy in copy_all(loads, sems):
        copy.wait()
    for copy in copy_all(stores, sems):
        copy.wait()


def pack_kernel(place_ref, rows_ref, w_out_ref, sent_ref, piece_ref, held, held_piece, sems):
    count = rows_ref.shape[0]
    part, columns = piece_ref.shape
    first = pl.multiple_of(place_ref[0] * part, 16)
    loads = [(w_out_ref.at[pl.ds(first, part), :], held_piece), (rows_ref, held.at[pl.ds(0, count), :])]
    for side in range(2):
        loads.append((
            w_out_ref.at[pl.ds(first + side * (part // 2), part // 2), :],
            held.at[pl.ds(count, part // 2), pl.ds(side * columns, columns)],
        ))
    run_copies(loads, [(held, sent_ref), (held_piece, piece_ref)], sems)


def pack(place, rows, w_out, share):
    part = w_out.shape[0] // share
    shapes = [(rows.shape[0] + part // 2, rows.shape[1]), (part, w_out.shape[1])]
    return pl.pallas_call(
        pack_kernel,
        out_shape=[pltpu.HBM(shape, jnp.bfloat16) for shape in shapes],
        in_specs=[SMEM] + [HBM] * 2,
        out_specs=[HBM] * 2,
        scratch_shapes=[pltpu.VMEM(shape, jnp.bfloat16) for shape in shapes] + [pltpu.SemaphoreType.DMA((4,))],
        compiler_params=pltpu.CompilerParams(vmem_limit_bytes=4 * MIB),
        cost_estimate=LIGHT,
        name="pack",
    )(place, *in_hbm(rows, w_out))


def bundle_kernel(query_ref, key_ref, value_ref, w_out_ref, front_ref, back_ref, sems):
    width, rows = query_ref.shape[1], w_out_ref.shape[0]
    loads = [
        (query_ref, front_ref.at[:, pl.ds(0, width)]),
        (key_ref, front_ref.at[:, pl.ds(width, width)]),
        (value_ref, back_ref.at[:, pl.ds(0, width)]),
    ]
    for side in range(2):
        loads.append((
            w_out_ref.at[:, pl.ds(side * width, width)],
            back_ref.at[pl.ds(side * rows, rows), pl.ds(width, width)],
        ))
    for load in copy_all(loads, sems):
        load.wait()


def bundle(w_query, w_key, w_value, w_out):
    shape = (w_query.shape[0], 2 * w_query.shape[1])
    return pl.pallas_call(
        bundle_kernel,
        out_shape=[jax.ShapeDtypeStruct(shape, jnp.bfloat16)] * 2,
        in_specs=[HBM] * 4,
        out_specs=[VMEM] * 2,
        scratch_shapes=[pltpu.SemaphoreType.DMA((5,))],
        compiler_params=pltpu.CompilerParams(vmem_limit_bytes=4 * MIB),
        cost_estimate=LIGHT,
        name="bundle",
    )(*in_hbm(w_query, w_key, w_value, w_out))


def join_kernel(count, first_ref, second_ref, piece_ref, out_ref, held, sems):
    part, columns = piece_ref.shape[0] // 2, piece_ref.shape[1]
    loads = [
        (source.at[pl.ds(count, part), :], held.at[pl.ds(place * part, part), :])
        for place, source in enumerate((first_ref, second_ref))
    ]
    for side in range(2):
        loads.append((
            piece_ref.at[pl.ds(side * part, part), :],
            held.at[pl.ds(2 * part, part), pl.ds(side * columns, columns)],
        ))
    run_copies(loads, [(held, out_ref)], sems)


def join(count, first, second, piece):
    shape = (3 * piece.shape[0] // 2, first.shape[1])
    return pl.pallas_call(
        functools.partial(join_kernel, count),
        out_shape=pltpu.HBM(shape, jnp.bfloat16),
        in_specs=[HBM] * 3,
        out_specs=HBM,
        scratch_shapes=[pltpu.VMEM(shape, jnp.bfloat16), pltpu.SemaphoreType.DMA((4,))],
        compiler_params=pltpu.CompilerParams(vmem_limit_bytes=4 * MIB),
        cost_estimate=LIGHT,
        name="join",
    )(first, second, piece)


def project_kernel(blocks, count, place_ref, gain_ref, own_front, own_back, far_front, far_back, *refs):
    rows = refs[:blocks]
    query_ref, pair_ref, held, query_held, pair_held, sems = refs[blocks:]
    depth, width = own_front.shape[0], query_ref.shape[1]
    first = place_ref[0] == 0
    loads = copy_all(
        [(rows[i].at[pl.ds(0, count), :], held.at[pl.ds(i * count, count), :]) for i in range(blocks)], sems
    )
    gain = gain_ref[...]
    mine, theirs = [], []
    for i in range(blocks):
        loads[i].wait()
        values = held[i * count:(i + 1) * count, :].astype(jnp.float32)
        center = values - jnp.mean(values, axis=-1, keepdims=True)
        spread = jnp.mean(center * center, axis=-1, keepdims=True)
        normalized = (center * lax.rsqrt(spread + epsilon) * gain).astype(jnp.bfloat16)
        low, high = normalized[:, :depth], normalized[:, depth:]
        mine.append(jnp.where(first, low, high))
        theirs.append(jnp.where(first, high, low))
    mine = mine[0] if blocks == 1 else jnp.concatenate(mine, axis=0)
    theirs = theirs[0] if blocks == 1 else jnp.concatenate(theirs, axis=0)
    stores = []
    for place in (1, 2, 0):
        own, far = ((own_front, far_front), (own_back, far_back))[place // 2]
        columns = slice(place % 2 * width, (place % 2 + 1) * width)
        got = jnp.dot(mine, own[:, columns], preferred_element_type=jnp.float32)
        got = (got + jnp.dot(theirs, far[:, columns], preferred_element_type=jnp.float32)).astype(jnp.bfloat16)
        sem = sems.at[pl.ds(blocks + place, 1)]
        if place == 0:
            query_held[...] = (got.astype(jnp.float32) * (HD ** -0.5)).astype(jnp.bfloat16)
            stores += copy_all([(query_held, query_ref)], sem)
        else:
            part = pl.ds((place - 1) * width, width)
            pair_held[:, (place - 1) * width:place * width] = got
            stores += copy_all([(pair_held.at[:, part], pair_ref.at[:, part])], sem)
    for store in stores:
        store.wait()


def project(place, rows, count, width, gain, own, far, cost):
    blocks, depth = len(rows), rows[0].shape[1]
    total = blocks * count
    return pl.pallas_call(
        functools.partial(project_kernel, blocks, count),
        out_shape=[pltpu.HBM((total, width), jnp.bfloat16), pltpu.HBM((total, 2 * width), jnp.bfloat16)],
        in_specs=[SMEM] + [VMEM] * 5 + [HBM] * blocks,
        out_specs=[HBM, HBM],
        scratch_shapes=[
            pltpu.VMEM((total, depth), jnp.bfloat16),
            pltpu.VMEM((total, width), jnp.bfloat16),
            pltpu.VMEM((total, 2 * width), jnp.bfloat16),
            pltpu.SemaphoreType.DMA((blocks + 3,)),
        ],
        compiler_params=pltpu.CompilerParams(vmem_limit_bytes=16 * MIB),
        cost_estimate=pl.CostEstimate(flops=cost, bytes_accessed=1, transcendentals=0),
        name="project",
    )(place, gain, *own, *far, *rows)


def window_kernel(shape, groups, joined, place_ref, *refs):
    kinds = len(shape)
    queries, owns, sides = refs[:kinds], refs[kinds:2 * kinds], refs[2 * kinds:4 * kinds]
    sources = refs[4 * kinds:4 * kinds + joined]
    q_all, kv_all, vt_all, join_ref, join_held, sems = refs[4 * kinds + joined:]
    block, width = q_all.shape
    rows = block // sum(shape)
    core = place_ref[0]
    chip_base = jnp.where(core == 0, 2 * block, 0)
    link_base = jnp.where(core == 0, 0, 2 * block)
    pairs, step = [], 0
    for kind in range(kinds):
        for inside in range(shape[kind]):
            at = place_ref[4 + step] * rows
            part = pl.ds(inside * rows, rows)
            pairs.append((queries[kind].at[part, :], q_all.at[pl.ds(pl.multiple_of(at, 64), rows), :]))
            for source, base in (
                (owns[kind], block), (sides[kind], chip_base), (sides[kinds + kind], link_base)
            ):
                to = pl.ds(pl.multiple_of(base + at, 64), rows)
                pairs.append((source.at[part, :], kv_all.at[to, :]))
            step += 1
    loads = copy_all(pairs, sems)
    parts, at = [], 0
    for source in sources:
        parts.append((source, join_held.at[pl.ds(at, source.shape[0]), :]))
        at += source.shape[0]
    parts = copy_all(parts, sems.at[pl.ds(len(loads), joined)])
    for load in loads + parts:
        load.wait()
    stores = copy_all([(join_held, join_ref)], sems.at[pl.ds(len(loads) + joined, 1)])
    for index in range(3 * groups):
        for pair in range(width // LANES):
            columns = slice(width + pair * LANES, width + (pair + 1) * LANES)
            vt_all[pair, index] = kv_all[index * GROUP:(index + 1) * GROUP, columns].T
    for store in stores:
        store.wait()


def window(place, groups, rows, queries, owns, chip_side, link_side, joined):
    shape = [query.shape[0] // rows for query in queries]
    width, block = queries[0].shape[1], sum(shape) * rows
    pairs = width // LANES
    join_shape = (sum(value.shape[0] for value in joined), joined[0].shape[1])
    return pl.pallas_call(
        functools.partial(window_kernel, shape, groups, len(joined)),
        out_shape=(
            jax.ShapeDtypeStruct((block, width), jnp.bfloat16),
            jax.ShapeDtypeStruct((3 * block, 2 * width), jnp.bfloat16),
            jax.ShapeDtypeStruct((pairs, 3 * groups, LANES, GROUP), jnp.bfloat16),
            pltpu.HBM(join_shape, jnp.bfloat16),
        ),
        in_specs=[SMEM] + [HBM] * (4 * len(shape) + len(joined)),
        out_specs=(VMEM,) * 3 + (HBM,),
        scratch_shapes=[
            pltpu.VMEM(join_shape, jnp.bfloat16), pltpu.SemaphoreType.DMA((4 * sum(shape) + len(joined) + 1,))
        ],
        compiler_params=pltpu.CompilerParams(vmem_limit_bytes=16 * MIB),
        cost_estimate=pl.CostEstimate(flops=0, bytes_accessed=2 * 14 * block * width, transcendentals=0),
        name="window",
    )(place, *in_hbm(*queries, *owns), *chip_side, *link_side, *in_hbm(joined[0]), *joined[1:])


def weight_copies(share, place_ref, own_ref, far_ref, pieces_ref, theirs_ref, weight_ref):
    core, layer, seq = (place_ref[i] for i in range(3))
    layers, _, depth, columns = weight_ref.shape
    part = depth // share // 2
    half = columns // 2
    pairs = [(own_ref, weight_ref.at[layer, core])]
    for side in range(2):
        pairs.append((
            far_ref.at[pl.ds(side * depth, depth), pl.ds(far_ref.shape[1] - half, half)],
            weight_ref.at[layer, 1 - core, :, pl.ds(side * half, half)],
        ))
    for other in range(share):
        there = seq ^ other
        for source, holder in ((pieces_ref, core), (theirs_ref, 1 - core)):
            at = lax.rem(there // 2 * 2 + holder, share) * 2 * part
            for step in range(layers - 1):
                row = (other * (layers - 1) + step) * part
                for side in range(2):
                    to = pl.ds(pl.multiple_of(at + side * part, 16), part)
                    pairs.append((
                        source.at[pl.ds(row, part), pl.ds(side * columns, columns)],
                        weight_ref.at[place_ref[3 + step], lax.rem(there, 2), to, :],
                    ))
    return pairs


def attend_kernel(groups, reach, count_rows, share, place_ref, band_ref, turn_ref, q_all, kv_all, vt_all, *refs):
    loads = []
    if share:
        sources, refs = refs[:5], refs[5:]
        weight, load_sems, refs = refs[-7], refs[-1], refs[:-7] + refs[-6:-1]
        loads = copy_all(weight_copies(share, *sources, weight), load_sems)
    outs, (score, ctx, chosen, limits, sems) = refs[:-5], refs[-5:]
    pairs, rows = vt_all.shape[0], outs[0].shape[0]
    first_group, total, length = (place_ref[i] for i in range(1, 4))
    first_row = turn_ref[0]
    slots = 2 * reach + 2
    half_mask = lax.broadcasted_iota(jnp.int32, (GROUP, LANES), 1) < HD
    row_ids = lax.broadcasted_iota(jnp.int32, (GROUP, 2 * GROUP), 0)
    part_group = lax.div(length, jnp.int32(GROUP))
    part_left = lax.rem(length, jnp.int32(GROUP))

    def one_group(place, carry):
        group = first_row // GROUP + place
        for slot in range(slots):
            chosen[slot] = groups + group
        offset = part_group - first_group - group
        column = jnp.clip(jnp.where(offset < 0, offset + reach, offset + reach - 1), 0, 2 * reach - 1)
        cut = (part_left > 0) & (offset != 0) & (jnp.abs(offset) <= reach) & (part_group < total)
        cut = cut & (band_ref[group, column] == 1)
        chosen[1] = jnp.where(cut, groups + group + offset, groups + group)
        limits[0] = jnp.where(cut, part_left, 0)
        count = 1 + cut.astype(jnp.int32)
        for column in range(2 * reach):
            offset = column - reach if column < reach else column - reach + 1
            there = first_group + group + offset
            good = (there >= 0) & (there < part_group) & (there < total) & (band_ref[group, column] == 1)
            chosen[count] = jnp.where(good, groups + group + offset, groups + group)
            limits[0] = jnp.where(good & (count == 1), GROUP, limits[0])
            count = count + good.astype(jnp.int32)
        query_at = pl.ds(pl.multiple_of(group * GROUP, GROUP), GROUP)
        out_at = pl.ds(pl.multiple_of(place * GROUP, GROUP), GROUP)

        def run(size):
            first_limit = limits[0]
            last_limit = jnp.where(count == size, GROUP, 0)
            indices = [chosen[slot] for slot in range(size)]
            best = []
            for pair in range(pairs):
                own = q_all[query_at, pair * LANES:(pair + 1) * LANES]
                zero = jnp.zeros_like(own)
                both = jnp.concatenate(
                    [jnp.where(half_mask, own, zero), jnp.where(half_mask, zero, own)], axis=0
                ).T
                top = None
                for slot in range(0, size, 2):
                    tiles = [
                        kv_all[pl.ds(pl.multiple_of(index * GROUP, GROUP), GROUP), pair * LANES:(pair + 1) * LANES]
                        for index in indices[slot:slot + 2]
                    ]
                    got = jnp.dot(jnp.concatenate(tiles, axis=0), both, preferred_element_type=jnp.float32)
                    for one in (slot, slot + 1):
                        part = got[(one - slot) * GROUP:(one - slot + 1) * GROUP]
                        if one == 1:
                            part = jnp.where(row_ids < first_limit, part, -jnp.inf)
                        elif one == size - 1:
                            part = jnp.where(row_ids < last_limit, part, -jnp.inf)
                        score[pair, one * GROUP:(one + 1) * GROUP, :] = part
                        high = jnp.max(part.reshape(GROUP // 8, 8, 2 * GROUP), axis=0)
                        top = high if top is None else jnp.maximum(top, high)
                best.append(jnp.max(top, axis=0, keepdims=True))
            for pair in range(pairs):
                total_sum = jnp.zeros((8, 2 * GROUP), jnp.float32)
                mixed = jnp.zeros((LANES, 2 * GROUP), jnp.float32)
                for slot in range(0, size, 2):
                    weights = jnp.exp(score[pair, slot * GROUP:(slot + 2) * GROUP, :] - best[pair])
                    total_sum += jnp.sum(weights.reshape(2 * GROUP // 8, 8, 2 * GROUP), axis=0)
                    tiles = [vt_all[pair, index] for index in indices[slot:slot + 2]]
                    mixed += jnp.dot(
                        jnp.concatenate(tiles, axis=1),
                        weights.astype(jnp.bfloat16),
                        preferred_element_type=jnp.float32,
                    )
                mixed = mixed / jnp.sum(total_sum, axis=0, keepdims=True)
                both_heads = jnp.concatenate([mixed[:HD, :GROUP], mixed[HD:, GROUP:]], axis=0)
                ctx[out_at, pair * LANES:(pair + 1) * LANES] = both_heads.T.astype(jnp.bfloat16)

        for size in range(2, slots + 1, 2):
            @pl.when((count == size) | (count == size - 1))
            def _():
                run(size)

        return carry

    lax.fori_loop(0, count_rows // GROUP, one_group, 0)
    stores = copy_all(
        [(ctx.at[pl.ds(pl.multiple_of(turn_ref[1 + i], 64), rows), :], out) for i, out in enumerate(outs)], sems
    )
    for copy in stores + loads:
        copy.wait()


def attend(place, band, turn, outs, q_all, kv_all, vt_all, share=0, layers=0, parts=()):
    groups, reach = band.shape[0], band.shape[1] // 2
    pairs, block = vt_all.shape[0], q_all.shape[0]
    rows = block // (2 * outs)
    slots = 2 * reach + 2
    out_shape = [pltpu.HBM((rows, pairs * LANES), jnp.bfloat16)] * outs
    scratch = [
        pltpu.VMEM((pairs, slots * GROUP, 2 * GROUP), jnp.float32),
        pltpu.VMEM((block // 2, pairs * LANES), jnp.bfloat16),
        pltpu.SMEM((slots + 2,), jnp.int32),
        pltpu.SMEM((1,), jnp.int32),
        pltpu.SemaphoreType.DMA((outs,)),
    ]
    if parts:
        depth, columns = parts[1].shape
        out_shape.append(jax.ShapeDtypeStruct((layers, 2, depth, columns), jnp.bfloat16))
        scratch.append(pltpu.SemaphoreType.DMA((3 + 4 * share * (layers - 1),)))
        parts = [parts[0], *in_hbm(parts[1]), parts[2], *in_hbm(parts[3]), parts[4]]
    return pl.pallas_call(
        functools.partial(attend_kernel, groups, reach, block // 2, share),
        out_shape=out_shape,
        in_specs=[SMEM, SMEM, SMEM] + [VMEM] * 3 + ([SMEM] + [HBM] * 4 if parts else []),
        out_specs=[HBM] * outs + ([VMEM] if parts else []),
        scratch_shapes=scratch,
        compiler_params=pltpu.CompilerParams(vmem_limit_bytes=16 * MIB),
        cost_estimate=pl.CostEstimate(flops=1 << 34, bytes_accessed=1 << 20, transcendentals=0),
        name="attend",
    )(place, band, turn, q_all, kv_all, vt_all, *parts)


def output_kernel(layers, place_ref, weight, *refs):
    contexts, out_ref = refs[:layers], refs[layers]
    columns = weight.shape[3]
    for side in range(2):
        total = None
        for step in range(layers):
            got = jnp.dot(contexts[step][...], weight[place_ref[step], side], preferred_element_type=jnp.float32)
            total = got if step == 0 else total + got
        out_ref[0, :, side * columns:(side + 1) * columns] = total.astype(jnp.bfloat16)


def output(place, weight, contexts):
    layers, _, depth, columns = weight.shape
    rows = contexts[0].shape[0]
    return pl.pallas_call(
        functools.partial(output_kernel, layers),
        out_shape=jax.ShapeDtypeStruct((1, rows, 2 * columns), jnp.bfloat16),
        in_specs=[SMEM] + [VMEM] * (1 + layers),
        out_specs=VMEM,
        compiler_params=pltpu.CompilerParams(vmem_limit_bytes=8 * MIB),
        cost_estimate=LIGHT,
        name="output",
    )(place, weight, *contexts)


def hold_kernel(*refs):
    del refs


def hold(values, cost=1 << 34):
    return pl.pallas_call(
        hold_kernel,
        out_shape=[jax.ShapeDtypeStruct(value.shape, value.dtype) for value in values],
        in_specs=[HBM] * len(values),
        out_specs=[HBM] * len(values),
        input_output_aliases={i: i for i in range(len(values))},
        compiler_params=pltpu.CompilerParams(vmem_limit_bytes=MIB),
        cost_estimate=pl.CostEstimate(flops=cost, bytes_accessed=1, transcendentals=0),
        name="hold",
    )(*values)


def together(*values):
    return lax.optimization_barrier(values)


def numbers(*values):
    return jnp.stack([jnp.asarray(value, jnp.int32) for value in values])


def local(frames, norm_gain, w_query, w_key, w_value, w_out, group_band, lengths):
    cores, seqs, layers = lax.axis_size("dp"), lax.axis_size("seq"), lax.axis_size("head")
    core, seq, layer = lax.axis_index("dp"), lax.axis_index("seq"), lax.axis_index("head")
    groups = group_band.shape[1]
    width = w_query.shape[1]
    here = [(c, s) for c in range(cores) for s in range(seqs)]

    def home(c, s):
        return s % 2, s // 2 * 2 + c

    def flat(c, s, z=None):
        return c * seqs + s if z is None else (c * seqs + s) * layers + z

    def moved(value, shift):
        pairs = [(flat(c, s, z), flat(*home(c, s), shift(z))) for c, s in here for z in range(layers)]
        return lax.ppermute(value, ("dp", "seq", "head"), pairs)

    after = ring_successors(layers)
    before = {after[z]: z for z in after}
    swap = [(c, cores - 1 - c) for c in range(cores)]
    over_link = [(flat(1, s), flat(0, s + 2)) for s in range(seqs - 2)]
    over_link += [(flat(0, s + 2), flat(1, s)) for s in range(seqs - 2)]
    share = 4

    def shared(value, behind):
        near = [lax.ppermute(value, "seq", [(s, s ^ step) for s in range(seqs)]) for step in (1, 2)]
        *near, _ = together(*near, behind)
        return [value] + near + [lax.ppermute(near[1], "seq", [(s, s ^ 1) for s in range(seqs)])]

    rows = frames[0]
    count = rows.shape[0]
    gain = norm_gain[None, :]

    def halos(pair):
        return lax.ppermute(pair, ("dp", "seq"), over_link), lax.ppermute(pair, "dp", swap)

    def ringed(value):
        return lax.ppermute(value, "head", [(z, after[z]) for z in range(layers)])

    sent, piece = pack(numbers(lax.rem(seq, share)), rows, w_out, share)
    piece = moved(piece, lambda z: before[z])
    first = moved(sent, lambda z: after[z])
    second = ringed(first)
    own = bundle(w_query, w_key, w_value, w_out)
    whole = moved(rows, lambda z: z)
    facts = jnp.concatenate([group_band[0], jnp.broadcast_to(lengths[:, None], (1, group_band.shape[2]))], axis=0)
    facts = lax.ppermute(facts, ("dp", "seq"), [(flat(c, s), flat(*home(c, s))) for c, s in here])
    *own, facts = together(*own, facts)
    far = [lax.ppermute(value, "dp", swap) for value in own]
    back = {z: before[z] for z in range(layers)}
    ids = [layer, lookup([back[z] for z in range(layers)], layer)]
    ids.append(lookup([back[back[z]] for z in range(layers)], layer))
    ids.append(lookup([after[z] for z in range(layers)], layer))
    place = numbers(core, (seq // 2 * 2 + core) * groups, groups * seqs, facts[groups, 0], *ids)
    band = facts[:groups]
    piece, = hold([piece], 1 << 33)
    half = layers // 2
    sides = (1 - layer // half, layer // half)
    turns = [
        numbers(side * half * count, *[lax.rem(layer + e, half) * count for e in range(half)]) for side in sides
    ]
    weight_place = numbers(core, layer, seq, ids[1], ids[2], ids[3])
    sources = numbers(*[side * half + lax.rem(layer + half - e, half) for side in sides for e in range(half)])
    core_at = numbers(core)
    whole, place, band, piece, weight_place, sources, core_at, *turns = together(
        whole, place, band, piece, weight_place, sources, core_at, *turns
    )

    query_a, pair_a = project(core_at, [whole, first], count, width, gain, own, far, 1)
    link_a, chip_a = halos(pair_a)
    second, link_a, chip_a = together(second, link_a, chip_a)
    third = ringed(second[:count])
    query_b, pair_b = project(core_at, [second], count, width, gain, own, far, 1)
    shares = shared(join(count, first, second, piece), query_b)
    link_b, chip_b = halos(pair_b)
    third, link_b, chip_b = together(third, link_b, chip_b)
    query_c, pair_c = project(core_at, [third], count, width, gain, own, far, 1 << 32)
    link_c, chip_c = halos(pair_c)
    q_all, kv_all, vt_all, mine = window(
        place, groups, count, [query_a, query_b, query_c], [pair_a, pair_b, pair_c],
        [chip_a, chip_b, chip_c], [link_a, link_b, link_c], shares,
    )
    theirs = lax.ppermute(mine, "dp", swap)

    contexts, arrived = [], []
    for near in (0, 1):
        if near:
            *got, weight = attend(
                place, band, turns[near], half, q_all, kv_all, vt_all, share, layers,
                [weight_place, w_out, far[1], mine, theirs],
            )
        else:
            got = list(attend(place, band, turns[near], half, q_all, kv_all, vt_all))
            got[0], q_all = together(got[0], q_all)
        contexts += got
    *contexts[1:half], contexts[half] = together(*contexts[1:half], contexts[half])
    for index, context in enumerate(contexts):
        near, e = divmod(index, half)

        def target(z, near=near, e=e):
            return (z // half if near else 1 - z // half) * half + (z + e) % half

        arrived.append(moved(context, target))
    arrived = list(hold(arrived[:1])) + arrived[1:]
    return output(sources, weight, arrived)


def solution(mesh):
    return jax.shard_map(
        local,
        mesh=mesh,
        in_specs=(
            P("dp", ("seq", "head"), None),
            P(),
            P("dp", "head"),
            P("dp", "head"),
            P("dp", "head"),
            P("head", "dp"),
            P("dp", "seq", None),
            P("dp"),
        ),
        out_specs=P("dp", ("seq", "head"), None),
        check_vma=False,
    )
```

```python
import functools

import jax
import jax.numpy as jnp
from jax import lax
from jax.experimental import pallas as pl
from jax.experimental.pallas import tpu as pltpu
from jax.sharding import PartitionSpec as P

HD = 64
GROUP = 128
LANES = 128

epsilon = 1e-05

VMEM = pl.BlockSpec(memory_space=pltpu.VMEM)
SMEM = pl.BlockSpec(memory_space=pltpu.SMEM)
HBM = pl.BlockSpec(memory_space=pltpu.HBM)
MIB = 1024 * 1024
LIGHT = pl.CostEstimate(flops=1, bytes_accessed=1, transcendentals=0)


def ring_successors(count):
    order = [0] + list(range(1, count, 2)) + list(range(count - 2 + count % 2, 0, -2))
    return {order[i]: order[(i + 1) % count] for i in range(count)}


def lookup(table, index):
    value = jnp.int32(table[0])
    for place in range(1, len(table)):
        value = jnp.where(index == place, jnp.int32(table[place]), value)
    return value


def copy_all(pairs, sems):
    copies = [pltpu.make_async_copy(source, target, sems.at[i]) for i, (source, target) in enumerate(pairs)]
    for copy in copies:
        copy.start()
    return copies


def in_hbm(*values):
    return [pltpu.with_memory_space_constraint(value, pltpu.HBM) for value in values]


def run_copies(loads, stores, sems):
    for copy in copy_all(loads, sems):
        copy.wait()
    for copy in copy_all(stores, sems):
        copy.wait()


def pack_kernel(place_ref, rows_ref, w_out_ref, sent_ref, piece_ref, held, held_piece, sems):
    count = rows_ref.shape[0]
    part, columns = piece_ref.shape
    first = pl.multiple_of(place_ref[0] * part, 16)
    loads = [(w_out_ref.at[pl.ds(first, part), :], held_piece), (rows_ref, held.at[pl.ds(0, count), :])]
    for side in range(2):
        loads.append((
            w_out_ref.at[pl.ds(first + side * (part // 2), part // 2), :],
            held.at[pl.ds(count, part // 2), pl.ds(side * columns, columns)],
        ))
    run_copies(loads, [(held, sent_ref), (held_piece, piece_ref)], sems)


def pack(place, rows, w_out, share):
    part = w_out.shape[0] // share
    shapes = [(rows.shape[0] + part // 2, rows.shape[1]), (part, w_out.shape[1])]
    return pl.pallas_call(
        pack_kernel,
        out_shape=[pltpu.HBM(shape, jnp.bfloat16) for shape in shapes],
        in_specs=[SMEM] + [HBM] * 2,
        out_specs=[HBM] * 2,
        scratch_shapes=[pltpu.VMEM(shape, jnp.bfloat16) for shape in shapes] + [pltpu.SemaphoreType.DMA((4,))],
        compiler_params=pltpu.CompilerParams(vmem_limit_bytes=4 * MIB),
        cost_estimate=LIGHT,
        name="pack",
    )(place, *in_hbm(rows, w_out))


def bundle_kernel(query_ref, key_ref, value_ref, w_out_ref, front_ref, back_ref, sems):
    width, rows = query_ref.shape[1], w_out_ref.shape[0]
    loads = [
        (query_ref, front_ref.at[:, pl.ds(0, width)]),
        (key_ref, front_ref.at[:, pl.ds(width, width)]),
        (value_ref, back_ref.at[:, pl.ds(0, width)]),
    ]
    for side in range(2):
        loads.append((
            w_out_ref.at[:, pl.ds(side * width, width)],
            back_ref.at[pl.ds(side * rows, rows), pl.ds(width, width)],
        ))
    for load in copy_all(loads, sems):
        load.wait()


def bundle(w_query, w_key, w_value, w_out):
    shape = (w_query.shape[0], 2 * w_query.shape[1])
    return pl.pallas_call(
        bundle_kernel,
        out_shape=[jax.ShapeDtypeStruct(shape, jnp.bfloat16)] * 2,
        in_specs=[HBM] * 4,
        out_specs=[VMEM] * 2,
        scratch_shapes=[pltpu.SemaphoreType.DMA((5,))],
        compiler_params=pltpu.CompilerParams(vmem_limit_bytes=4 * MIB),
        cost_estimate=LIGHT,
        name="bundle",
    )(*in_hbm(w_query, w_key, w_value, w_out))


def join_kernel(count, first_ref, second_ref, piece_ref, out_ref, held, sems):
    part, columns = piece_ref.shape[0] // 2, piece_ref.shape[1]
    loads = [
        (source.at[pl.ds(count, part), :], held.at[pl.ds(place * part, part), :])
        for place, source in enumerate((first_ref, second_ref))
    ]
    for side in range(2):
        loads.append((
            piece_ref.at[pl.ds(side * part, part), :],
            held.at[pl.ds(2 * part, part), pl.ds(side * columns, columns)],
        ))
    run_copies(loads, [(held, out_ref)], sems)


def join(count, first, second, piece):
    shape = (3 * piece.shape[0] // 2, first.shape[1])
    return pl.pallas_call(
        functools.partial(join_kernel, count),
        out_shape=pltpu.HBM(shape, jnp.bfloat16),
        in_specs=[HBM] * 3,
        out_specs=HBM,
        scratch_shapes=[pltpu.VMEM(shape, jnp.bfloat16), pltpu.SemaphoreType.DMA((4,))],
        compiler_params=pltpu.CompilerParams(vmem_limit_bytes=4 * MIB),
        cost_estimate=LIGHT,
        name="join",
    )(first, second, piece)


def project_kernel(blocks, count, place_ref, gain_ref, own_front, own_back, far_front, far_back, *refs):
    rows = refs[:blocks]
    query_ref, pair_ref, held, query_held, pair_held, sems = refs[blocks:]
    depth, width = own_front.shape[0], query_ref.shape[1]
    first = place_ref[0] == 0
    loads = copy_all(
        [(rows[i].at[pl.ds(0, count), :], held.at[pl.ds(i * count, count), :]) for i in range(blocks)], sems
    )
    gain = gain_ref[...]
    mine, theirs = [], []
    for i in range(blocks):
        loads[i].wait()
        values = held[i * count:(i + 1) * count, :].astype(jnp.float32)
        center = values - jnp.mean(values, axis=-1, keepdims=True)
        spread = jnp.mean(center * center, axis=-1, keepdims=True)
        normalized = (center * lax.rsqrt(spread + epsilon) * gain).astype(jnp.bfloat16)
        low, high = normalized[:, :depth], normalized[:, depth:]
        mine.append(jnp.where(first, low, high))
        theirs.append(jnp.where(first, high, low))
    mine = mine[0] if blocks == 1 else jnp.concatenate(mine, axis=0)
    theirs = theirs[0] if blocks == 1 else jnp.concatenate(theirs, axis=0)
    stores = []
    for place in (1, 2, 0):
        own, far = ((own_front, far_front), (own_back, far_back))[place // 2]
        columns = slice(place % 2 * width, (place % 2 + 1) * width)
        got = jnp.dot(mine, own[:, columns], preferred_element_type=jnp.float32)
        got = (got + jnp.dot(theirs, far[:, columns], preferred_element_type=jnp.float32)).astype(jnp.bfloat16)
        sem = sems.at[pl.ds(blocks + place, 1)]
        if place == 0:
            query_held[...] = (got.astype(jnp.float32) * (HD ** -0.5)).astype(jnp.bfloat16)
            stores += copy_all([(query_held, query_ref)], sem)
        else:
            part = pl.ds((place - 1) * width, width)
            pair_held[:, (place - 1) * width:place * width] = got
            stores += copy_all([(pair_held.at[:, part], pair_ref.at[:, part])], sem)
    for store in stores:
        store.wait()


def project(place, rows, count, width, gain, own, far, cost):
    blocks, depth = len(rows), rows[0].shape[1]
    total = blocks * count
    return pl.pallas_call(
        functools.partial(project_kernel, blocks, count),
        out_shape=[pltpu.HBM((total, width), jnp.bfloat16), pltpu.HBM((total, 2 * width), jnp.bfloat16)],
        in_specs=[SMEM] + [VMEM] * 5 + [HBM] * blocks,
        out_specs=[HBM, HBM],
        scratch_shapes=[
            pltpu.VMEM((total, depth), jnp.bfloat16),
            pltpu.VMEM((total, width), jnp.bfloat16),
            pltpu.VMEM((total, 2 * width), jnp.bfloat16),
            pltpu.SemaphoreType.DMA((blocks + 3,)),
        ],
        compiler_params=pltpu.CompilerParams(vmem_limit_bytes=16 * MIB),
        cost_estimate=pl.CostEstimate(flops=cost, bytes_accessed=1, transcendentals=0),
        name="project",
    )(place, gain, *own, *far, *rows)


def window_kernel(shape, groups, joined, place_ref, *refs):
    kinds = len(shape)
    queries, owns, sides = refs[:kinds], refs[kinds:2 * kinds], refs[2 * kinds:4 * kinds]
    sources = refs[4 * kinds:4 * kinds + joined]
    q_all, kv_all, vt_all, join_ref, join_held, sems = refs[4 * kinds + joined:]
    block, width = q_all.shape
    rows = block // sum(shape)
    core = place_ref[0]
    chip_base = jnp.where(core == 0, 2 * block, 0)
    link_base = jnp.where(core == 0, 0, 2 * block)
    pairs, step = [], 0
    for kind in range(kinds):
        for inside in range(shape[kind]):
            at = place_ref[4 + step] * rows
            part = pl.ds(inside * rows, rows)
            pairs.append((queries[kind].at[part, :], q_all.at[pl.ds(pl.multiple_of(at, 64), rows), :]))
            for source, base in (
                (owns[kind], block), (sides[kind], chip_base), (sides[kinds + kind], link_base)
            ):
                to = pl.ds(pl.multiple_of(base + at, 64), rows)
                pairs.append((source.at[part, :], kv_all.at[to, :]))
            step += 1
    loads = copy_all(pairs, sems)
    parts, at = [], 0
    for source in sources:
        parts.append((source, join_held.at[pl.ds(at, source.shape[0]), :]))
        at += source.shape[0]
    parts = copy_all(parts, sems.at[pl.ds(len(loads), joined)])
    for load in loads + parts:
        load.wait()
    stores = copy_all([(join_held, join_ref)], sems.at[pl.ds(len(loads) + joined, 1)])
    for index in range(3 * groups):
        for pair in range(width // LANES):
            columns = slice(width + pair * LANES, width + (pair + 1) * LANES)
            vt_all[pair, index] = kv_all[index * GROUP:(index + 1) * GROUP, columns].T
    for store in stores:
        store.wait()


def window(place, groups, rows, queries, owns, chip_side, link_side, joined):
    shape = [query.shape[0] // rows for query in queries]
    width, block = queries[0].shape[1], sum(shape) * rows
    pairs = width // LANES
    join_shape = (sum(value.shape[0] for value in joined), joined[0].shape[1])
    return pl.pallas_call(
        functools.partial(window_kernel, shape, groups, len(joined)),
        out_shape=(
            jax.ShapeDtypeStruct((block, width), jnp.bfloat16),
            jax.ShapeDtypeStruct((3 * block, 2 * width), jnp.bfloat16),
            jax.ShapeDtypeStruct((pairs, 3 * groups, LANES, GROUP), jnp.bfloat16),
            pltpu.HBM(join_shape, jnp.bfloat16),
        ),
        in_specs=[SMEM] + [HBM] * (4 * len(shape) + len(joined)),
        out_specs=(VMEM,) * 3 + (HBM,),
        scratch_shapes=[
            pltpu.VMEM(join_shape, jnp.bfloat16), pltpu.SemaphoreType.DMA((4 * sum(shape) + len(joined) + 1,))
        ],
        compiler_params=pltpu.CompilerParams(vmem_limit_bytes=16 * MIB),
        cost_estimate=pl.CostEstimate(flops=0, bytes_accessed=2 * 14 * block * width, transcendentals=0),
        name="window",
    )(place, *in_hbm(*queries, *owns), *chip_side, *link_side, *in_hbm(joined[0]), *joined[1:])


def weight_copies(share, place_ref, own_ref, far_ref, pieces_ref, theirs_ref, weight_ref):
    core, layer, seq = (place_ref[i] for i in range(3))
    layers, _, depth, columns = weight_ref.shape
    part = depth // share // 2
    half = columns // 2
    pairs = [(own_ref, weight_ref.at[layer, core])]
    for side in range(2):
        pairs.append((
            far_ref.at[pl.ds(side * depth, depth), pl.ds(far_ref.shape[1] - half, half)],
            weight_ref.at[layer, 1 - core, :, pl.ds(side * half, half)],
        ))
    for other in range(share):
        there = seq ^ other
        for source, holder in ((pieces_ref, core), (theirs_ref, 1 - core)):
            at = lax.rem(there // 2 * 2 + holder, share) * 2 * part
            for step in range(layers - 1):
                row = (other * (layers - 1) + step) * part
                for side in range(2):
                    to = pl.ds(pl.multiple_of(at + side * part, 16), part)
                    pairs.append((
                        source.at[pl.ds(row, part), pl.ds(side * columns, columns)],
                        weight_ref.at[place_ref[3 + step], lax.rem(there, 2), to, :],
                    ))
    return pairs


def attend_kernel(groups, reach, count_rows, share, place_ref, band_ref, turn_ref, q_all, kv_all, vt_all, *refs):
    loads = []
    if share:
        sources, refs = refs[:5], refs[5:]
        weight, load_sems, refs = refs[-7], refs[-1], refs[:-7] + refs[-6:-1]
        loads = copy_all(weight_copies(share, *sources, weight), load_sems)
    outs, (score, ctx, chosen, limits, sems) = refs[:-5], refs[-5:]
    pairs, rows = vt_all.shape[0], outs[0].shape[0]
    first_group, total, length = (place_ref[i] for i in range(1, 4))
    first_row = turn_ref[0]
    slots = 2 * reach + 2
    half_mask = lax.broadcasted_iota(jnp.int32, (GROUP, LANES), 1) < HD
    row_ids = lax.broadcasted_iota(jnp.int32, (GROUP, 2 * GROUP), 0)
    part_group = lax.div(length, jnp.int32(GROUP))
    part_left = lax.rem(length, jnp.int32(GROUP))

    def one_group(place, carry):
        group = first_row // GROUP + place
        for slot in range(slots):
            chosen[slot] = groups + group
        offset = part_group - first_group - group
        column = jnp.clip(jnp.where(offset < 0, offset + reach, offset + reach - 1), 0, 2 * reach - 1)
        cut = (part_left > 0) & (offset != 0) & (jnp.abs(offset) <= reach) & (part_group < total)
        cut = cut & (band_ref[group, column] == 1)
        chosen[1] = jnp.where(cut, groups + group + offset, groups + group)
        limits[0] = jnp.where(cut, part_left, 0)
        count = 1 + cut.astype(jnp.int32)
        for column in range(2 * reach):
            offset = column - reach if column < reach else column - reach + 1
            there = first_group + group + offset
            good = (there >= 0) & (there < part_group) & (there < total) & (band_ref[group, column] == 1)
            chosen[count] = jnp.where(good, groups + group + offset, groups + group)
            limits[0] = jnp.where(good & (count == 1), GROUP, limits[0])
            count = count + good.astype(jnp.int32)
        query_at = pl.ds(pl.multiple_of(group * GROUP, GROUP), GROUP)
        out_at = pl.ds(pl.multiple_of(place * GROUP, GROUP), GROUP)

        def run(size):
            first_limit = limits[0]
            last_limit = jnp.where(count == size, GROUP, 0)
            indices = [chosen[slot] for slot in range(size)]
            best = []
            for pair in range(pairs):
                own = q_all[query_at, pair * LANES:(pair + 1) * LANES]
                zero = jnp.zeros_like(own)
                both = jnp.concatenate(
                    [jnp.where(half_mask, own, zero), jnp.where(half_mask, zero, own)], axis=0
                ).T
                top = None
                for slot in range(0, size, 2):
                    tiles = [
                        kv_all[pl.ds(pl.multiple_of(index * GROUP, GROUP), GROUP), pair * LANES:(pair + 1) * LANES]
                        for index in indices[slot:slot + 2]
                    ]
                    got = jnp.dot(jnp.concatenate(tiles, axis=0), both, preferred_element_type=jnp.float32)
                    for one in (slot, slot + 1):
                        part = got[(one - slot) * GROUP:(one - slot + 1) * GROUP]
                        if one == 1:
                            part = jnp.where(row_ids < first_limit, part, -jnp.inf)
                        elif one == size - 1:
                            part = jnp.where(row_ids < last_limit, part, -jnp.inf)
                        score[pair, one * GROUP:(one + 1) * GROUP, :] = part
                        high = jnp.max(part.reshape(GROUP // 8, 8, 2 * GROUP), axis=0)
                        top = high if top is None else jnp.maximum(top, high)
                best.append(jnp.max(top, axis=0, keepdims=True))
            for pair in range(pairs):
                total_sum = jnp.zeros((8, 2 * GROUP), jnp.float32)
                mixed = jnp.zeros((LANES, 2 * GROUP), jnp.float32)
                for slot in range(0, size, 2):
                    weights = jnp.exp(score[pair, slot * GROUP:(slot + 2) * GROUP, :] - best[pair])
                    total_sum += jnp.sum(weights.reshape(2 * GROUP // 8, 8, 2 * GROUP), axis=0)
                    tiles = [vt_all[pair, index] for index in indices[slot:slot + 2]]
                    mixed += jnp.dot(
                        jnp.concatenate(tiles, axis=1),
                        weights.astype(jnp.bfloat16),
                        preferred_element_type=jnp.float32,
                    )
                mixed = mixed / jnp.sum(total_sum, axis=0, keepdims=True)
                both_heads = jnp.concatenate([mixed[:HD, :GROUP], mixed[HD:, GROUP:]], axis=0)
                ctx[out_at, pair * LANES:(pair + 1) * LANES] = both_heads.T.astype(jnp.bfloat16)

        for size in range(2, slots + 1, 2):
            @pl.when((count == size) | (count == size - 1))
            def _():
                run(size)

        return carry

    lax.fori_loop(0, count_rows // GROUP, one_group, 0)
    stores = copy_all(
        [(ctx.at[pl.ds(pl.multiple_of(turn_ref[1 + i], 64), rows), :], out) for i, out in enumerate(outs)], sems
    )
    for copy in stores + loads:
        copy.wait()


def attend(place, band, turn, outs, q_all, kv_all, vt_all, share=0, layers=0, parts=()):
    groups, reach = band.shape[0], band.shape[1] // 2
    pairs, block = vt_all.shape[0], q_all.shape[0]
    rows = block // (2 * outs)
    slots = 2 * reach + 2
    out_shape = [pltpu.HBM((rows, pairs * LANES), jnp.bfloat16)] * outs
    scratch = [
        pltpu.VMEM((pairs, slots * GROUP, 2 * GROUP), jnp.float32),
        pltpu.VMEM((block // 2, pairs * LANES), jnp.bfloat16),
        pltpu.SMEM((slots + 2,), jnp.int32),
        pltpu.SMEM((1,), jnp.int32),
        pltpu.SemaphoreType.DMA((outs,)),
    ]
    if parts:
        depth, columns = parts[1].shape
        out_shape.append(jax.ShapeDtypeStruct((layers, 2, depth, columns), jnp.bfloat16))
        scratch.append(pltpu.SemaphoreType.DMA((3 + 4 * share * (layers - 1),)))
        parts = [parts[0], *in_hbm(parts[1]), parts[2], *in_hbm(parts[3]), parts[4]]
    return pl.pallas_call(
        functools.partial(attend_kernel, groups, reach, block // 2, share),
        out_shape=out_shape,
        in_specs=[SMEM, SMEM, SMEM] + [VMEM] * 3 + ([SMEM] + [HBM] * 4 if parts else []),
        out_specs=[HBM] * outs + ([VMEM] if parts else []),
        scratch_shapes=scratch,
        compiler_params=pltpu.CompilerParams(vmem_limit_bytes=16 * MIB),
        cost_estimate=pl.CostEstimate(flops=1 << 34, bytes_accessed=1 << 20, transcendentals=0),
        name="attend",
    )(place, band, turn, q_all, kv_all, vt_all, *parts)


def output_kernel(layers, place_ref, weight, *refs):
    contexts, out_ref = refs[:layers], refs[layers]
    columns = weight.shape[3]
    for side in range(2):
        total = None
        for step in range(layers):
            got = jnp.dot(contexts[step][...], weight[place_ref[step], side], preferred_element_type=jnp.float32)
            total = got if step == 0 else total + got
        out_ref[0, :, side * columns:(side + 1) * columns] = total.astype(jnp.bfloat16)


def output(place, weight, contexts):
    layers, _, depth, columns = weight.shape
    rows = contexts[0].shape[0]
    return pl.pallas_call(
        functools.partial(output_kernel, layers),
        out_shape=jax.ShapeDtypeStruct((1, rows, 2 * columns), jnp.bfloat16),
        in_specs=[SMEM] + [VMEM] * (1 + layers),
        out_specs=VMEM,
        compiler_params=pltpu.CompilerParams(vmem_limit_bytes=8 * MIB),
        cost_estimate=LIGHT,
        name="output",
    )(place, weight, *contexts)


def hold_kernel(*refs):
    del refs


def hold(values, cost=1 << 34):
    return pl.pallas_call(
        hold_kernel,
        out_shape=[jax.ShapeDtypeStruct(value.shape, value.dtype) for value in values],
        in_specs=[HBM] * len(values),
        out_specs=[HBM] * len(values),
        input_output_aliases={i: i for i in range(len(values))},
        compiler_params=pltpu.CompilerParams(vmem_limit_bytes=MIB),
        cost_estimate=pl.CostEstimate(flops=cost, bytes_accessed=1, transcendentals=0),
        name="hold",
    )(*values)


def together(*values):
    return lax.optimization_barrier(values)


def numbers(*values):
    return jnp.stack([jnp.asarray(value, jnp.int32) for value in values])


def local(frames, norm_gain, w_query, w_key, w_value, w_out, group_band, lengths):
    cores, seqs, layers = lax.axis_size("dp"), lax.axis_size("seq"), lax.axis_size("head")
    core, seq, layer = lax.axis_index("dp"), lax.axis_index("seq"), lax.axis_index("head")
    groups = group_band.shape[1]
    width = w_query.shape[1]
    here = [(c, s) for c in range(cores) for s in range(seqs)]

    def home(c, s):
        return s % 2, s // 2 * 2 + c

    def flat(c, s, z=None):
        return c * seqs + s if z is None else (c * seqs + s) * layers + z

    def moved(value, shift):
        pairs = [(flat(c, s, z), flat(*home(c, s), shift(z))) for c, s in here for z in range(layers)]
        return lax.ppermute(value, ("dp", "seq", "head"), pairs)

    after = ring_successors(layers)
    before = {after[z]: z for z in after}
    swap = [(c, cores - 1 - c) for c in range(cores)]
    over_link = [(flat(1, s), flat(0, s + 2)) for s in range(seqs - 2)]
    over_link += [(flat(0, s + 2), flat(1, s)) for s in range(seqs - 2)]
    share = 4

    def shared(value, behind):
        near = [lax.ppermute(value, "seq", [(s, s ^ step) for s in range(seqs)]) for step in (1, 2)]
        *near, _ = together(*near, behind)
        return [value] + near + [lax.ppermute(near[1], "seq", [(s, s ^ 1) for s in range(seqs)])]

    rows = frames[0]
    count = rows.shape[0]
    gain = norm_gain[None, :]

    def halos(pair):
        return lax.ppermute(pair, ("dp", "seq"), over_link), lax.ppermute(pair, "dp", swap)

    def ringed(value):
        return lax.ppermute(value, "head", [(z, after[z]) for z in range(layers)])

    sent, piece = pack(numbers(lax.rem(seq, share)), rows, w_out, share)
    first = moved(sent, lambda z: after[z])
    second = ringed(first)
    own = bundle(w_query, w_key, w_value, w_out)
    whole = moved(rows, lambda z: z)
    facts = jnp.concatenate([group_band[0], jnp.broadcast_to(lengths[:, None], (1, group_band.shape[2]))], axis=0)
    facts = lax.ppermute(facts, ("dp", "seq"), [(flat(c, s), flat(*home(c, s))) for c, s in here])
    *own, facts = together(*own, facts)
    far = [lax.ppermute(value, "dp", swap) for value in own]
    back = {z: before[z] for z in range(layers)}
    ids = [layer, lookup([back[z] for z in range(layers)], layer)]
    ids.append(lookup([back[back[z]] for z in range(layers)], layer))
    ids.append(lookup([after[z] for z in range(layers)], layer))
    place = numbers(core, (seq // 2 * 2 + core) * groups, groups * seqs, facts[groups, 0], *ids)
    band = facts[:groups]
    whole, = hold([whole], 1 << 33)
    half = layers // 2
    sides = (1 - layer // half, layer // half)
    turns = [
        numbers(side * half * count, *[lax.rem(layer + e, half) * count for e in range(half)]) for side in sides
    ]
    weight_place = numbers(core, layer, seq, ids[1], ids[2], ids[3])
    sources = numbers(*[side * half + lax.rem(layer + half - e, half) for side in sides for e in range(half)])
    core_at = numbers(core)
    whole, place, band, weight_place, sources, core_at, *turns = together(
        whole, place, band, weight_place, sources, core_at, *turns
    )

    query_a, pair_a = project(core_at, [whole, first], count, width, gain, own, far, 1)
    link_a, chip_a = halos(pair_a)
    piece, pair_a = together(piece, pair_a)
    piece = moved(piece, lambda z: before[z])
    second, piece = together(second, piece)
    third = ringed(second[:count])
    piece, link_a, chip_a = together(piece, link_a, chip_a)
    query_b, pair_b = project(core_at, [second], count, width, gain, own, far, 1)
    shares = shared(join(count, first, second, piece), query_b)
    link_b, chip_b = halos(pair_b)
    third, link_b, chip_b = together(third, link_b, chip_b)
    query_c, pair_c = project(core_at, [third], count, width, gain, own, far, 1 << 30)
    link_c, chip_c = halos(pair_c)
    q_all, kv_all, vt_all, mine = window(
        place, groups, count, [query_a, query_b, query_c], [pair_a, pair_b, pair_c],
        [chip_a, chip_b, chip_c], [link_a, link_b, link_c], shares,
    )
    theirs = lax.ppermute(mine, "dp", swap)

    contexts, arrived = [], []
    for near in (0, 1):
        if near:
            *got, weight = attend(
                place, band, turns[near], half, q_all, kv_all, vt_all, share, layers,
                [weight_place, w_out, far[1], mine, theirs],
            )
        else:
            got = list(attend(place, band, turns[near], half, q_all, kv_all, vt_all))
            got[0], q_all = together(got[0], q_all)
        contexts += got
    *contexts[1:half], contexts[half] = together(*contexts[1:half], contexts[half])
    for index, context in enumerate(contexts):
        near, e = divmod(index, half)

        def target(z, near=near, e=e):
            return (z // half if near else 1 - z // half) * half + (z + e) % half

        arrived.append(moved(context, target))
    arrived = list(hold(arrived[:1])) + arrived[1:]
    return output(sources, weight, arrived)


def solution(mesh):
    return jax.shard_map(
        local,
        mesh=mesh,
        in_specs=(
            P("dp", ("seq", "head"), None),
            P(),
            P("dp", "head"),
            P("dp", "head"),
            P("dp", "head"),
            P("head", "dp"),
            P("dp", "seq", None),
            P("dp"),
        ),
        out_specs=P("dp", ("seq", "head"), None),
        check_vma=False,
    )
```

```python
import functools

import jax
import jax.numpy as jnp
from jax import lax
from jax.experimental import pallas as pl
from jax.experimental.pallas import tpu as pltpu
from jax.sharding import PartitionSpec as P

HD = 64
GROUP = 128
LANES = 128

epsilon = 1e-05

VMEM = pl.BlockSpec(memory_space=pltpu.VMEM)
SMEM = pl.BlockSpec(memory_space=pltpu.SMEM)
HBM = pl.BlockSpec(memory_space=pltpu.HBM)
MIB = 1024 * 1024
LIGHT = pl.CostEstimate(flops=1, bytes_accessed=1, transcendentals=0)


def ring_successors(count):
    order = [0] + list(range(1, count, 2)) + list(range(count - 2 + count % 2, 0, -2))
    return {order[i]: order[(i + 1) % count] for i in range(count)}


def lookup(table, index):
    value = jnp.int32(table[0])
    for place in range(1, len(table)):
        value = jnp.where(index == place, jnp.int32(table[place]), value)
    return value


def copy_all(pairs, sems):
    copies = [pltpu.make_async_copy(source, target, sems.at[i]) for i, (source, target) in enumerate(pairs)]
    for copy in copies:
        copy.start()
    return copies


def in_hbm(*values):
    return [pltpu.with_memory_space_constraint(value, pltpu.HBM) for value in values]


def run_copies(loads, stores, sems):
    for copy in copy_all(loads, sems):
        copy.wait()
    for copy in copy_all(stores, sems):
        copy.wait()


def pack_kernel(place_ref, rows_ref, w_out_ref, sent_ref, piece_ref, held, held_piece, sems):
    count = rows_ref.shape[0]
    part, columns = piece_ref.shape
    first = pl.multiple_of(place_ref[0] * part, 16)
    loads = [(w_out_ref.at[pl.ds(first, part), :], held_piece), (rows_ref, held.at[pl.ds(0, count), :])]
    for side in range(2):
        loads.append((
            w_out_ref.at[pl.ds(first + side * (part // 2), part // 2), :],
            held.at[pl.ds(count, part // 2), pl.ds(side * columns, columns)],
        ))
    run_copies(loads, [(held, sent_ref), (held_piece, piece_ref)], sems)


def pack(place, rows, w_out, share):
    part = w_out.shape[0] // share
    shapes = [(rows.shape[0] + part // 2, rows.shape[1]), (part, w_out.shape[1])]
    return pl.pallas_call(
        pack_kernel,
        out_shape=[pltpu.HBM(shape, jnp.bfloat16) for shape in shapes],
        in_specs=[SMEM] + [HBM] * 2,
        out_specs=[HBM] * 2,
        scratch_shapes=[pltpu.VMEM(shape, jnp.bfloat16) for shape in shapes] + [pltpu.SemaphoreType.DMA((4,))],
        compiler_params=pltpu.CompilerParams(vmem_limit_bytes=4 * MIB),
        cost_estimate=LIGHT,
        name="pack",
    )(place, *in_hbm(rows, w_out))


def bundle_kernel(query_ref, key_ref, value_ref, w_out_ref, front_ref, back_ref, sems):
    width, rows = query_ref.shape[1], w_out_ref.shape[0]
    loads = [
        (query_ref, front_ref.at[:, pl.ds(0, width)]),
        (key_ref, front_ref.at[:, pl.ds(width, width)]),
        (value_ref, back_ref.at[:, pl.ds(0, width)]),
    ]
    for side in range(2):
        loads.append((
            w_out_ref.at[:, pl.ds(side * width, width)],
            back_ref.at[pl.ds(side * rows, rows), pl.ds(width, width)],
        ))
    for load in copy_all(loads, sems):
        load.wait()


def bundle(w_query, w_key, w_value, w_out):
    shape = (w_query.shape[0], 2 * w_query.shape[1])
    return pl.pallas_call(
        bundle_kernel,
        out_shape=[jax.ShapeDtypeStruct(shape, jnp.bfloat16)] * 2,
        in_specs=[HBM] * 4,
        out_specs=[VMEM] * 2,
        scratch_shapes=[pltpu.SemaphoreType.DMA((5,))],
        compiler_params=pltpu.CompilerParams(vmem_limit_bytes=4 * MIB),
        cost_estimate=LIGHT,
        name="bundle",
    )(*in_hbm(w_query, w_key, w_value, w_out))


def join_kernel(count, first_ref, second_ref, piece_ref, out_ref, held, sems):
    part, columns = piece_ref.shape[0] // 2, piece_ref.shape[1]
    loads = [
        (source.at[pl.ds(count, part), :], held.at[pl.ds(place * part, part), :])
        for place, source in enumerate((first_ref, second_ref))
    ]
    for side in range(2):
        loads.append((
            piece_ref.at[pl.ds(side * part, part), :],
            held.at[pl.ds(2 * part, part), pl.ds(side * columns, columns)],
        ))
    run_copies(loads, [(held, out_ref)], sems)


def join(count, first, second, piece):
    shape = (3 * piece.shape[0] // 2, first.shape[1])
    return pl.pallas_call(
        functools.partial(join_kernel, count),
        out_shape=pltpu.HBM(shape, jnp.bfloat16),
        in_specs=[HBM] * 3,
        out_specs=HBM,
        scratch_shapes=[pltpu.VMEM(shape, jnp.bfloat16), pltpu.SemaphoreType.DMA((4,))],
        compiler_params=pltpu.CompilerParams(vmem_limit_bytes=4 * MIB),
        cost_estimate=LIGHT,
        name="join",
    )(first, second, piece)


def project_kernel(blocks, count, place_ref, gain_ref, own_front, own_back, far_front, far_back, *refs):
    rows = refs[:blocks]
    query_ref, pair_ref, held, query_held, pair_held, sems = refs[blocks:]
    depth, width = own_front.shape[0], query_ref.shape[1]
    first = place_ref[0] == 0
    loads = []
    if blocks > 1:
        loads = copy_all(
            [(rows[i].at[pl.ds(0, count), :], held.at[pl.ds(i * count, count), :]) for i in range(blocks)], sems
        )
    gain = gain_ref[...]
    mine, theirs = [], []
    for i in range(blocks):
        if blocks > 1:
            loads[i].wait()
            values = held[i * count:(i + 1) * count, :].astype(jnp.float32)
        else:
            values = rows[0][:count, :].astype(jnp.float32)
        center = values - jnp.mean(values, axis=-1, keepdims=True)
        spread = jnp.mean(center * center, axis=-1, keepdims=True)
        normalized = (center * lax.rsqrt(spread + epsilon) * gain).astype(jnp.bfloat16)
        low, high = normalized[:, :depth], normalized[:, depth:]
        mine.append(jnp.where(first, low, high))
        theirs.append(jnp.where(first, high, low))
    mine = mine[0] if blocks == 1 else jnp.concatenate(mine, axis=0)
    theirs = theirs[0] if blocks == 1 else jnp.concatenate(theirs, axis=0)
    stores = []
    for place in (1, 2, 0):
        own, far = ((own_front, far_front), (own_back, far_back))[place // 2]
        columns = slice(place % 2 * width, (place % 2 + 1) * width)
        got = jnp.dot(mine, own[:, columns], preferred_element_type=jnp.float32)
        got = (got + jnp.dot(theirs, far[:, columns], preferred_element_type=jnp.float32)).astype(jnp.bfloat16)
        sem = sems.at[pl.ds(blocks + place, 1)]
        if place == 0:
            query_held[...] = (got.astype(jnp.float32) * (HD ** -0.5)).astype(jnp.bfloat16)
            stores += copy_all([(query_held, query_ref)], sem)
        else:
            part = pl.ds((place - 1) * width, width)
            pair_held[:, (place - 1) * width:place * width] = got
            stores += copy_all([(pair_held.at[:, part], pair_ref.at[:, part])], sem)
    for store in stores:
        store.wait()


def project(place, rows, count, width, gain, own, far, cost):
    blocks, depth = len(rows), rows[0].shape[1]
    total = blocks * count
    return pl.pallas_call(
        functools.partial(project_kernel, blocks, count),
        out_shape=[pltpu.HBM((total, width), jnp.bfloat16), pltpu.HBM((total, 2 * width), jnp.bfloat16)],
        in_specs=[SMEM] + [VMEM] * 5 + ([HBM] * blocks if blocks > 1 else [VMEM]),
        out_specs=[HBM, HBM],
        scratch_shapes=[
            pltpu.VMEM((total, depth), jnp.bfloat16),
            pltpu.VMEM((total, width), jnp.bfloat16),
            pltpu.VMEM((total, 2 * width), jnp.bfloat16),
            pltpu.SemaphoreType.DMA((blocks + 3,)),
        ],
        compiler_params=pltpu.CompilerParams(vmem_limit_bytes=16 * MIB),
        cost_estimate=pl.CostEstimate(flops=cost, bytes_accessed=1, transcendentals=0),
        name="project",
    )(place, gain, *own, *far, *rows)


def window_kernel(shape, groups, joined, place_ref, *refs):
    kinds = len(shape)
    queries, owns, sides = refs[:kinds], refs[kinds:2 * kinds], refs[2 * kinds:4 * kinds]
    sources = refs[4 * kinds:4 * kinds + joined]
    q_all, kv_all, vt_all, join_ref, join_held, sems = refs[4 * kinds + joined:]
    block, width = q_all.shape
    rows = block // sum(shape)
    core = place_ref[0]
    chip_base = jnp.where(core == 0, 2 * block, 0)
    link_base = jnp.where(core == 0, 0, 2 * block)
    pairs, step = [], 0
    for kind in range(kinds):
        for inside in range(shape[kind]):
            at = place_ref[4 + step] * rows
            part = pl.ds(inside * rows, rows)
            pairs.append((queries[kind].at[part, :], q_all.at[pl.ds(pl.multiple_of(at, 64), rows), :]))
            for source, base in (
                (owns[kind], block), (sides[kind], chip_base), (sides[kinds + kind], link_base)
            ):
                to = pl.ds(pl.multiple_of(base + at, 64), rows)
                pairs.append((source.at[part, :], kv_all.at[to, :]))
            step += 1
    loads = copy_all(pairs, sems)
    parts, at = [], 0
    for source in sources:
        parts.append((source, join_held.at[pl.ds(at, source.shape[0]), :]))
        at += source.shape[0]
    parts = copy_all(parts, sems.at[pl.ds(len(loads), joined)])
    for load in loads + parts:
        load.wait()
    stores = copy_all([(join_held, join_ref)], sems.at[pl.ds(len(loads) + joined, 1)])
    for index in range(3 * groups):
        for pair in range(width // LANES):
            columns = slice(width + pair * LANES, width + (pair + 1) * LANES)
            vt_all[pair, index] = kv_all[index * GROUP:(index + 1) * GROUP, columns].T
    for store in stores:
        store.wait()


def window(place, groups, rows, queries, owns, chip_side, link_side, joined):
    shape = [query.shape[0] // rows for query in queries]
    width, block = queries[0].shape[1], sum(shape) * rows
    pairs = width // LANES
    join_shape = (sum(value.shape[0] for value in joined), joined[0].shape[1])
    return pl.pallas_call(
        functools.partial(window_kernel, shape, groups, len(joined)),
        out_shape=(
            jax.ShapeDtypeStruct((block, width), jnp.bfloat16),
            jax.ShapeDtypeStruct((3 * block, 2 * width), jnp.bfloat16),
            jax.ShapeDtypeStruct((pairs, 3 * groups, LANES, GROUP), jnp.bfloat16),
            pltpu.HBM(join_shape, jnp.bfloat16),
        ),
        in_specs=[SMEM] + [HBM] * (4 * len(shape) + len(joined)),
        out_specs=(VMEM,) * 3 + (HBM,),
        scratch_shapes=[
            pltpu.VMEM(join_shape, jnp.bfloat16), pltpu.SemaphoreType.DMA((4 * sum(shape) + len(joined) + 1,))
        ],
        compiler_params=pltpu.CompilerParams(vmem_limit_bytes=16 * MIB),
        cost_estimate=pl.CostEstimate(flops=0, bytes_accessed=2 * 14 * block * width, transcendentals=0),
        name="window",
    )(place, *in_hbm(*queries, *owns), *chip_side, *link_side, *in_hbm(joined[0]), *joined[1:])


def weight_copies(share, place_ref, own_ref, far_ref, pieces_ref, theirs_ref, weight_ref):
    core, layer, seq = (place_ref[i] for i in range(3))
    layers, _, depth, columns = weight_ref.shape
    part = depth // share // 2
    half = columns // 2
    pairs = [(own_ref, weight_ref.at[layer, core])]
    for side in range(2):
        pairs.append((
            far_ref.at[pl.ds(side * depth, depth), pl.ds(far_ref.shape[1] - half, half)],
            weight_ref.at[layer, 1 - core, :, pl.ds(side * half, half)],
        ))
    for other in range(share):
        there = seq ^ other
        for source, holder in ((pieces_ref, core), (theirs_ref, 1 - core)):
            at = lax.rem(there // 2 * 2 + holder, share) * 2 * part
            for step in range(layers - 1):
                row = (other * (layers - 1) + step) * part
                for side in range(2):
                    to = pl.ds(pl.multiple_of(at + side * part, 16), part)
                    pairs.append((
                        source.at[pl.ds(row, part), pl.ds(side * columns, columns)],
                        weight_ref.at[place_ref[3 + step], lax.rem(there, 2), to, :],
                    ))
    return pairs


def attend_kernel(groups, reach, count_rows, share, place_ref, band_ref, turn_ref, q_all, kv_all, vt_all, *refs):
    loads = []
    if share:
        sources, refs = refs[:5], refs[5:]
        weight, load_sems, refs = refs[-7], refs[-1], refs[:-7] + refs[-6:-1]
        loads = copy_all(weight_copies(share, *sources, weight), load_sems)
    outs, (score, ctx, chosen, limits, sems) = refs[:-5], refs[-5:]
    pairs, rows = vt_all.shape[0], outs[0].shape[0]
    first_group, total, length = (place_ref[i] for i in range(1, 4))
    first_row = turn_ref[0]
    slots = 2 * reach + 2
    half_mask = lax.broadcasted_iota(jnp.int32, (GROUP, LANES), 1) < HD
    row_ids = lax.broadcasted_iota(jnp.int32, (GROUP, 2 * GROUP), 0)
    part_group = lax.div(length, jnp.int32(GROUP))
    part_left = lax.rem(length, jnp.int32(GROUP))

    def one_group(place, carry):
        group = first_row // GROUP + place
        for slot in range(slots):
            chosen[slot] = groups + group
        offset = part_group - first_group - group
        column = jnp.clip(jnp.where(offset < 0, offset + reach, offset + reach - 1), 0, 2 * reach - 1)
        cut = (part_left > 0) & (offset != 0) & (jnp.abs(offset) <= reach) & (part_group < total)
        cut = cut & (band_ref[group, column] == 1)
        chosen[1] = jnp.where(cut, groups + group + offset, groups + group)
        limits[0] = jnp.where(cut, part_left, 0)
        count = 1 + cut.astype(jnp.int32)
        for column in range(2 * reach):
            offset = column - reach if column < reach else column - reach + 1
            there = first_group + group + offset
            good = (there >= 0) & (there < part_group) & (there < total) & (band_ref[group, column] == 1)
            chosen[count] = jnp.where(good, groups + group + offset, groups + group)
            limits[0] = jnp.where(good & (count == 1), GROUP, limits[0])
            count = count + good.astype(jnp.int32)
        query_at = pl.ds(pl.multiple_of(group * GROUP, GROUP), GROUP)
        out_at = pl.ds(pl.multiple_of(place * GROUP, GROUP), GROUP)

        def run(size):
            first_limit = limits[0]
            last_limit = jnp.where(count == size, GROUP, 0)
            indices = [chosen[slot] for slot in range(size)]
            best = []
            for pair in range(pairs):
                own = q_all[query_at, pair * LANES:(pair + 1) * LANES]
                zero = jnp.zeros_like(own)
                both = jnp.concatenate(
                    [jnp.where(half_mask, own, zero), jnp.where(half_mask, zero, own)], axis=0
                ).T
                top = None
                for slot in range(0, size, 2):
                    tiles = [
                        kv_all[pl.ds(pl.multiple_of(index * GROUP, GROUP), GROUP), pair * LANES:(pair + 1) * LANES]
                        for index in indices[slot:slot + 2]
                    ]
                    got = jnp.dot(jnp.concatenate(tiles, axis=0), both, preferred_element_type=jnp.float32)
                    for one in (slot, slot + 1):
                        part = got[(one - slot) * GROUP:(one - slot + 1) * GROUP]
                        if one == 1:
                            part = jnp.where(row_ids < first_limit, part, -jnp.inf)
                        elif one == size - 1:
                            part = jnp.where(row_ids < last_limit, part, -jnp.inf)
                        score[pair, one * GROUP:(one + 1) * GROUP, :] = part
                        high = jnp.max(part.reshape(GROUP // 8, 8, 2 * GROUP), axis=0)
                        top = high if top is None else jnp.maximum(top, high)
                best.append(jnp.max(top, axis=0, keepdims=True))
            for pair in range(pairs):
                total_sum = jnp.zeros((8, 2 * GROUP), jnp.float32)
                mixed = jnp.zeros((LANES, 2 * GROUP), jnp.float32)
                for slot in range(0, size, 2):
                    weights = jnp.exp(score[pair, slot * GROUP:(slot + 2) * GROUP, :] - best[pair])
                    total_sum += jnp.sum(weights.reshape(2 * GROUP // 8, 8, 2 * GROUP), axis=0)
                    tiles = [vt_all[pair, index] for index in indices[slot:slot + 2]]
                    mixed += jnp.dot(
                        jnp.concatenate(tiles, axis=1),
                        weights.astype(jnp.bfloat16),
                        preferred_element_type=jnp.float32,
                    )
                mixed = mixed / jnp.sum(total_sum, axis=0, keepdims=True)
                both_heads = jnp.concatenate([mixed[:HD, :GROUP], mixed[HD:, GROUP:]], axis=0)
                ctx[out_at, pair * LANES:(pair + 1) * LANES] = both_heads.T.astype(jnp.bfloat16)

        for size in range(2, slots + 1, 2):
            @pl.when((count == size) | (count == size - 1))
            def _():
                run(size)

        return carry

    lax.fori_loop(0, count_rows // GROUP, one_group, 0)
    stores = copy_all(
        [(ctx.at[pl.ds(pl.multiple_of(turn_ref[1 + i], 64), rows), :], out) for i, out in enumerate(outs)], sems
    )
    for copy in stores + loads:
        copy.wait()


def attend(place, band, turn, outs, q_all, kv_all, vt_all, share=0, layers=0, parts=()):
    groups, reach = band.shape[0], band.shape[1] // 2
    pairs, block = vt_all.shape[0], q_all.shape[0]
    rows = block // (2 * outs)
    slots = 2 * reach + 2
    out_shape = [pltpu.HBM((rows, pairs * LANES), jnp.bfloat16)] * outs
    scratch = [
        pltpu.VMEM((pairs, slots * GROUP, 2 * GROUP), jnp.float32),
        pltpu.VMEM((block // 2, pairs * LANES), jnp.bfloat16),
        pltpu.SMEM((slots + 2,), jnp.int32),
        pltpu.SMEM((1,), jnp.int32),
        pltpu.SemaphoreType.DMA((outs,)),
    ]
    if parts:
        depth, columns = parts[1].shape
        out_shape.append(jax.ShapeDtypeStruct((layers, 2, depth, columns), jnp.bfloat16))
        scratch.append(pltpu.SemaphoreType.DMA((3 + 4 * share * (layers - 1),)))
        parts = [parts[0], *in_hbm(parts[1]), parts[2], *in_hbm(parts[3]), parts[4]]
    return pl.pallas_call(
        functools.partial(attend_kernel, groups, reach, block // 2, share),
        out_shape=out_shape,
        in_specs=[SMEM, SMEM, SMEM] + [VMEM] * 3 + ([SMEM] + [HBM] * 4 if parts else []),
        out_specs=[HBM] * outs + ([VMEM] if parts else []),
        scratch_shapes=scratch,
        compiler_params=pltpu.CompilerParams(vmem_limit_bytes=16 * MIB),
        cost_estimate=pl.CostEstimate(flops=1 << 34, bytes_accessed=1 << 20, transcendentals=0),
        name="attend",
    )(place, band, turn, q_all, kv_all, vt_all, *parts)


def output_kernel(layers, place_ref, weight, *refs):
    contexts, out_ref = refs[:layers], refs[layers]
    columns = weight.shape[3]
    for side in range(2):
        total = None
        for step in range(layers):
            got = jnp.dot(contexts[step][...], weight[place_ref[step], side], preferred_element_type=jnp.float32)
            total = got if step == 0 else total + got
        out_ref[0, :, side * columns:(side + 1) * columns] = total.astype(jnp.bfloat16)


def output(place, weight, contexts):
    layers, _, depth, columns = weight.shape
    rows = contexts[0].shape[0]
    return pl.pallas_call(
        functools.partial(output_kernel, layers),
        out_shape=jax.ShapeDtypeStruct((1, rows, 2 * columns), jnp.bfloat16),
        in_specs=[SMEM] + [VMEM] * (1 + layers),
        out_specs=VMEM,
        compiler_params=pltpu.CompilerParams(vmem_limit_bytes=8 * MIB),
        cost_estimate=LIGHT,
        name="output",
    )(place, weight, *contexts)


def hold_kernel(*refs):
    del refs


def hold(values, cost=1 << 34):
    return pl.pallas_call(
        hold_kernel,
        out_shape=[jax.ShapeDtypeStruct(value.shape, value.dtype) for value in values],
        in_specs=[HBM] * len(values),
        out_specs=[HBM] * len(values),
        input_output_aliases={i: i for i in range(len(values))},
        compiler_params=pltpu.CompilerParams(vmem_limit_bytes=MIB),
        cost_estimate=pl.CostEstimate(flops=cost, bytes_accessed=1, transcendentals=0),
        name="hold",
    )(*values)


def together(*values):
    return lax.optimization_barrier(values)


def numbers(*values):
    return jnp.stack([jnp.asarray(value, jnp.int32) for value in values])


def local(frames, norm_gain, w_query, w_key, w_value, w_out, group_band, lengths):
    cores, seqs, layers = lax.axis_size("dp"), lax.axis_size("seq"), lax.axis_size("head")
    core, seq, layer = lax.axis_index("dp"), lax.axis_index("seq"), lax.axis_index("head")
    groups = group_band.shape[1]
    width = w_query.shape[1]
    here = [(c, s) for c in range(cores) for s in range(seqs)]

    def home(c, s):
        return s % 2, s // 2 * 2 + c

    def flat(c, s, z=None):
        return c * seqs + s if z is None else (c * seqs + s) * layers + z

    def moved(value, shift):
        pairs = [(flat(c, s, z), flat(*home(c, s), shift(z))) for c, s in here for z in range(layers)]
        return lax.ppermute(value, ("dp", "seq", "head"), pairs)

    after = ring_successors(layers)
    before = {after[z]: z for z in after}
    swap = [(c, cores - 1 - c) for c in range(cores)]
    over_link = [(flat(1, s), flat(0, s + 2)) for s in range(seqs - 2)]
    over_link += [(flat(0, s + 2), flat(1, s)) for s in range(seqs - 2)]
    share = 4

    def shared(value, behind):
        near = [lax.ppermute(value, "seq", [(s, s ^ step) for s in range(seqs)]) for step in (1, 2)]
        *near, _ = together(*near, behind)
        return [value] + near + [lax.ppermute(near[1], "seq", [(s, s ^ 1) for s in range(seqs)])]

    rows = frames[0]
    count = rows.shape[0]
    gain = norm_gain[None, :]

    def halos(pair):
        return lax.ppermute(pair, ("dp", "seq"), over_link), lax.ppermute(pair, "dp", swap)

    def ringed(value):
        return lax.ppermute(value, "head", [(z, after[z]) for z in range(layers)])

    sent, piece = pack(numbers(lax.rem(seq, share)), rows, w_out, share)
    piece = moved(piece, lambda z: before[z])
    first = moved(sent, lambda z: after[z])
    second = ringed(first)
    own = bundle(w_query, w_key, w_value, w_out)
    whole = moved(rows, lambda z: z)
    facts = jnp.concatenate([group_band[0], jnp.broadcast_to(lengths[:, None], (1, group_band.shape[2]))], axis=0)
    facts = lax.ppermute(facts, ("dp", "seq"), [(flat(c, s), flat(*home(c, s))) for c, s in here])
    *own, facts = together(*own, facts)
    far = [lax.ppermute(value, "dp", swap) for value in own]
    back = {z: before[z] for z in range(layers)}
    ids = [layer, lookup([back[z] for z in range(layers)], layer)]
    ids.append(lookup([back[back[z]] for z in range(layers)], layer))
    ids.append(lookup([after[z] for z in range(layers)], layer))
    place = numbers(core, (seq // 2 * 2 + core) * groups, groups * seqs, facts[groups, 0], *ids)
    band = facts[:groups]
    piece, = hold([piece], 1 << 33)
    half = layers // 2
    sides = (1 - layer // half, layer // half)
    turns = [
        numbers(side * half * count, *[lax.rem(layer + e, half) * count for e in range(half)]) for side in sides
    ]
    weight_place = numbers(core, layer, seq, ids[1], ids[2], ids[3])
    sources = numbers(*[side * half + lax.rem(layer + half - e, half) for side in sides for e in range(half)])
    core_at = numbers(core)
    whole, place, band, piece, weight_place, sources, core_at, *turns = together(
        whole, place, band, piece, weight_place, sources, core_at, *turns
    )

    query_a, pair_a = project(core_at, [whole, first], count, width, gain, own, far, 1)
    link_a, chip_a = halos(pair_a)
    third = ringed(second[:count])
    piece, link_a, chip_a = together(piece, link_a, chip_a)
    query_b, pair_b = project(core_at, [second], count, width, gain, own, far, 1)
    shares = shared(join(count, first, second, piece), query_b)
    link_b, chip_b = halos(pair_b)
    third, link_b, chip_b = together(third, link_b, chip_b)
    query_c, pair_c = project(core_at, [third], count, width, gain, own, far, 1 << 30)
    link_c, chip_c = halos(pair_c)
    q_all, kv_all, vt_all, mine = window(
        place, groups, count, [query_a, query_b, query_c], [pair_a, pair_b, pair_c],
        [chip_a, chip_b, chip_c], [link_a, link_b, link_c], shares,
    )
    theirs = lax.ppermute(mine, "dp", swap)

    contexts, arrived = [], []
    for near in (0, 1):
        if near:
            *got, weight = attend(
                place, band, turns[near], half, q_all, kv_all, vt_all, share, layers,
                [weight_place, w_out, far[1], mine, theirs],
            )
        else:
            got = list(attend(place, band, turns[near], half, q_all, kv_all, vt_all))
            got[0], q_all = together(got[0], q_all)
        contexts += got
    *contexts[1:half], contexts[half] = together(*contexts[1:half], contexts[half])
    for index, context in enumerate(contexts):
        near, e = divmod(index, half)

        def target(z, near=near, e=e):
            return (z // half if near else 1 - z // half) * half + (z + e) % half

        arrived.append(moved(context, target))
    arrived = list(hold(arrived[:1])) + arrived[1:]
    return output(sources, weight, arrived)


def solution(mesh):
    return jax.shard_map(
        local,
        mesh=mesh,
        in_specs=(
            P("dp", ("seq", "head"), None),
            P(),
            P("dp", "head"),
            P("dp", "head"),
            P("dp", "head"),
            P("head", "dp"),
            P("dp", "seq", None),
            P("dp"),
        ),
        out_specs=P("dp", ("seq", "head"), None),
        check_vma=False,
    )
```

```python
import functools

import jax
import jax.numpy as jnp
from jax import lax
from jax.experimental import pallas as pl
from jax.experimental.pallas import tpu as pltpu
from jax.sharding import PartitionSpec as P

HD = 64
GROUP = 128
LANES = 128

epsilon = 1e-05

VMEM = pl.BlockSpec(memory_space=pltpu.VMEM)
SMEM = pl.BlockSpec(memory_space=pltpu.SMEM)
HBM = pl.BlockSpec(memory_space=pltpu.HBM)
MIB = 1024 * 1024
LIGHT = pl.CostEstimate(flops=1, bytes_accessed=1, transcendentals=0)


def ring_successors(count):
    order = [0] + list(range(1, count, 2)) + list(range(count - 2 + count % 2, 0, -2))
    return {order[i]: order[(i + 1) % count] for i in range(count)}


def lookup(table, index):
    value = jnp.int32(table[0])
    for place in range(1, len(table)):
        value = jnp.where(index == place, jnp.int32(table[place]), value)
    return value


def copy_all(pairs, sems):
    copies = [pltpu.make_async_copy(source, target, sems.at[i]) for i, (source, target) in enumerate(pairs)]
    for copy in copies:
        copy.start()
    return copies


def in_hbm(*values):
    return [pltpu.with_memory_space_constraint(value, pltpu.HBM) for value in values]


def run_copies(loads, stores, sems):
    for copy in copy_all(loads, sems):
        copy.wait()
    for copy in copy_all(stores, sems):
        copy.wait()


def pack_kernel(place_ref, rows_ref, w_out_ref, sent_ref, piece_ref, held, held_piece, sems):
    count = rows_ref.shape[0]
    part, columns = piece_ref.shape
    first = pl.multiple_of(place_ref[0] * part, 16)
    loads = [(w_out_ref.at[pl.ds(first, part), :], held_piece), (rows_ref, held.at[pl.ds(0, count), :])]
    for side in range(2):
        loads.append((
            w_out_ref.at[pl.ds(first + side * (part // 2), part // 2), :],
            held.at[pl.ds(count, part // 2), pl.ds(side * columns, columns)],
        ))
    run_copies(loads, [(held, sent_ref), (held_piece, piece_ref)], sems)


def pack(place, rows, w_out, share):
    part = w_out.shape[0] // share
    shapes = [(rows.shape[0] + part // 2, rows.shape[1]), (part, w_out.shape[1])]
    return pl.pallas_call(
        pack_kernel,
        out_shape=[pltpu.HBM(shape, jnp.bfloat16) for shape in shapes],
        in_specs=[SMEM] + [HBM] * 2,
        out_specs=[HBM] * 2,
        scratch_shapes=[pltpu.VMEM(shape, jnp.bfloat16) for shape in shapes] + [pltpu.SemaphoreType.DMA((4,))],
        compiler_params=pltpu.CompilerParams(vmem_limit_bytes=4 * MIB),
        cost_estimate=LIGHT,
        name="pack",
    )(place, *in_hbm(rows, w_out))


def bundle_kernel(query_ref, key_ref, value_ref, w_out_ref, front_ref, back_ref, sems):
    width, rows = query_ref.shape[1], w_out_ref.shape[0]
    loads = [
        (query_ref, front_ref.at[:, pl.ds(0, width)]),
        (key_ref, front_ref.at[:, pl.ds(width, width)]),
        (value_ref, back_ref.at[:, pl.ds(0, width)]),
    ]
    for side in range(2):
        loads.append((
            w_out_ref.at[:, pl.ds(side * width, width)],
            back_ref.at[pl.ds(side * rows, rows), pl.ds(width, width)],
        ))
    for load in copy_all(loads, sems):
        load.wait()


def bundle(w_query, w_key, w_value, w_out):
    shape = (w_query.shape[0], 2 * w_query.shape[1])
    return pl.pallas_call(
        bundle_kernel,
        out_shape=[jax.ShapeDtypeStruct(shape, jnp.bfloat16)] * 2,
        in_specs=[HBM] * 4,
        out_specs=[VMEM] * 2,
        scratch_shapes=[pltpu.SemaphoreType.DMA((5,))],
        compiler_params=pltpu.CompilerParams(vmem_limit_bytes=4 * MIB),
        cost_estimate=LIGHT,
        name="bundle",
    )(*in_hbm(w_query, w_key, w_value, w_out))


def join_kernel(count, first_ref, second_ref, piece_ref, out_ref, held, sems):
    part, columns = piece_ref.shape[0] // 2, piece_ref.shape[1]
    loads = [
        (source.at[pl.ds(count, part), :], held.at[pl.ds(place * part, part), :])
        for place, source in enumerate((first_ref, second_ref))
    ]
    for side in range(2):
        loads.append((
            piece_ref.at[pl.ds(side * part, part), :],
            held.at[pl.ds(2 * part, part), pl.ds(side * columns, columns)],
        ))
    run_copies(loads, [(held, out_ref)], sems)


def join(count, first, second, piece):
    shape = (3 * piece.shape[0] // 2, first.shape[1])
    return pl.pallas_call(
        functools.partial(join_kernel, count),
        out_shape=pltpu.HBM(shape, jnp.bfloat16),
        in_specs=[HBM] * 3,
        out_specs=HBM,
        scratch_shapes=[pltpu.VMEM(shape, jnp.bfloat16), pltpu.SemaphoreType.DMA((4,))],
        compiler_params=pltpu.CompilerParams(vmem_limit_bytes=4 * MIB),
        cost_estimate=LIGHT,
        name="join",
    )(first, second, piece)


def project_kernel(blocks, count, place_ref, gain_ref, own_front, own_back, far_front, far_back, *refs):
    rows = refs[:blocks]
    query_ref, pair_ref, held, query_held, pair_held, sems = refs[blocks:]
    depth, width = own_front.shape[0], query_ref.shape[1]
    first = place_ref[0] == 0
    loads = []
    if blocks > 1:
        loads = copy_all(
            [(rows[i].at[pl.ds(0, count), :], held.at[pl.ds(i * count, count), :]) for i in range(blocks)], sems
        )
    gain = gain_ref[...]
    mine, theirs = [], []
    for i in range(blocks):
        if blocks > 1:
            loads[i].wait()
            values = held[i * count:(i + 1) * count, :].astype(jnp.float32)
        else:
            values = rows[0][:count, :].astype(jnp.float32)
        center = values - jnp.mean(values, axis=-1, keepdims=True)
        spread = jnp.mean(center * center, axis=-1, keepdims=True)
        normalized = (center * lax.rsqrt(spread + epsilon) * gain).astype(jnp.bfloat16)
        low, high = normalized[:, :depth], normalized[:, depth:]
        mine.append(jnp.where(first, low, high))
        theirs.append(jnp.where(first, high, low))
    mine = mine[0] if blocks == 1 else jnp.concatenate(mine, axis=0)
    theirs = theirs[0] if blocks == 1 else jnp.concatenate(theirs, axis=0)
    stores = []
    for place in (1, 2, 0):
        own, far = ((own_front, far_front), (own_back, far_back))[place // 2]
        columns = slice(place % 2 * width, (place % 2 + 1) * width)
        got = jnp.dot(mine, own[:, columns], preferred_element_type=jnp.float32)
        got = (got + jnp.dot(theirs, far[:, columns], preferred_element_type=jnp.float32)).astype(jnp.bfloat16)
        sem = sems.at[pl.ds(blocks + place, 1)]
        if place == 0:
            query_held[...] = (got.astype(jnp.float32) * (HD ** -0.5)).astype(jnp.bfloat16)
            stores += copy_all([(query_held, query_ref)], sem)
        else:
            part = pl.ds((place - 1) * width, width)
            pair_held[:, (place - 1) * width:place * width] = got
            stores += copy_all([(pair_held.at[:, part], pair_ref.at[:, part])], sem)
    for store in stores:
        store.wait()


def project(place, rows, count, width, gain, own, far, cost):
    blocks, depth = len(rows), rows[0].shape[1]
    total = blocks * count
    return pl.pallas_call(
        functools.partial(project_kernel, blocks, count),
        out_shape=[pltpu.HBM((total, width), jnp.bfloat16), pltpu.HBM((total, 2 * width), jnp.bfloat16)],
        in_specs=[SMEM] + [VMEM] * 5 + ([HBM] * blocks if blocks > 1 else [VMEM]),
        out_specs=[HBM, HBM],
        scratch_shapes=[
            pltpu.VMEM((total, depth), jnp.bfloat16),
            pltpu.VMEM((total, width), jnp.bfloat16),
            pltpu.VMEM((total, 2 * width), jnp.bfloat16),
            pltpu.SemaphoreType.DMA((blocks + 3,)),
        ],
        compiler_params=pltpu.CompilerParams(vmem_limit_bytes=16 * MIB),
        cost_estimate=pl.CostEstimate(flops=cost, bytes_accessed=1, transcendentals=0),
        name="project",
    )(place, gain, *own, *far, *rows)


def window_kernel(shape, groups, joined, place_ref, *refs):
    kinds = len(shape)
    queries, owns, sides = refs[:kinds], refs[kinds:2 * kinds], refs[2 * kinds:4 * kinds]
    sources = refs[4 * kinds:4 * kinds + joined]
    q_all, kv_all, vt_all, join_ref, join_held, sems = refs[4 * kinds + joined:]
    block, width = q_all.shape
    rows = block // sum(shape)
    core = place_ref[0]
    chip_base = jnp.where(core == 0, 2 * block, 0)
    link_base = jnp.where(core == 0, 0, 2 * block)
    pairs, step = [], 0
    for kind in range(kinds):
        for inside in range(shape[kind]):
            at = place_ref[4 + step] * rows
            part = pl.ds(inside * rows, rows)
            pairs.append((queries[kind].at[part, :], q_all.at[pl.ds(pl.multiple_of(at, 64), rows), :]))
            for source, base in (
                (owns[kind], block), (sides[kind], chip_base), (sides[kinds + kind], link_base)
            ):
                to = pl.ds(pl.multiple_of(base + at, 64), rows)
                pairs.append((source.at[part, :], kv_all.at[to, :]))
            step += 1
    loads = copy_all(pairs, sems)
    parts, at = [], 0
    for source in sources:
        parts.append((source, join_held.at[pl.ds(at, source.shape[0]), :]))
        at += source.shape[0]
    parts = copy_all(parts, sems.at[pl.ds(len(loads), joined)])
    for load in loads + parts:
        load.wait()
    stores = copy_all([(join_held, join_ref)], sems.at[pl.ds(len(loads) + joined, 1)])
    for index in range(3 * groups):
        for pair in range(width // LANES):
            columns = slice(width + pair * LANES, width + (pair + 1) * LANES)
            vt_all[pair, index] = kv_all[index * GROUP:(index + 1) * GROUP, columns].T
    for store in stores:
        store.wait()


def window(place, groups, rows, queries, owns, chip_side, link_side, joined):
    shape = [query.shape[0] // rows for query in queries]
    width, block = queries[0].shape[1], sum(shape) * rows
    pairs = width // LANES
    join_shape = (sum(value.shape[0] for value in joined), joined[0].shape[1])
    return pl.pallas_call(
        functools.partial(window_kernel, shape, groups, len(joined)),
        out_shape=(
            jax.ShapeDtypeStruct((block, width), jnp.bfloat16),
            jax.ShapeDtypeStruct((3 * block, 2 * width), jnp.bfloat16),
            jax.ShapeDtypeStruct((pairs, 3 * groups, LANES, GROUP), jnp.bfloat16),
            pltpu.HBM(join_shape, jnp.bfloat16),
        ),
        in_specs=[SMEM] + [HBM] * (4 * len(shape) + len(joined)),
        out_specs=(VMEM,) * 3 + (HBM,),
        scratch_shapes=[
            pltpu.VMEM(join_shape, jnp.bfloat16), pltpu.SemaphoreType.DMA((4 * sum(shape) + len(joined) + 1,))
        ],
        compiler_params=pltpu.CompilerParams(vmem_limit_bytes=16 * MIB),
        cost_estimate=pl.CostEstimate(flops=0, bytes_accessed=2 * 14 * block * width, transcendentals=0),
        name="window",
    )(place, *in_hbm(*queries, *owns), *chip_side, *link_side, *in_hbm(joined[0]), *joined[1:])


def weight_copies(share, place_ref, own_ref, far_ref, pieces_ref, theirs_ref, weight_ref):
    core, layer, seq = (place_ref[i] for i in range(3))
    layers, _, depth, columns = weight_ref.shape
    part = depth // share // 2
    half = columns // 2
    pairs = [(own_ref, weight_ref.at[layer, core])]
    for side in range(2):
        pairs.append((
            far_ref.at[pl.ds(side * depth, depth), pl.ds(far_ref.shape[1] - half, half)],
            weight_ref.at[layer, 1 - core, :, pl.ds(side * half, half)],
        ))
    for other in range(share):
        there = seq ^ other
        for source, holder in ((pieces_ref, core), (theirs_ref, 1 - core)):
            at = lax.rem(there // 2 * 2 + holder, share) * 2 * part
            for step in range(layers - 1):
                row = (other * (layers - 1) + step) * part
                for side in range(2):
                    to = pl.ds(pl.multiple_of(at + side * part, 16), part)
                    pairs.append((
                        source.at[pl.ds(row, part), pl.ds(side * columns, columns)],
                        weight_ref.at[place_ref[3 + step], lax.rem(there, 2), to, :],
                    ))
    return pairs


def attend_kernel(groups, reach, count_rows, share, place_ref, band_ref, turn_ref, q_all, kv_all, vt_all, *refs):
    loads = []
    if share:
        sources, refs = refs[:5], refs[5:]
        weight, load_sems, refs = refs[-7], refs[-1], refs[:-7] + refs[-6:-1]
        loads = copy_all(weight_copies(share, *sources, weight), load_sems)
    outs, (score, ctx, chosen, limits, sems) = refs[:-5], refs[-5:]
    pairs, rows = vt_all.shape[0], outs[0].shape[0]
    first_group, total, length = (place_ref[i] for i in range(1, 4))
    first_row = turn_ref[0]
    slots = 2 * reach + 2
    half_mask = lax.broadcasted_iota(jnp.int32, (GROUP, LANES), 1) < HD
    row_ids = lax.broadcasted_iota(jnp.int32, (GROUP, 2 * GROUP), 0)
    part_group = lax.div(length, jnp.int32(GROUP))
    part_left = lax.rem(length, jnp.int32(GROUP))

    def one_group(place, carry):
        group = first_row // GROUP + place
        for slot in range(slots):
            chosen[slot] = groups + group
        offset = part_group - first_group - group
        column = jnp.clip(jnp.where(offset < 0, offset + reach, offset + reach - 1), 0, 2 * reach - 1)
        cut = (part_left > 0) & (offset != 0) & (jnp.abs(offset) <= reach) & (part_group < total)
        cut = cut & (band_ref[group, column] == 1)
        chosen[1] = jnp.where(cut, groups + group + offset, groups + group)
        limits[0] = jnp.where(cut, part_left, 0)
        count = 1 + cut.astype(jnp.int32)
        for column in range(2 * reach):
            offset = column - reach if column < reach else column - reach + 1
            there = first_group + group + offset
            good = (there >= 0) & (there < part_group) & (there < total) & (band_ref[group, column] == 1)
            chosen[count] = jnp.where(good, groups + group + offset, groups + group)
            limits[0] = jnp.where(good & (count == 1), GROUP, limits[0])
            count = count + good.astype(jnp.int32)
        query_at = pl.ds(pl.multiple_of(group * GROUP, GROUP), GROUP)
        out_at = pl.ds(pl.multiple_of(place * GROUP, GROUP), GROUP)

        def run(size):
            first_limit = limits[0]
            last_limit = jnp.where(count == size, GROUP, 0)
            indices = [chosen[slot] for slot in range(size)]
            best = []
            for pair in range(pairs):
                own = q_all[query_at, pair * LANES:(pair + 1) * LANES]
                zero = jnp.zeros_like(own)
                both = jnp.concatenate(
                    [jnp.where(half_mask, own, zero), jnp.where(half_mask, zero, own)], axis=0
                ).T
                top = None
                for slot in range(0, size, 2):
                    tiles = [
                        kv_all[pl.ds(pl.multiple_of(index * GROUP, GROUP), GROUP), pair * LANES:(pair + 1) * LANES]
                        for index in indices[slot:slot + 2]
                    ]
                    got = jnp.dot(jnp.concatenate(tiles, axis=0), both, preferred_element_type=jnp.float32)
                    for one in (slot, slot + 1):
                        part = got[(one - slot) * GROUP:(one - slot + 1) * GROUP]
                        if one == 1:
                            part = jnp.where(row_ids < first_limit, part, -jnp.inf)
                        elif one == size - 1:
                            part = jnp.where(row_ids < last_limit, part, -jnp.inf)
                        score[pair, one * GROUP:(one + 1) * GROUP, :] = part
                        high = jnp.max(part.reshape(GROUP // 8, 8, 2 * GROUP), axis=0)
                        top = high if top is None else jnp.maximum(top, high)
                best.append(jnp.max(top, axis=0, keepdims=True))
            for pair in range(pairs):
                total_sum = jnp.zeros((8, 2 * GROUP), jnp.float32)
                mixed = jnp.zeros((LANES, 2 * GROUP), jnp.float32)
                for slot in range(0, size, 2):
                    weights = jnp.exp(score[pair, slot * GROUP:(slot + 2) * GROUP, :] - best[pair])
                    total_sum += jnp.sum(weights.reshape(2 * GROUP // 8, 8, 2 * GROUP), axis=0)
                    tiles = [vt_all[pair, index] for index in indices[slot:slot + 2]]
                    mixed += jnp.dot(
                        jnp.concatenate(tiles, axis=1),
                        weights.astype(jnp.bfloat16),
                        preferred_element_type=jnp.float32,
                    )
                mixed = mixed / jnp.sum(total_sum, axis=0, keepdims=True)
                both_heads = jnp.concatenate([mixed[:HD, :GROUP], mixed[HD:, GROUP:]], axis=0)
                ctx[out_at, pair * LANES:(pair + 1) * LANES] = both_heads.T.astype(jnp.bfloat16)

        for size in range(2, slots + 1, 2):
            @pl.when((count == size) | (count == size - 1))
            def _():
                run(size)

        return carry

    lax.fori_loop(0, count_rows // GROUP, one_group, 0)
    stores = copy_all(
        [(ctx.at[pl.ds(pl.multiple_of(turn_ref[1 + i], 64), rows), :], out) for i, out in enumerate(outs)], sems
    )
    for copy in stores + loads:
        copy.wait()


def attend(place, band, turn, outs, q_all, kv_all, vt_all, share=0, layers=0, parts=()):
    groups, reach = band.shape[0], band.shape[1] // 2
    pairs, block = vt_all.shape[0], q_all.shape[0]
    rows = block // (2 * outs)
    slots = 2 * reach + 2
    out_shape = [pltpu.HBM((rows, pairs * LANES), jnp.bfloat16)] * outs
    scratch = [
        pltpu.VMEM((pairs, slots * GROUP, 2 * GROUP), jnp.float32),
        pltpu.VMEM((block // 2, pairs * LANES), jnp.bfloat16),
        pltpu.SMEM((slots + 2,), jnp.int32),
        pltpu.SMEM((1,), jnp.int32),
        pltpu.SemaphoreType.DMA((outs,)),
    ]
    if parts:
        depth, columns = parts[1].shape
        out_shape.append(jax.ShapeDtypeStruct((layers, 2, depth, columns), jnp.bfloat16))
        scratch.append(pltpu.SemaphoreType.DMA((3 + 4 * share * (layers - 1),)))
        parts = [parts[0], *in_hbm(parts[1]), parts[2], *in_hbm(parts[3]), parts[4]]
    return pl.pallas_call(
        functools.partial(attend_kernel, groups, reach, block // 2, share),
        out_shape=out_shape,
        in_specs=[SMEM, SMEM, SMEM] + [VMEM] * 3 + ([SMEM] + [HBM] * 4 if parts else []),
        out_specs=[HBM] * outs + ([VMEM] if parts else []),
        scratch_shapes=scratch,
        compiler_params=pltpu.CompilerParams(vmem_limit_bytes=16 * MIB),
        cost_estimate=pl.CostEstimate(flops=1 << 34, bytes_accessed=1 << 20, transcendentals=0),
        name="attend",
    )(place, band, turn, q_all, kv_all, vt_all, *parts)


def output_kernel(layers, place_ref, weight, *refs):
    contexts, out_ref = refs[:layers], refs[layers]
    columns = weight.shape[3]
    for side in range(2):
        total = None
        for step in range(layers):
            got = jnp.dot(contexts[step][...], weight[place_ref[step], side], preferred_element_type=jnp.float32)
            total = got if step == 0 else total + got
        out_ref[0, :, side * columns:(side + 1) * columns] = total.astype(jnp.bfloat16)


def output(place, weight, contexts):
    layers, _, depth, columns = weight.shape
    rows = contexts[0].shape[0]
    return pl.pallas_call(
        functools.partial(output_kernel, layers),
        out_shape=jax.ShapeDtypeStruct((1, rows, 2 * columns), jnp.bfloat16),
        in_specs=[SMEM] + [VMEM] * (1 + layers),
        out_specs=VMEM,
        compiler_params=pltpu.CompilerParams(vmem_limit_bytes=8 * MIB),
        cost_estimate=LIGHT,
        name="output",
    )(place, weight, *contexts)


def hold_kernel(*refs):
    del refs


def hold(values, cost=1 << 34):
    return pl.pallas_call(
        hold_kernel,
        out_shape=[jax.ShapeDtypeStruct(value.shape, value.dtype) for value in values],
        in_specs=[HBM] * len(values),
        out_specs=[HBM] * len(values),
        input_output_aliases={i: i for i in range(len(values))},
        compiler_params=pltpu.CompilerParams(vmem_limit_bytes=MIB),
        cost_estimate=pl.CostEstimate(flops=cost, bytes_accessed=1, transcendentals=0),
        name="hold",
    )(*values)


def together(*values):
    return lax.optimization_barrier(values)


def numbers(*values):
    return jnp.stack([jnp.asarray(value, jnp.int32) for value in values])


def local(frames, norm_gain, w_query, w_key, w_value, w_out, group_band, lengths):
    cores, seqs, layers = lax.axis_size("dp"), lax.axis_size("seq"), lax.axis_size("head")
    core, seq, layer = lax.axis_index("dp"), lax.axis_index("seq"), lax.axis_index("head")
    groups = group_band.shape[1]
    width = w_query.shape[1]
    here = [(c, s) for c in range(cores) for s in range(seqs)]

    def home(c, s):
        return s % 2, s // 2 * 2 + c

    def flat(c, s, z=None):
        return c * seqs + s if z is None else (c * seqs + s) * layers + z

    def moved(value, shift):
        pairs = [(flat(c, s, z), flat(*home(c, s), shift(z))) for c, s in here for z in range(layers)]
        return lax.ppermute(value, ("dp", "seq", "head"), pairs)

    after = ring_successors(layers)
    before = {after[z]: z for z in after}
    swap = [(c, cores - 1 - c) for c in range(cores)]
    over_link = [(flat(1, s), flat(0, s + 2)) for s in range(seqs - 2)]
    over_link += [(flat(0, s + 2), flat(1, s)) for s in range(seqs - 2)]
    share = 4

    def shared(value, behind):
        near = [lax.ppermute(value, "seq", [(s, s ^ step) for s in range(seqs)]) for step in (1, 2)]
        *near, _ = together(*near, behind)
        return [value] + near + [lax.ppermute(near[1], "seq", [(s, s ^ 1) for s in range(seqs)])]

    rows = frames[0]
    count = rows.shape[0]
    gain = norm_gain[None, :]

    def halos(pair):
        return lax.ppermute(pair, ("dp", "seq"), over_link), lax.ppermute(pair, "dp", swap)

    def ringed(value):
        return lax.ppermute(value, "head", [(z, after[z]) for z in range(layers)])

    sent, piece = pack(numbers(lax.rem(seq, share)), rows, w_out, share)
    piece = moved(piece, lambda z: before[z])
    first = moved(sent, lambda z: after[z])
    second = ringed(first)
    own = bundle(w_query, w_key, w_value, w_out)
    whole = moved(rows, lambda z: z)
    facts = jnp.concatenate([group_band[0], jnp.broadcast_to(lengths[:, None], (1, group_band.shape[2]))], axis=0)
    facts = lax.ppermute(facts, ("dp", "seq"), [(flat(c, s), flat(*home(c, s))) for c, s in here])
    *own, facts = together(*own, facts)
    far = [lax.ppermute(value, "dp", swap) for value in own]
    back = {z: before[z] for z in range(layers)}
    ids = [layer, lookup([back[z] for z in range(layers)], layer)]
    ids.append(lookup([back[back[z]] for z in range(layers)], layer))
    ids.append(lookup([after[z] for z in range(layers)], layer))
    place = numbers(core, (seq // 2 * 2 + core) * groups, groups * seqs, facts[groups, 0], *ids)
    band = facts[:groups]
    piece, = hold([piece], 1 << 33)
    half = layers // 2
    sides = (1 - layer // half, layer // half)
    turns = [
        numbers(side * half * count, *[lax.rem(layer + e, half) * count for e in range(half)]) for side in sides
    ]
    weight_place = numbers(core, layer, seq, ids[1], ids[2], ids[3])
    sources = numbers(*[side * half + lax.rem(layer + half - e, half) for side in sides for e in range(half)])
    core_at = numbers(core)
    whole, place, band, piece, weight_place, sources, core_at, *turns = together(
        whole, place, band, piece, weight_place, sources, core_at, *turns
    )

    query_a, pair_a = project(core_at, [whole, first], count, width, gain, own, far, 1)
    link_a, chip_a = halos(pair_a)
    third = ringed(second[:count])
    piece, link_a, chip_a = together(piece, link_a, chip_a)
    query_b, pair_b = project(core_at, [second], count, width, gain, own, far, 1)
    shares = shared(join(count, first, second, piece), query_b)
    link_b, chip_b = halos(pair_b)
    query_c, pair_c = project(core_at, [third], count, width, gain, own, far, 1 << 32)
    link_c, chip_c = halos(pair_c)
    q_all, kv_all, vt_all, mine = window(
        place, groups, count, [query_a, query_b, query_c], [pair_a, pair_b, pair_c],
        [chip_a, chip_b, chip_c], [link_a, link_b, link_c], shares,
    )
    theirs = lax.ppermute(mine, "dp", swap)

    contexts, arrived = [], []
    for near in (0, 1):
        if near:
            *got, weight = attend(
                place, band, turns[near], half, q_all, kv_all, vt_all, share, layers,
                [weight_place, w_out, far[1], mine, theirs],
            )
        else:
            got = list(attend(place, band, turns[near], half, q_all, kv_all, vt_all))
            got[0], q_all = together(got[0], q_all)
        contexts += got
    *contexts[1:half], contexts[half] = together(*contexts[1:half], contexts[half])
    for index, context in enumerate(contexts):
        near, e = divmod(index, half)

        def target(z, near=near, e=e):
            return (z // half if near else 1 - z // half) * half + (z + e) % half

        arrived.append(moved(context, target))
    arrived = list(hold(arrived[:1])) + arrived[1:]
    return output(sources, weight, arrived)


def solution(mesh):
    return jax.shard_map(
        local,
        mesh=mesh,
        in_specs=(
            P("dp", ("seq", "head"), None),
            P(),
            P("dp", "head"),
            P("dp", "head"),
            P("dp", "head"),
            P("head", "dp"),
            P("dp", "seq", None),
            P("dp"),
        ),
        out_specs=P("dp", ("seq", "head"), None),
        check_vma=False,
    )
```
